128 devices in a mesh: page: 16 (over y, x_lo, core), blk: 8 (over z, x_hi).
Axes of the slice: x: 4 (x_hi: 2, x_lo: 2; x = x_hi * 2 + x_lo), y: 4, z: 4, core: 2. Of those that a mesh axis runs over, the one named last changes fastest.
Arguments:
- tokens: bfloat16 [32, 1024, 1024], P('page', 'blk'), may hold values from -6 to 6
- memory: bfloat16 [32, 1024, 1024], P('page', 'blk'), may hold values from -6 to 6
- lengths: int32 [32], P('page'), may hold values from 512 to 1024, as said below
- patch_counts: int32 [32], P('page'), may hold values from 256 to 1024, as said below
- self_qkv: bfloat16 [1024, 3072], replicated, may hold values from -0.1875 to 0.1875
- self_out: bfloat16 [1024, 1024], replicated, may hold values from -1.5 to 1.5
- cross_query: bfloat16 [1024, 1024], replicated, may hold values from -0.1875 to 0.1875
- cross_kv: bfloat16 [1024, 2048], replicated, may hold values from -0.1875 to 0.1875
- cross_out: bfloat16 [1024, 1024], replicated, may hold values from -1.5 to 1.5
- ffn_in: bfloat16 [1024, 4096], replicated, may hold values from -0.1875 to 0.1875
- ffn_out: bfloat16 [4096, 1024], replicated, may hold values from -0.09375 to 0.09375
- norm_gains: float32 [3, 1024], replicated, may hold values from 0.5 to 1.5
- norm_shifts: float32 [3, 1024], replicated, may hold values from -3 to 3
- proj_biases: float32 [7, 1024], replicated, may hold values from -3 to 3
- ffn_bias: float32 [4096], replicated, may hold values from -3 to 3
- cotangent: bfloat16 [32, 1024, 1024], P('page', 'blk'), may hold values from -6 to 6
Outputs:
- layer_out: bfloat16 [32, 1024, 1024], P('page', 'blk')
- token_grad: bfloat16 [32, 1024, 1024], P('page', 'blk')
- memory_grad: bfloat16 [32, 1024, 1024], P('page', 'blk')
- grad_self_qkv: float32 [1024, 3072], P(None, ('page', 'blk'))
- grad_self_out: float32 [1024, 1024], P(None, ('page', 'blk'))
- grad_cross_query: float32 [1024, 1024], P(None, ('page', 'blk'))
- grad_cross_kv: float32 [1024, 2048], P(None, ('page', 'blk'))
- grad_cross_out: float32 [1024, 1024], P(None, ('page', 'blk'))
- grad_ffn_in: float32 [1024, 4096], P(None, ('page', 'blk'))
- grad_ffn_out: float32 [4096, 1024], P(None, ('page', 'blk'))
- grad_norm_gains: float32 [3, 1024], P(None, ('page', 'blk'))
- grad_norm_shifts: float32 [3, 1024], P(None, ('page', 'blk'))
- grad_proj_biases: float32 [7, 1024], P(None, ('page', 'blk'))
- grad_ffn_bias: float32 [4096], P(('page', 'blk'))
The draws below stay inside these ranges and needn't reach their ends.
Inputs may be any that keep to these rules, and one draw needn't show every extreme that they name: `lengths`: pages of one group are 2 consecutive pages; in each group one page, drawn from the seed, has length 1024. `patch_counts`: each page has 1024 or 256 live patches, the first ones of its slots; in each group one page, drawn from the seed, has 1024.
All inputs are finite; a program needn't handle non-finite values.
Results may differ from the reference program's by a relative error of at most 0.02.
Values may be sent and summed in bfloat16 or wider, within the bound.
No kernel may reach another device: no remote copies, remote signals or barrier semaphores. Data moves between devices by JAX's collectives and lax.ppermute only.
A program may use at most 256 MiB of HBM per device.

```python
import jax
import jax.numpy as jnp
from jax import lax

D = 1024
FF = 4096
ENC = 1024
HEADS = 16
HEAD = 64
PAGES_GRP = 2
SEQ = 1024
PATCHES = 1024
PAGES = 32


def chosen_slots(key_pick):
    chosen = jax.random.randint(key_pick, (PAGES // PAGES_GRP, 1), 0, PAGES_GRP)
    return jnp.arange(PAGES_GRP)[None, :] == chosen


def draw_lengths(key, part):
    key = jax.random.fold_in(key, 11)
    key_draw, key_pick = jax.random.split(key)
    drawn_rows = jax.random.randint(key_draw, (PAGES // PAGES_GRP, PAGES_GRP), SEQ // 2, SEQ + 1)
    picked = chosen_slots(key_pick)
    return jnp.where(picked, SEQ, drawn_rows).reshape(PAGES).astype(jnp.int32)


def draw_patch_counts(key, part):
    key = jax.random.fold_in(key, 23)
    key_draw, key_pick = jax.random.split(key)
    smaller = jax.random.randint(key_draw, (PAGES // PAGES_GRP, PAGES_GRP), 0, 2)
    drawn_rows = jnp.where(smaller == 1, PATCHES // 4, PATCHES)
    picked = chosen_slots(key_pick)
    return jnp.where(picked, PATCHES, drawn_rows).reshape(PAGES).astype(jnp.int32)


def level_of(key, shape, pieces, low, top_value):
    def one(axis_at, blocks):
        heights = jax.random.uniform(jax.random.fold_in(jax.random.fold_in(key, 6), axis_at), (blocks,), jnp.float32, low / len(pieces), top_value / len(pieces))
        return jnp.repeat(jnp.exp(heights), shape[axis_at] // blocks).reshape((-1,) + (1,) * (len(shape) - axis_at - 1))

    gain = one(*pieces[0])
    for cut in pieces[1:]:
        gain = gain * one(*cut)
    return gain


def scatter_about(own_key, extent, width, most, cuts=(), dtype=jnp.bfloat16):
    level = level_of(own_key, extent, cuts, -0.22, 0.18) if cuts else 1.0
    array = jax.random.normal(own_key, extent, jnp.float32) * width * level
    return jnp.minimum(jnp.maximum(array, -most), most).astype(dtype)


def setup_inputs(seed: int = 0) -> dict:
    arg_keys = jax.random.split(jax.random.key(seed), 17)
    return {
        "tokens": scatter_about(arg_keys[0], (PAGES, SEQ, D), 1.0, 6.0, ((0, 16), (1, 8))),
        "memory": scatter_about(arg_keys[1], (PAGES, PATCHES, ENC), 1.0, 6.0, ((0, 16), (1, 8))),
        "lengths": draw_lengths(jax.random.fold_in(arg_keys[16], 71), 0),
        "patch_counts": draw_patch_counts(jax.random.fold_in(arg_keys[16], 71), 0),
        "self_qkv": scatter_about(arg_keys[4], (D, 3 * D), D ** -0.5, 0.1875),
        "self_out": scatter_about(arg_keys[5], (D, D), (max(D // 64, 1)) ** -0.5, 1.5),
        "cross_query": scatter_about(arg_keys[6], (D, D), D ** -0.5, 0.1875),
        "cross_kv": scatter_about(arg_keys[7], (ENC, 2 * D), ENC ** -0.5, 0.1875),
        "cross_out": scatter_about(arg_keys[8], (D, D), (max(D // 64, 1)) ** -0.5, 1.5),
        "ffn_in": scatter_about(arg_keys[9], (D, FF), D ** -0.5, 0.1875),
        "ffn_out": scatter_about(arg_keys[10], (FF, D), FF ** -0.5, 0.09375),
        "norm_gains": jnp.clip(1.0 + 0.1 * jax.random.normal(arg_keys[11], (3, D), jnp.float32), 0.5, 1.5),
        "norm_shifts": scatter_about(arg_keys[12], (3, D), 0.2, 3.0, (), jnp.float32),
        "proj_biases": scatter_about(arg_keys[13], (7, D), 0.2, 3.0, (), jnp.float32),
        "ffn_bias": scatter_about(arg_keys[14], (FF,), 0.2, 3.0, (), jnp.float32),
        "cotangent": scatter_about(arg_keys[15], (PAGES, SEQ, D), 1.0, 6.0, ((0, 16), (1, 8))),
    }


EPS = 1e-05
SCALE = 0.125
NEG = -1e+30
HIGH = lax.Precision.HIGHEST

@jax.custom_vjp
def low(v):
    return lax.optimization_barrier(v.astype(jnp.bfloat16)).astype(jnp.float32)

@jax.custom_vjp
def low_back(v):
    return v

def low_keep(v):
    return (low(v), None)

def low_pass(kept, grad):
    return (grad,)

def back_keep(v):
    return (v, None)

def back_low(kept, grad):
    return (low(grad),)
low.defvjp(low_keep, low_pass)
low_back.defvjp(back_keep, back_low)

def matmul(left_side, right_side):
    return jnp.dot(left_side, right_side, precision=HIGH)

def two_way(tensor):
    return low_back(low(tensor))

def normalize(inputs, gain_row, offset_row):
    centred = inputs - lax.optimization_barrier(jnp.mean(inputs, axis=-1, keepdims=True))
    spread = lax.optimization_barrier(jnp.mean(centred * centred, axis=-1, keepdims=True))
    return centred * lax.rsqrt(spread + EPS) * gain_row + offset_row

def attend(queries, key_rows, value_rows, allowed):
    scores = low_back(jnp.einsum('qhe,khe->hqk', queries, key_rows, precision=HIGH) * SCALE)
    scores = jnp.where(allowed[None], scores, NEG)
    shares = jax.nn.softmax(scores, axis=-1)
    return jnp.einsum('hqk,khe->qhe', low(shares), value_rows, precision=HIGH)

def page_layer(one_page, params):
    inputs, patches, length, patch_count = one_page
    self_qkv, self_out, cross_query, cross_kv, cross_out, ffn_in, ffn_out, norm_gains, norm_shifts, proj_biases, ffn_bias = params
    positions = jnp.arange(SEQ)
    causal = positions[None, :] <= positions[:, None]
    normed_one = low(normalize(inputs, norm_gains[0], norm_shifts[0]))
    joined = matmul(normed_one, self_qkv)
    queries = two_way(joined[:, :D] + proj_biases[0]).reshape(SEQ, HEADS, HEAD)
    key_rows = two_way(joined[:, D:2 * D]).reshape(SEQ, HEADS, HEAD)
    value_rows = two_way(joined[:, 2 * D:] + proj_biases[1]).reshape(SEQ, HEADS, HEAD)
    mixture = two_way(attend(queries, key_rows, value_rows, causal).reshape(SEQ, D))
    after_self = inputs + low_back(matmul(mixture, self_out)) + proj_biases[2]
    normed_two = low(normalize(after_self, norm_gains[1], norm_shifts[1]))
    cross_queries = two_way(matmul(normed_two, cross_query) + proj_biases[3]).reshape(SEQ, HEADS, HEAD)
    patch_proj = matmul(patches, cross_kv)
    patch_keys = two_way(patch_proj[:, :D]).reshape(PATCHES, HEADS, HEAD)
    patch_values = two_way(patch_proj[:, D:] + proj_biases[4]).reshape(PATCHES, HEADS, HEAD)
    allowed = jnp.broadcast_to(jnp.arange(PATCHES)[None, :] < patch_count, (SEQ, PATCHES))
    cross_mixture = two_way(attend(cross_queries, patch_keys, patch_values, allowed).reshape(SEQ, D))
    after_cross = after_self + low_back(matmul(cross_mixture, cross_out)) + proj_biases[5]
    normed_three = low(normalize(after_cross, norm_gains[2], norm_shifts[2]))
    before = low_back(matmul(normed_three, ffn_in) + ffn_bias)
    hidden = low(jax.nn.gelu(before, approximate=False))
    result = after_cross + low_back(matmul(hidden, ffn_out)) + proj_biases[6]
    return jnp.where((positions < length)[:, None], result, 0.0)

def reference(tokens, memory, lengths, patch_counts, self_qkv, self_out, cross_query, cross_kv, cross_out, ffn_in, ffn_out, norm_gains, norm_shifts, proj_biases, ffn_bias, cotangent):
    params = tuple((matrix.astype(jnp.float32) for matrix in (self_qkv, self_out, cross_query, cross_kv, cross_out, ffn_in, ffn_out, norm_gains, norm_shifts, proj_biases, ffn_bias)))
    checked = jax.checkpoint(page_layer)

    def forward(token_rows, patch_rows, weights):
        return lax.map(lambda one_page: checked(one_page, weights), (token_rows, patch_rows, lengths, patch_counts))
    outputs, pullback = jax.vjp(forward, tokens.astype(jnp.float32), memory.astype(jnp.float32), params)
    token_grad, memory_grad, grads = pullback(cotangent.astype(jnp.float32))
    return (outputs.astype(jnp.bfloat16), token_grad.astype(jnp.bfloat16), memory_grad.astype(jnp.bfloat16), grads[0], grads[1], grads[2], grads[3], grads[4], grads[5], grads[6], grads[7], grads[8], grads[9], grads[10])
```

```python
import functools

import jax
import jax.numpy as jnp
import numpy as np
from jax import lax
from jax.experimental import pallas as pl
from jax.experimental.pallas import tpu as pltpu
from jax.sharding import PartitionSpec as P

EPS = 1e-05

BF = jnp.bfloat16
F32 = jnp.float32
NEG = -1e30
TILE = 256
PAIR = 128


def dot_tt(a, b):
    return lax.dot_general(a, b, (((1,), (1,)), ((), ())), preferred_element_type=F32)


def dot_nn(a, b):
    return lax.dot_general(a, b, (((1,), (0,)), ((), ())), preferred_element_type=F32)


def head_lanes(rows, head):
    lanes = lax.broadcasted_iota(jnp.int32, rows.shape, 1)
    mine = (lanes >= 64) if head else (lanes < 64)
    return jnp.where(mine, rows, jnp.zeros_like(rows))


def later_key():
    keys = lax.broadcasted_iota(jnp.int32, (TILE, TILE), 0)
    return keys > lax.broadcasted_iota(jnp.int32, (TILE, TILE), 1)


def span(tile):
    return pl.ds(tile * TILE, TILE)


def forward_tiles(key_tiles, causal, q_ref, k_ref, o_ref, lse_ref, vt_ref, s_ref):
    for i in range(q_ref.shape[0] // TILE):
        tiles = i + 1 if causal else key_tiles
        queries = q_ref[span(i), :] * 0.125
        halves = []
        for head in range(2):
            mine = head_lanes(queries, head)
            top = None
            for j in range(tiles):
                scores = dot_tt(k_ref[span(j), :], mine)
                if causal and j == i:
                    scores = jnp.where(later_key(), NEG, scores)
                s_ref[span(j), :] = scores
                tile_top = jnp.max(scores, axis=0, keepdims=True)
                top = tile_top if top is None else jnp.maximum(top, tile_top)
            total, mixed = None, None
            for j in range(tiles):
                shares = jnp.exp(s_ref[span(j), :] - top)
                tile_sum = jnp.sum(shares, axis=0, keepdims=True)
                tile_mix = dot_nn(vt_ref[:, span(j)], shares.astype(BF))
                total = tile_sum if total is None else total + tile_sum
                mixed = tile_mix if mixed is None else mixed + tile_mix
            lse_ref[0, head : head + 1, span(i)] = top + jnp.log(total)
            halves.append((mixed / total)[head * 64 : head * 64 + 64, :])
        o_ref[span(i), :] = jnp.concatenate(halves, axis=0).T.astype(o_ref.dtype)


def by_count(count_ref, tiles, run):
    if count_ref is None:
        run(tiles)
    else:
        count = count_ref[0]
        pl.when(count > TILE)(lambda: run(tiles))
        pl.when(count <= TILE)(lambda: run(1))


def forward_kernel(causal, *refs):
    if causal:
        count_ref, (q_ref, k_ref, v_ref, o_ref, lse_ref, vt_ref, s_ref) = None, refs
    else:
        count_ref, q_ref, k_ref, v_ref, o_ref, lse_ref, vt_ref, s_ref = refs
    vt_ref[...] = v_ref[...].T
    by_count(
        count_ref,
        k_ref.shape[0] // TILE,
        lambda tiles: forward_tiles(tiles, causal, q_ref, k_ref, o_ref, lse_ref, vt_ref, s_ref),
    )


def backward_tiles(
    key_tiles, causal, q_ref, k_ref, v_ref, o_ref, do_ref, lse_ref, dq_ref, kt_ref, dk_ref, dv_ref
):
    ones = jnp.ones((8, PAIR), F32)
    for i in range(q_ref.shape[0] // TILE):
        tiles = i + 1 if causal else key_tiles
        queries = q_ref[span(i), :] * 0.125
        grads = do_ref[span(i), :]
        halves = []
        for head in range(2):
            mine = head_lanes(queries, head)
            pulled = head_lanes(grads, head)
            weighed = pulled.astype(F32) * o_ref[span(i), :].astype(F32)
            dots = lax.dot_general(
                ones,
                weighed,
                (((1,), (1,)), ((), ())),
                preferred_element_type=F32,
                precision=lax.Precision.HIGHEST,
            )[0:1, :]
            level = lse_ref[0, head : head + 1, span(i)]
            drawn = None
            for j in range(tiles):
                shares = jnp.exp(dot_tt(k_ref[span(j), :], mine) - level)
                if causal and j == i:
                    shares = jnp.where(later_key(), 0.0, shares)
                grad_shares = dot_tt(v_ref[span(j), :], pulled)
                grad_scores = (shares * (grad_shares - dots)).astype(BF)
                dv_ref[span(j), :] += dot_nn(shares.astype(BF), pulled)
                dk_ref[span(j), :] += dot_nn(grad_scores, mine)
                tile_drawn = dot_nn(kt_ref[:, span(j)], grad_scores)
                drawn = tile_drawn if drawn is None else drawn + tile_drawn
            halves.append(drawn[head * 64 : head * 64 + 64, :] * 0.125)
        dq_ref[span(i), :] = jnp.concatenate(halves, axis=0).T.astype(dq_ref.dtype)


def backward_kernel(causal, *refs):
    count_ref = None if causal else refs[0]
    refs = refs if causal else refs[1:]
    q_ref, k_ref, v_ref, o_ref, do_ref, lse_ref, dq_ref, dk_out, dv_out, kt_ref, dk_ref, dv_ref = refs
    kt_ref[...] = k_ref[...].T
    dk_ref[...] = jnp.zeros_like(dk_ref)
    dv_ref[...] = jnp.zeros_like(dv_ref)
    by_count(
        count_ref,
        k_ref.shape[0] // TILE,
        lambda tiles: backward_tiles(
            tiles, causal, q_ref, k_ref, v_ref, o_ref, do_ref, lse_ref, dq_ref, kt_ref, dk_ref, dv_ref
        ),
    )
    dk_out[...] = dk_ref[...].astype(BF)
    dv_out[...] = dv_ref[...].astype(BF)


def column_block(rows, first=0):
    return pl.BlockSpec((rows, PAIR), lambda p: (0, first + p))


LSE_BLOCK = lambda rows: pl.BlockSpec((1, 2, rows), lambda p: (p, 0, 0))
SCALAR = pl.BlockSpec(memory_space=pltpu.SMEM)


def attend(q_rows, key_rows, pairs, causal, q, k, v, firsts, count=None):
    specs = [column_block(q_rows, firsts[0]), column_block(key_rows, firsts[1]), column_block(key_rows, firsts[2])]
    flops = pairs * 2 * q_rows * key_rows * 64 * 4
    return pl.pallas_call(
        functools.partial(forward_kernel, causal),
        grid=(pairs,),
        in_specs=([] if causal else [SCALAR]) + specs,
        out_specs=[column_block(q_rows), LSE_BLOCK(q_rows)],
        out_shape=[
            jax.ShapeDtypeStruct((q_rows, pairs * PAIR), BF),
            jax.ShapeDtypeStruct((pairs, 2, q_rows), F32),
        ],
        scratch_shapes=[pltpu.VMEM((PAIR, key_rows), BF), pltpu.VMEM((key_rows, TILE), F32)],
        compiler_params=pltpu.CompilerParams(vmem_limit_bytes=32 * 1024 * 1024),
        cost_estimate=pl.CostEstimate(flops=flops, bytes_accessed=4 * 1024 * 1024, transcendentals=flops // 256),
    )(*(() if causal else (count,)), q, k, v)


def attend_back(q_rows, key_rows, pairs, causal, q, k, v, firsts, o, do, lse, count=None):
    specs = [
        column_block(q_rows, firsts[0]),
        column_block(key_rows, firsts[1]),
        column_block(key_rows, firsts[2]),
        column_block(q_rows),
        column_block(q_rows),
        LSE_BLOCK(q_rows),
    ]
    flops = pairs * 2 * q_rows * key_rows * 64 * 10
    return pl.pallas_call(
        functools.partial(backward_kernel, causal),
        grid=(pairs,),
        in_specs=([] if causal else [SCALAR]) + specs,
        out_specs=[column_block(q_rows), column_block(key_rows), column_block(key_rows)],
        out_shape=[
            jax.ShapeDtypeStruct((q_rows, pairs * PAIR), BF),
            jax.ShapeDtypeStruct((key_rows, pairs * PAIR), BF),
            jax.ShapeDtypeStruct((key_rows, pairs * PAIR), BF),
        ],
        scratch_shapes=[
            pltpu.VMEM((PAIR, key_rows), BF),
            pltpu.VMEM((key_rows, PAIR), F32),
            pltpu.VMEM((key_rows, PAIR), F32),
        ],
        compiler_params=pltpu.CompilerParams(vmem_limit_bytes=32 * 1024 * 1024),
        cost_estimate=pl.CostEstimate(flops=flops, bytes_accessed=8 * 1024 * 1024, transcendentals=flops // 640),
    )(*(() if causal else (count,)), q, k, v, o, do, lse)

AXES = ("y", "xl", "c", "z", "xh")
MESH_SHAPE = (4, 2, 2, 4, 2)
RING = 4


def ring_pairs(step):
    return [(i, (i + step) % RING) for i in range(RING)]


def x_slot(x):
    return (x % 2) * 2 + x // 2


def x_pairs(step):
    return [(x_slot(x), x_slot((x + step) % RING)) for x in range(RING)]


FLIP = [(0, 1), (1, 0)]
STEPS = (1, 3, 2)


def around(step, coord):
    return lax.rem(coord + step, RING)


def swap_in(blocks, side):
    own = lax.dynamic_index_in_dim(blocks, side, 0, keepdims=False)
    got = lax.ppermute(lax.dynamic_index_in_dim(blocks, 1 - side, 0, keepdims=False), "xh", FLIP)
    return jnp.concatenate([jnp.where(side == 0, own, got), jnp.where(side == 0, got, own)], axis=0)


def swap_out(rows, side):
    blocks = rows.reshape(2, rows.shape[0] // 2, rows.shape[1])
    own = lax.dynamic_index_in_dim(blocks, side, 0, keepdims=False)
    got = lax.ppermute(lax.dynamic_index_in_dim(blocks, 1 - side, 0, keepdims=False), "xh", FLIP)
    return jnp.stack([jnp.where(side == 0, own, got), jnp.where(side == 0, got, own)])


def spread(pick, place, z):
    place(z, pick(z))
    for step in STEPS:
        got = lax.ppermute(pick(around(step, z)), "z", ring_pairs(step))
        place(around(RING - step, z), got)


def gather_rows(rows, z):
    height = rows.shape[0]
    full = [jnp.zeros((RING * height, rows.shape[1]), rows.dtype)]

    def place(source, part):
        full[0] = lax.dynamic_update_slice(full[0], part, (source * height, 0))

    spread(lambda target: rows, place, z)
    return full[0]


def rows_to_heads(rows, z):
    height, width = rows.shape[0], rows.shape[1] // RING
    full = [jnp.zeros((RING * height, width), rows.dtype)]

    def place(source, part):
        full[0] = lax.dynamic_update_slice(full[0], part, (source * height, 0))

    spread(lambda target: lax.dynamic_slice(rows, (0, target * width), (height, width)), place, z)
    return full[0]


def heads_to_rows(heads, z):
    height, width = heads.shape[0] // RING, heads.shape[1]
    full = [jnp.zeros((height, RING * width), heads.dtype)]

    def place(source, part):
        full[0] = lax.dynamic_update_slice(full[0], part, (0, source * width))

    spread(lambda target: lax.dynamic_slice(heads, (target * height, 0), (height, width)), place, z)
    return full[0]


def ring_sum(pick, coord, axis, pairs):
    total = pick(coord).astype(F32)
    for step in STEPS:
        got = lax.ppermute(pick(around(step, coord)).astype(BF), axis, pairs(step))
        total = total + got.astype(F32)
    return total


def after(value, *others):
    return lax.optimization_barrier((value, *others))[0]


def product(left, right):
    return jnp.dot(left, right, preferred_element_type=F32)


def back_product(grads, matrix):
    return lax.dot_general(grads, matrix, (((1,), (1,)), ((), ())), preferred_element_type=F32)


def outer(grads, inputs):
    return lax.dot_general(grads, inputs, (((0,), (0,)), ((), ())), preferred_element_type=F32)


def unit(rows):
    centred = rows - jnp.mean(rows, axis=-1, keepdims=True)
    inverse = lax.rsqrt(jnp.mean(centred * centred, axis=-1, keepdims=True) + EPS)
    return centred * inverse, inverse


def unit_back(normal, inverse, grads, gain):
    scaled = grads * gain
    mean = jnp.mean(scaled, axis=-1, keepdims=True)
    along = jnp.mean(scaled * normal, axis=-1, keepdims=True)
    return inverse * (scaled - mean - normal * along)


def chunks_kernel(weights, coord_ref, go_ref, gg_ref, xo_ref, xg_ref, *refs):
    outs, turned_ref = refs[:RING], refs[RING]
    width, tokens = outs[0].shape[0], go_ref.shape[0]
    step = pl.program_id(0)

    @pl.when(step == 0)
    def _():
        for weight in range(weights):
            for place, hop in enumerate((0,) + STEPS):
                at = weight * RING * width + around(hop, coord_ref[0]) * width
                cols = pl.ds(pl.multiple_of(at, 128), width)
                turned_ref[weight, place * width : place * width + width, :tokens] = go_ref[:, cols].T
                turned_ref[weight, place * width : place * width + width, tokens:] = gg_ref[:, cols].T

    weight = step // (pl.num_programs(0) // weights)
    for place, out in enumerate(outs):
        rows = turned_ref.at[weight, place * width : place * width + width, :]
        total = dot_nn(rows[:, :tokens], xo_ref[...]) + dot_nn(rows[:, tokens:], xg_ref[...])
        out[...] = total.astype(out.dtype)


def outer_chunks(coord, grads, got_grads, inputs, got_inputs, features, weights=1, first=0, got_first=0):
    tokens, cols = grads.shape
    width, block = cols // (RING * weights), 512
    flops = 4 * tokens * cols * features // weights
    whole = lambda rows: pl.BlockSpec((rows, cols), lambda j: (0, 0))
    part = lambda at: pl.BlockSpec((tokens, block), lambda j: (0, at // block + j))
    own = pl.BlockSpec((width, block), lambda j: (0, j))
    return pl.pallas_call(
        functools.partial(chunks_kernel, weights),
        grid=(features // block,),
        in_specs=[SCALAR, whole(tokens), whole(tokens), part(first), part(got_first)],
        out_specs=[own] * RING,
        out_shape=[jax.ShapeDtypeStruct((width, features), F32)]
        + [jax.ShapeDtypeStruct((width, features), BF)] * 3,
        scratch_shapes=[pltpu.VMEM((weights, RING * width, 2 * tokens), BF)],
        compiler_params=pltpu.CompilerParams(vmem_limit_bytes=32 * 1024 * 1024),
        cost_estimate=pl.CostEstimate(
            flops=flops, bytes_accessed=10 * width * features + 4 * tokens * (cols + features), transcendentals=0
        ),
    )(coord.reshape(1), grads, got_grads, inputs, got_inputs)


def column_sums(rows):
    return jnp.sum(rows.astype(F32), axis=0)


def eight_order():
    cols = np.arange(1024).reshape(4, 2, 2, 4, 2, 8)
    return cols.transpose(2, 4, 1, 0, 3, 5).reshape(-1)


def shuffle_matrix(order):
    cols = order.shape[0]
    return (lax.broadcasted_iota(jnp.int32, (cols, cols), 0) == order[None, :]).astype(BF)


def qkv_order():
    order = np.zeros((4, 32, 3, 8), np.int32)
    pairs = [[], [], []]
    for z in range(4):
        groups = [third * 128 + z * 32 + k for third in range(3) for k in range(32)]
        for slot in range(3):
            chosen = [g for g in groups if g % 3 == slot]
            for place, group in enumerate(chosen):
                c, x, y = place // 16, place // 4 % 4, place % 4
                source = (((y * 2 + x % 2) * 2 + c) * 4 + z) * 2 + x // 2
                pairs[slot].append((source, group // 3))
                local = (group // 128) * 256 + (group % 32) * 8
                order[z, place, slot] = local + np.arange(8)
    return order.reshape(4, 768), pairs


def on_device(
    tokens,
    memory,
    lengths,
    patch_counts,
    self_qkv,
    self_out,
    cross_query,
    cross_kv,
    cross_out,
    ffn_in,
    ffn_out,
    norm_gains,
    norm_shifts,
    proj_biases,
    ffn_bias,
    cotangent,
):
    y, xl, c, z, xh = (lax.axis_index(axis) for axis in AXES)
    x = xh * 2 + xl
    width = tokens.shape[2]
    rows = 2 * tokens.shape[1]
    page_rows = RING * rows
    length = lax.dynamic_index_in_dim(lengths, xh, 0, keepdims=False)
    count = lax.dynamic_slice(patch_counts, (xh,), (1,))
    valid = (z * rows + jnp.arange(rows) < length)[:, None]

    def swap_cores(part):
        return lax.ppermute(part, "c", FLIP)

    eights = shuffle_matrix(jnp.asarray(eight_order()))

    def own_eights(grads):
        halves = product(grads, eights).astype(BF)
        return tuple(
            lax.dynamic_slice(halves, (0, side * 512), (grads.shape[0], 512)) for side in (c, 1 - c)
        )

    def own_wides(grads):
        cols = grads.shape[1] // 16
        pairs = [
            (grads[:, at : at + cols], grads[:, at + cols : at + 2 * cols])
            for at in range(0, grads.shape[1], 2 * cols)
        ]
        keep = jnp.concatenate([jnp.where(c == 0, a, b) for a, b in pairs], axis=1)
        send = jnp.concatenate([jnp.where(c == 0, b, a) for a, b in pairs], axis=1)
        return keep, send

    def sum_chunks(chunks, axis, pairs):
        total = chunks[0]
        for step, chunk in zip(STEPS, chunks[1:]):
            total = total + lax.ppermute(chunk, axis, pairs(step)).astype(F32)
        return total.astype(BF)

    def x_chunks(chunks):
        return sum_chunks(chunks, ("xl", "xh"), x_pairs)

    def y_chunks(chunks):
        return sum_chunks(chunks, "y", ring_pairs)

    def then_y(part):
        part = part.reshape(4, 32, part.shape[1])
        return ring_sum(
            lambda target: lax.dynamic_index_in_dim(part, target, 0, keepdims=False), y, "y", ring_pairs
        ).astype(BF)

    def then_x(part):
        each = part.shape[0] // 16
        part = part.reshape(2, 4, 2, each, part.shape[1])

        def cut(target):
            piece = lax.dynamic_slice(
                part, (target % 2, 0, target // 2, 0, 0), (1, 4, 1, each, part.shape[4])
            )
            return piece.reshape(4 * each, part.shape[4])

        return ring_sum(cut, x, ("xl", "xh"), x_pairs).astype(BF)

    def sum_z(parts):
        lines = [part.reshape(4, -1, 1024) for part in parts]
        line = jnp.concatenate(lines, axis=1)
        total = ring_sum(
            lambda target: lax.dynamic_index_in_dim(line, target, 0, keepdims=False), z, "z", ring_pairs
        )
        done, at = [], 0
        for part, own in zip(parts, lines):
            done.append(total[at : at + own.shape[1]].reshape(-1, part.shape[-1]))
            at += own.shape[1]
        return done

    own_tokens = swap_in(tokens, xh)
    joint = after(jnp.concatenate([memory, cotangent], axis=2), own_tokens)
    both = swap_in(joint, xh)
    own_memory = both[:, :width]
    grad_low = jnp.where(valid, both[:, width:], 0)
    page_tokens = gather_rows(own_tokens, z)
    normal_one, inverse_one = unit(page_tokens.astype(F32))
    low_one = (normal_one * norm_gains[0] + norm_shifts[0]).astype(BF)

    def head_cols(matrix, third):
        return lax.dynamic_slice(matrix, (0, third * width + z * 256), (matrix.shape[0], 256))

    heads_qkv = jnp.concatenate([head_cols(self_qkv, third) for third in range(3)], axis=1)
    bias_q = lax.dynamic_slice(proj_biases, (0, z * 256), (1, 256))
    bias_v = lax.dynamic_slice(proj_biases, (1, z * 256), (1, 256))
    bias_qkv = jnp.concatenate([bias_q, jnp.zeros_like(bias_q), bias_v], axis=1)
    joined = (product(low_one, heads_qkv) + bias_qkv).astype(BF)
    heads_mix, self_level = attend(page_rows, page_rows, 2, True, joined, joined, joined, (0, 2, 4))

    patch_proj = product(own_memory, cross_kv)
    patch_bias = jnp.concatenate([jnp.zeros_like(proj_biases[4]), proj_biases[4]])
    own_kv = after((patch_proj + patch_bias).astype(BF), page_tokens)
    page_kv = lax.all_gather(own_kv, "z", axis=0, tiled=True)

    mixture = heads_to_rows(heads_mix, z)
    after_self = own_tokens.astype(F32) + product(mixture, self_out) + proj_biases[2]
    normal_two, inverse_two = unit(after_self)
    low_two = (normal_two * norm_gains[1] + norm_shifts[1]).astype(BF)
    cross_queries = (product(low_two, cross_query) + proj_biases[3]).astype(BF)
    cross_mix, cross_level = attend(
        rows, page_rows, 8, False, cross_queries, page_kv, page_kv, (0, 0, 8), count
    )
    after_cross = after_self + product(cross_mix, cross_out) + proj_biases[5]
    normal_three, inverse_three = unit(after_cross)
    low_three = (normal_three * norm_gains[2] + norm_shifts[2]).astype(BF)
    before = product(low_three, ffn_in) + ffn_bias
    below = 0.5 * (1.0 + lax.erf(before * np.float32(np.sqrt(0.5))))
    hidden = (before * below).astype(BF)
    slope = below + before * jnp.exp(-0.5 * before * before) * np.float32(1 / np.sqrt(2 * np.pi))
    result = after_cross + product(hidden, ffn_out) + proj_biases[6]
    layer_out = swap_out(jnp.where(valid, result, 0.0).astype(BF), xh)

    early = jnp.concatenate([cross_mix, low_two, mixture, own_memory, low_three], axis=1)
    early_got = swap_cores(early)
    out_keep, out_send = own_eights(grad_low)
    hidden_got = swap_cores(jnp.concatenate([hidden, out_send], axis=1))
    ffn_out_chunks = outer_chunks(x, out_keep, hidden_got[:, 4 * width :], hidden, hidden_got, 4 * width)
    grad_before = (back_product(grad_low, ffn_out) * slope).astype(BF)
    in_keep, in_send = own_wides(grad_before)
    in_got = swap_cores(in_send)
    ffn_in_chunks = outer_chunks(
        y, in_keep, in_got, early, early_got, width, first=4 * width, got_first=4 * width
    )
    grad_three = back_product(grad_before, ffn_in)
    grad_after_cross = grad_low.astype(F32) + unit_back(
        normal_three, inverse_three, grad_three, norm_gains[2]
    )

    cross_low = grad_after_cross.astype(BF)
    grad_cross_mix = back_product(cross_low, cross_out).astype(BF)
    grad_cross_mix = after(grad_cross_mix, *ffn_out_chunks, *ffn_in_chunks)
    ffn_out_part = x_chunks(ffn_out_chunks)
    ffn_in_part = y_chunks(ffn_in_chunks)
    cross_query_low, patch_dk, patch_dv = attend_back(
        rows,
        page_rows,
        8,
        False,
        cross_queries,
        page_kv,
        page_kv,
        (0, 0, 8),
        cross_mix,
        grad_cross_mix,
        cross_level,
        count,
    )
    owned_grad = lax.psum_scatter(
        jnp.concatenate([patch_dk, patch_dv], axis=1), "z", scatter_dimension=0, tiled=True
    )
    grad_two = back_product(cross_query_low, cross_query)
    grad_after_self = grad_after_cross + unit_back(normal_two, inverse_two, grad_two, norm_gains[1])

    self_low = grad_after_self.astype(BF)
    grad_mixture = rows_to_heads(back_product(self_low, self_out).astype(BF), z)
    keeps, sends = zip(*(own_eights(grads) for grads in (cross_low, cross_query_low, self_low)))
    out_got = swap_cores(jnp.concatenate(sends, axis=1))
    three_chunks = outer_chunks(
        x, jnp.concatenate(keeps, axis=1), out_got, early, early_got, 3 * width, weights=3
    )
    grad_mixture = after(grad_mixture, *three_chunks, ffn_out_part, ffn_in_part)
    three_part = then_y(x_chunks(three_chunks))
    ffn_out_part = then_y(ffn_out_part)
    ffn_in_part = then_x(ffn_in_part)
    head_dq, head_dk, head_dv = attend_back(
        page_rows, page_rows, 2, True, joined, joined, joined, (0, 2, 4), heads_mix, grad_mixture, self_level
    )
    grad_joined = jnp.concatenate([head_dq, head_dk, head_dv], axis=1)
    grad_one = back_product(grad_joined, heads_qkv)
    grad_one_low = grad_one.astype(BF)
    grad_own = ring_sum(
        lambda target: lax.dynamic_slice(grad_one_low, (target * rows, 0), (rows, width)), z, "z", ring_pairs
    )
    own_normal, own_inverse = unit(own_tokens.astype(F32))
    token_rows = grad_after_self + unit_back(own_normal, own_inverse, grad_own, norm_gains[0])
    token_grad = swap_out(token_rows.astype(BF), xh)

    order, owner_pairs = qkv_order()
    shuffled = product(
        grad_joined, shuffle_matrix(lax.dynamic_index_in_dim(jnp.asarray(order), z, 0, keepdims=False))
    ).astype(BF)

    def core_half(target):
        return outer(lax.dynamic_slice(shuffled, (0, target * 384), (page_rows, 384)), low_one)

    core_sum = core_half(c) + swap_cores(core_half(1 - c).astype(BF)).astype(F32)
    core_sum = core_sum.astype(BF).reshape(4, 4, 24, width)
    def at_heads(sums):
        return lax.dynamic_update_slice(jnp.zeros((width,), F32), sums, (z * 256,))

    vectors = [
        column_sums(grad_one * normal_one),
        column_sums(grad_two * normal_two),
        column_sums(grad_three * normal_three),
        column_sums(grad_one),
        column_sums(grad_two),
        column_sums(grad_three),
        at_heads(column_sums(head_dq)),
        at_heads(column_sums(head_dv)),
        column_sums(grad_after_self),
        column_sums(cross_query_low),
        column_sums(owned_grad[:, width:]),
        column_sums(grad_after_cross),
        column_sums(grad_low),
    ]
    small = jnp.concatenate([jnp.stack(vectors), column_sums(grad_before).reshape(width, 4).T], axis=0)
    small = lax.dot_general(
        small, eights.astype(F32), (((1,), (0,)), ((), ())), precision=lax.Precision.HIGHEST
    )
    small = small.reshape(17, 2, 16, 4, 8).transpose(1, 2, 3, 0, 4).reshape(2, 16, 4, 17 * 8)
    small = jnp.pad(small, ((0, 0), (0, 0), (0, 0), (0, 256 - 17 * 8))).reshape(2, 16, width).astype(BF)
    small_keep = lax.dynamic_index_in_dim(small, c, 0, keepdims=False)
    small_send = lax.dynamic_index_in_dim(small, 1 - c, 0, keepdims=False)
    small_sum = (small_keep.astype(F32) + swap_cores(small_send).astype(F32)).astype(BF)
    small_sum = jnp.pad(small_sum.reshape(4, 4, 1, width), ((0, 0), (0, 0), (0, 7), (0, 0)))
    core_sum = jnp.concatenate([core_sum, small_sum], axis=2)
    x_sum = ring_sum(
        lambda target: lax.dynamic_index_in_dim(core_sum, target, 0, keepdims=False),
        x,
        ("xl", "xh"),
        x_pairs,
    ).astype(BF)
    y_sum = ring_sum(
        lambda target: lax.dynamic_index_in_dim(x_sum, target, 0, keepdims=False), y, "y", ring_pairs
    )
    small_part = jnp.pad(y_sum[24].astype(BF).reshape(4, 256), ((0, 0), (0, 768)))
    grad_qkv = jnp.concatenate(
        [lax.ppermute(y_sum[8 * slot : 8 * slot + 8], AXES, owner_pairs[slot]) for slot in range(3)], axis=0
    )

    memory_grad = swap_out(back_product(owned_grad, cross_kv).astype(BF), xh)
    kv_keep, kv_send = own_wides(owned_grad)
    cross_kv_chunks = outer_chunks(
        y, kv_keep, swap_cores(kv_send), early, early_got, width, first=3 * width, got_first=3 * width
    )
    cross_kv_part = then_x(y_chunks(cross_kv_chunks))

    ffn_out_rows, ffn_in_rows, three_rows, cross_kv_rows, small = sum_z(
        [ffn_out_part, ffn_in_part, three_part, cross_kv_part, small_part]
    )
    cross_out_rows, cross_query_rows, self_out_rows = (
        three_rows[:, at * width : at * width + width] for at in range(3)
    )
    small = small[0, : 17 * 8].reshape(17, 8)

    return (
        layer_out,
        token_grad,
        memory_grad,
        grad_qkv.T,
        self_out_rows.T,
        cross_query_rows.T,
        cross_kv_rows.T,
        cross_out_rows.T,
        ffn_in_rows.T,
        ffn_out_rows.T,
        small[:3],
        small[3:6],
        small[6:13],
        small[13:].T.reshape(-1),
    )


def solution(mesh):
    split = jax.sharding.Mesh(mesh.devices.reshape(MESH_SHAPE), AXES)
    page, blk = AXES[:3], AXES[3:]
    blocks, cols = P(page, blk, None), P(None, AXES)
    in_specs = (blocks, blocks, P(page), P(page)) + (P(),) * 11 + (blocks,)
    out_specs = (blocks,) * 3 + (cols,) * 10 + (P(AXES),)
    return jax.shard_map(
        on_device, mesh=split, in_specs=in_specs, out_specs=out_specs, check_vma=False
    )
```

```python
import functools

import jax
import jax.numpy as jnp
import numpy as np
from jax import lax
from jax.experimental import pallas as pl
from jax.experimental.pallas import tpu as pltpu
from jax.sharding import PartitionSpec as P

EPS = 1e-05

BF = jnp.bfloat16
F32 = jnp.float32
NEG = -1e30
TILE = 256
PAIR = 128


def dot_tt(a, b):
    return lax.dot_general(a, b, (((1,), (1,)), ((), ())), preferred_element_type=F32)


def dot_nn(a, b):
    return lax.dot_general(a, b, (((1,), (0,)), ((), ())), preferred_element_type=F32)


def head_lanes(rows, head):
    lanes = lax.broadcasted_iota(jnp.int32, rows.shape, 1)
    mine = (lanes >= 64) if head else (lanes < 64)
    return jnp.where(mine, rows, jnp.zeros_like(rows))


def later_key():
    keys = lax.broadcasted_iota(jnp.int32, (TILE, TILE), 0)
    return keys > lax.broadcasted_iota(jnp.int32, (TILE, TILE), 1)


def span(tile):
    return pl.ds(tile * TILE, TILE)


def forward_tiles(key_tiles, causal, q_ref, k_ref, o_ref, lse_ref, vt_ref, s_ref):
    for i in range(q_ref.shape[0] // TILE):
        tiles = i + 1 if causal else key_tiles
        queries = q_ref[span(i), :] * 0.125
        halves = []
        for head in range(2):
            mine = head_lanes(queries, head)
            top = None
            for j in range(tiles):
                scores = dot_tt(k_ref[span(j), :], mine)
                if causal and j == i:
                    scores = jnp.where(later_key(), NEG, scores)
                s_ref[span(j), :] = scores
                tile_top = jnp.max(scores, axis=0, keepdims=True)
                top = tile_top if top is None else jnp.maximum(top, tile_top)
            total, mixed = None, None
            for j in range(tiles):
                shares = jnp.exp(s_ref[span(j), :] - top)
                tile_sum = jnp.sum(shares, axis=0, keepdims=True)
                tile_mix = dot_nn(vt_ref[:, span(j)], shares.astype(BF))
                total = tile_sum if total is None else total + tile_sum
                mixed = tile_mix if mixed is None else mixed + tile_mix
            lse_ref[0, head : head + 1, span(i)] = top + jnp.log(total)
            halves.append((mixed / total)[head * 64 : head * 64 + 64, :])
        o_ref[span(i), :] = jnp.concatenate(halves, axis=0).T.astype(o_ref.dtype)


def by_count(count_ref, tiles, run):
    if count_ref is None:
        run(tiles)
    else:
        count = count_ref[0]
        pl.when(count > TILE)(lambda: run(tiles))
        pl.when(count <= TILE)(lambda: run(1))


def forward_kernel(causal, *refs):
    if causal:
        count_ref, (q_ref, k_ref, v_ref, o_ref, lse_ref, vt_ref, s_ref) = None, refs
    else:
        count_ref, q_ref, k_ref, v_ref, o_ref, lse_ref, vt_ref, s_ref = refs
    vt_ref[...] = v_ref[...].T
    by_count(
        count_ref,
        k_ref.shape[0] // TILE,
        lambda tiles: forward_tiles(tiles, causal, q_ref, k_ref, o_ref, lse_ref, vt_ref, s_ref),
    )


def backward_tiles(
    key_tiles, causal, q_ref, k_ref, v_ref, o_ref, do_ref, lse_ref, dq_ref, kt_ref, dk_ref, dv_ref
):
    ones = jnp.ones((8, PAIR), F32)
    for i in range(q_ref.shape[0] // TILE):
        tiles = i + 1 if causal else key_tiles
        queries = q_ref[span(i), :] * 0.125
        grads = do_ref[span(i), :]
        halves = []
        for head in range(2):
            mine = head_lanes(queries, head)
            pulled = head_lanes(grads, head)
            weighed = pulled.astype(F32) * o_ref[span(i), :].astype(F32)
            dots = lax.dot_general(
                ones,
                weighed,
                (((1,), (1,)), ((), ())),
                preferred_element_type=F32,
                precision=lax.Precision.HIGHEST,
            )[0:1, :]
            level = lse_ref[0, head : head + 1, span(i)]
            drawn = None
            for j in range(tiles):
                shares = jnp.exp(dot_tt(k_ref[span(j), :], mine) - level)
                if causal and j == i:
                    shares = jnp.where(later_key(), 0.0, shares)
                grad_shares = dot_tt(v_ref[span(j), :], pulled)
                grad_scores = (shares * (grad_shares - dots)).astype(BF)
                dv_ref[span(j), :] += dot_nn(shares.astype(BF), pulled)
                dk_ref[span(j), :] += dot_nn(grad_scores, mine)
                tile_drawn = dot_nn(kt_ref[:, span(j)], grad_scores)
                drawn = tile_drawn if drawn is None else drawn + tile_drawn
            halves.append(drawn[head * 64 : head * 64 + 64, :] * 0.125)
        dq_ref[span(i), :] = jnp.concatenate(halves, axis=0).T.astype(dq_ref.dtype)


def backward_kernel(causal, *refs):
    count_ref = None if causal else refs[0]
    refs = refs if causal else refs[1:]
    q_ref, k_ref, v_ref, o_ref, do_ref, lse_ref, dq_ref, dkv_out, kt_ref, dk_ref, dv_ref = refs
    kt_ref[...] = k_ref[...].T
    dk_ref[...] = jnp.zeros_like(dk_ref)
    dv_ref[...] = jnp.zeros_like(dv_ref)
    by_count(
        count_ref,
        k_ref.shape[0] // TILE,
        lambda tiles: backward_tiles(
            tiles, causal, q_ref, k_ref, v_ref, o_ref, do_ref, lse_ref, dq_ref, kt_ref, dk_ref, dv_ref
        ),
    )
    dkv_out[0] = dk_ref[...].astype(BF)
    dkv_out[1] = dv_ref[...].astype(BF)


def column_block(rows, first=0):
    return pl.BlockSpec((rows, PAIR), lambda p: (0, first + p))


LSE_BLOCK = lambda rows: pl.BlockSpec((1, 2, rows), lambda p: (p, 0, 0))
SCALAR = pl.BlockSpec(memory_space=pltpu.SMEM)


def attend(q_rows, key_rows, pairs, causal, q, k, v, firsts, count=None):
    specs = [column_block(q_rows, firsts[0]), column_block(key_rows, firsts[1]), column_block(key_rows, firsts[2])]
    flops = pairs * 2 * q_rows * key_rows * 64 * 4
    return pl.pallas_call(
        functools.partial(forward_kernel, causal),
        grid=(pairs,),
        in_specs=([] if causal else [SCALAR]) + specs,
        out_specs=[column_block(q_rows), LSE_BLOCK(q_rows)],
        out_shape=[
            jax.ShapeDtypeStruct((q_rows, pairs * PAIR), BF),
            jax.ShapeDtypeStruct((pairs, 2, q_rows), F32),
        ],
        scratch_shapes=[pltpu.VMEM((PAIR, key_rows), BF), pltpu.VMEM((key_rows, TILE), F32)],
        compiler_params=pltpu.CompilerParams(vmem_limit_bytes=32 * 1024 * 1024),
        cost_estimate=pl.CostEstimate(flops=flops, bytes_accessed=4 * 1024 * 1024, transcendentals=flops // 256),
    )(*(() if causal else (count,)), q, k, v)


def attend_back(q_rows, key_rows, pairs, causal, q, k, v, firsts, o, do, lse, count=None):
    specs = [
        column_block(q_rows, firsts[0]),
        column_block(key_rows, firsts[1]),
        column_block(key_rows, firsts[2]),
        column_block(q_rows),
        column_block(q_rows),
        LSE_BLOCK(q_rows),
    ]
    flops = pairs * 2 * q_rows * key_rows * 64 * 10
    return pl.pallas_call(
        functools.partial(backward_kernel, causal),
        grid=(pairs,),
        in_specs=([] if causal else [SCALAR]) + specs,
        out_specs=[column_block(q_rows), pl.BlockSpec((2, key_rows, PAIR), lambda p: (0, 0, p))],
        out_shape=[
            jax.ShapeDtypeStruct((q_rows, pairs * PAIR), BF),
            jax.ShapeDtypeStruct((2, key_rows, pairs * PAIR), BF),
        ],
        scratch_shapes=[
            pltpu.VMEM((PAIR, key_rows), BF),
            pltpu.VMEM((key_rows, PAIR), F32),
            pltpu.VMEM((key_rows, PAIR), F32),
        ],
        compiler_params=pltpu.CompilerParams(vmem_limit_bytes=32 * 1024 * 1024),
        cost_estimate=pl.CostEstimate(flops=flops, bytes_accessed=8 * 1024 * 1024, transcendentals=flops // 640),
    )(*(() if causal else (count,)), q, k, v, o, do, lse)

AXES = ("y", "xl", "c", "z", "xh")
MESH_SHAPE = (4, 2, 2, 4, 2)
RING = 4


def ring_pairs(step):
    return [(i, (i + step) % RING) for i in range(RING)]


def x_slot(x):
    return (x % 2) * 2 + x // 2


def x_pairs(step):
    return [(x_slot(x), x_slot((x + step) % RING)) for x in range(RING)]


FLIP = [(0, 1), (1, 0)]
STEPS = (1, 3, 2)


def around(step, coord):
    return lax.rem(coord + step, RING)


def swap_in(blocks, side):
    own = lax.dynamic_index_in_dim(blocks, side, 0, keepdims=False)
    got = lax.ppermute(lax.dynamic_index_in_dim(blocks, 1 - side, 0, keepdims=False), "xh", FLIP)
    return jnp.concatenate([jnp.where(side == 0, own, got), jnp.where(side == 0, got, own)], axis=0)


def swap_out(rows, side):
    blocks = rows.reshape(2, rows.shape[0] // 2, rows.shape[1])
    own = lax.dynamic_index_in_dim(blocks, side, 0, keepdims=False)
    got = lax.ppermute(lax.dynamic_index_in_dim(blocks, 1 - side, 0, keepdims=False), "xh", FLIP)
    return jnp.stack([jnp.where(side == 0, own, got), jnp.where(side == 0, got, own)])


def exchange(pick, z, behind=()):
    got = [lax.ppermute(pick(around(step, z)), "z", ring_pairs(step)) for step in STEPS]
    got = lax.optimization_barrier((*got, *behind))[: len(STEPS)]
    return [(z, pick(z))] + [(around(RING - step, z), part) for step, part in zip(STEPS, got)]


def rows_to_heads(rows, z, behind=()):
    height, width = rows.shape[0], rows.shape[1] // RING
    full = jnp.zeros((RING * height, width), rows.dtype)
    pick = lambda target: lax.dynamic_slice(rows, (0, target * width), (height, width))
    for source, part in exchange(pick, z, behind):
        full = lax.dynamic_update_slice(full, part, (source * height, 0))
    return full


def heads_to_rows(heads, z, behind=()):
    height, width = heads.shape[0] // RING, heads.shape[1]
    full = jnp.zeros((height, RING * width), heads.dtype)
    pick = lambda target: lax.dynamic_slice(heads, (target * height, 0), (height, width))
    for source, part in exchange(pick, z, behind):
        full = lax.dynamic_update_slice(full, part, (0, source * width))
    return full


def ring_sum(pick, coord, axis, pairs):
    total = pick(coord).astype(F32)
    for step in STEPS:
        got = lax.ppermute(pick(around(step, coord)).astype(BF), axis, pairs(step))
        total = total + got.astype(F32)
    return total


def after(value, *others):
    return lax.optimization_barrier((value, *others))[0]


def product(left, right):
    return jnp.dot(left, right, preferred_element_type=F32)


def back_product(grads, matrix):
    return lax.dot_general(grads, matrix, (((1,), (1,)), ((), ())), preferred_element_type=F32)


def outer(grads, inputs):
    return lax.dot_general(grads, inputs, (((0,), (0,)), ((), ())), preferred_element_type=F32)


def unit(rows):
    centred = rows - jnp.mean(rows, axis=-1, keepdims=True)
    inverse = lax.rsqrt(jnp.mean(centred * centred, axis=-1, keepdims=True) + EPS)
    return centred * inverse, inverse


def unit_back(normal, inverse, grads, gain):
    scaled = grads * gain
    mean = jnp.mean(scaled, axis=-1, keepdims=True)
    along = jnp.mean(scaled * normal, axis=-1, keepdims=True)
    return inverse * (scaled - mean - normal * along)


def chunks_kernel(starts, coord_ref, *refs):
    count, (own_ref, plus_ref, minus_ref, far_a_ref, far_b_ref), turned_ref = len(starts), refs[-6:-1], refs[-1]
    extra_ref = refs[4 * count] if len(refs) > 4 * count + 6 else None
    width, tokens = own_ref.shape[0], refs[0].shape[0]
    half, each = width // 2, width // 4
    step, steps = pl.program_id(0), pl.num_programs(0)

    def put(pick):
        own_ref[...] = pick(0, 0, width).astype(F32)
        plus_ref[...] = pick(1, 0, width).astype(BF)
        minus_ref[...] = pick(3, 0, width).astype(BF)
        far_a_ref[...] = pick(2, 0, half).astype(BF)
        far_b_ref[...] = pick(2, half, half).astype(BF)

    @pl.when(step == 0)
    def _():
        for at in range(count):
            for hop in range(RING):
                cols = pl.ds(pl.multiple_of(around(hop, coord_ref[0]) * width, 128), width)
                turned_ref[at, hop * width : hop * width + width, :tokens] = refs[4 * at][:, cols].T
                turned_ref[at, hop * width : hop * width + width, tokens:] = refs[4 * at + 1][:, cols].T

    def products(at):
        def pick(hop, first, rows):
            turned = turned_ref.at[at, hop * width + first : hop * width + first + rows, :]
            total = dot_nn(turned[:, :tokens], refs[4 * at + 2][...])
            return total + dot_nn(turned[:, tokens:], refs[4 * at + 3][...])

        put(pick)

    def handed_on():
        def pick(hop, first, rows):
            target = around(hop, coord_ref[0])
            zs = range(first // each, (first + rows) // each)
            return jnp.concatenate([extra_ref[target % 2, zz, target // 2] for zz in zs], axis=0)

        put(pick)

    ends = starts[1:] + ((steps - 1 if extra_ref is not None else steps),)
    for at, (start, end) in enumerate(zip(starts, ends)):
        pl.when((step >= start) & (step < end))(functools.partial(products, at))
    if extra_ref is not None:
        pl.when(step == steps - 1)(handed_on)


def outer_chunks(coord, width, block, segments, extra=None):
    cols = RING * width
    tokens = segments[0][0][0].shape[0]
    starts, step, operands, specs = [], 0, [], []

    def columns(wide, first, blocks, start):
        return pl.BlockSpec((tokens, wide), lambda j: (0, first // wide + jnp.clip(j - start, 0, blocks - 1)))

    flops = 0
    for grads, got_grads, inputs, got_inputs, blocks in segments:
        starts.append(step)
        for (array, first), wide, many in (
            (grads, cols, 1),
            (got_grads, cols, 1),
            (inputs, block, blocks),
            (got_inputs, block, blocks),
        ):
            operands.append(array)
            specs.append(columns(wide, first, many, step))
        flops += 4 * tokens * cols * block * blocks
        step += blocks
    if extra is not None:
        operands.append(extra.reshape(2, 4, 2, width // 4, block))
        specs.append(pl.BlockSpec((2, 4, 2, width // 4, block), lambda j: (0, 0, 0, 0, 0)))
        step += 1
    out = lambda rows: pl.BlockSpec((rows, block), lambda j: (0, j))
    shape = lambda rows, dtype: jax.ShapeDtypeStruct((rows, step * block), dtype)
    return pl.pallas_call(
        functools.partial(chunks_kernel, tuple(starts)),
        grid=(step,),
        in_specs=[SCALAR] + specs,
        out_specs=[out(width)] * 3 + [out(width // 2)] * 2,
        out_shape=[shape(width, F32), shape(width, BF), shape(width, BF)] + [shape(width // 2, BF)] * 2,
        scratch_shapes=[pltpu.VMEM((len(segments), cols, 2 * tokens), BF)],
        compiler_params=pltpu.CompilerParams(vmem_limit_bytes=40 * 1024 * 1024),
        cost_estimate=pl.CostEstimate(
            flops=flops, bytes_accessed=10 * width * step * block, transcendentals=0
        ),
    )(coord.reshape(1), *operands)


def project_kernel(place_ref, *refs):
    early, late = refs[:RING], refs[RING : 2 * RING]
    matrix_ref, bias_ref, gain_ref, shift_ref, joined_ref, low_ref, normal_ref = refs[2 * RING :]

    def run(at):
        first = jnp.where(place_ref[1] == 0, early[at][...], late[at][...])
        second = jnp.where(place_ref[1] == 0, late[at][...], early[at][...])
        normal, _ = unit(jnp.concatenate([first, second], axis=0).astype(F32))
        low = (normal * gain_ref[...] + shift_ref[...]).astype(BF)
        low_ref[...] = low
        normal_ref[...] = normal.astype(BF)
        joined_ref[...] = (dot_nn(low, matrix_ref[...]) + bias_ref[...]).astype(BF)

    for at in range(RING):
        pl.when(pl.program_id(0) == at)(functools.partial(run, at))


def project_heads(z, side, early, late, matrix, bias, gain, shift):
    half, width = early[0].shape
    rows = 2 * half

    def row_block(j, place):
        hop = jnp.where(j == 0, 0, jnp.where(j == 1, STEPS[0], jnp.where(j == 2, STEPS[1], STEPS[2])))
        return (lax.rem(place[0] + RING - hop, RING), 0)

    whole = lambda shape: pl.BlockSpec(shape, lambda j, place: (0, 0))
    return pl.pallas_call(
        project_kernel,
        grid_spec=pltpu.PrefetchScalarGridSpec(
            num_scalar_prefetch=1,
            grid=(RING,),
            in_specs=[whole((half, width))] * 8
            + [whole((width, 768)), whole((1, 768)), whole((1, width)), whole((1, width))],
            out_specs=[
                pl.BlockSpec((rows, 768), row_block),
                pl.BlockSpec((rows, width), row_block),
                pl.BlockSpec((rows, width), row_block),
            ],
        ),
        out_shape=[
            jax.ShapeDtypeStruct((RING * rows, 768), BF),
            jax.ShapeDtypeStruct((RING * rows, width), BF),
            jax.ShapeDtypeStruct((RING * rows, width), BF),
        ],
        compiler_params=pltpu.CompilerParams(vmem_limit_bytes=40 * 1024 * 1024),
        cost_estimate=pl.CostEstimate(
            flops=2 * RING * rows * width * 768, bytes_accessed=8 * 1024 * 1024, transcendentals=0
        ),
    )(jnp.stack([z, side]), *early, *late, matrix, bias, gain, shift)


def split_kernel(core_ref, grads_ref, keep_ref, send_ref):
    for at in range(grads_ref.shape[1] // 512):
        first = grads_ref[:, 512 * at : 512 * at + 256]
        second = grads_ref[:, 512 * at + 256 : 512 * at + 512]
        keep_ref[:, 256 * at : 256 * at + 256] = jnp.where(core_ref[0] == 0, first, second)
        send_ref[:, 256 * at : 256 * at + 256] = jnp.where(core_ref[0] == 0, second, first)


def split_wides(core, grads):
    rows, cols = grads.shape
    put = pl.BlockSpec((rows // 2, cols // 2), lambda j: (j, 0))
    return pl.pallas_call(
        split_kernel,
        grid=(2,),
        in_specs=[SCALAR, pl.BlockSpec((rows // 2, cols), lambda j: (j, 0))],
        out_specs=[put, put],
        out_shape=[jax.ShapeDtypeStruct((rows, cols // 2), BF)] * 2,
        compiler_params=pltpu.CompilerParams(vmem_limit_bytes=32 * 1024 * 1024),
        cost_estimate=pl.CostEstimate(flops=1024, bytes_accessed=4 * rows * cols, transcendentals=0),
    )(core.reshape(1), grads)


def patch_kernel(side_ref, grads_ref, inputs_ref, out_ref):
    out_ref[...] = outer(grads_ref[0], inputs_ref[...]).astype(out_ref.dtype)


def patch_outer(side, grads, inputs, dtype):
    patches, width = inputs.shape
    return pl.pallas_call(
        patch_kernel,
        grid_spec=pltpu.PrefetchScalarGridSpec(
            num_scalar_prefetch=1,
            grid=(8,),
            in_specs=[
                pl.BlockSpec((1, patches, 128), lambda j, side: (j // 4, 0, j % 4 * 2 + side[0])),
                pl.BlockSpec((patches, width), lambda j, side: (0, 0)),
            ],
            out_specs=pl.BlockSpec((128, width), lambda j, side: (j, 0)),
        ),
        out_shape=jax.ShapeDtypeStruct((1024, width), dtype),
        compiler_params=pltpu.CompilerParams(vmem_limit_bytes=32 * 1024 * 1024),
        cost_estimate=pl.CostEstimate(
            flops=2 * patches * 1024 * width, bytes_accessed=10 * 1024 * 1024, transcendentals=0
        ),
    )(side.reshape(1), grads, inputs)


def column_sums(rows):
    return jnp.sum(rows.astype(F32), axis=0)


def eight_order():
    cols = np.arange(1024).reshape(4, 2, 2, 4, 2, 8)
    return cols.transpose(2, 4, 1, 0, 3, 5).reshape(-1)


def shuffle_matrix(order):
    cols = order.shape[0]
    return (lax.broadcasted_iota(jnp.int32, (cols, cols), 0) == order[None, :]).astype(BF)


def qkv_order():
    order = np.zeros((4, 32, 3, 8), np.int32)
    pairs = [[], [], []]
    for z in range(4):
        groups = [third * 128 + z * 32 + k for third in range(3) for k in range(32)]
        for slot in range(3):
            chosen = [g for g in groups if g % 3 == slot]
            for place, group in enumerate(chosen):
                c, x, y = place // 16, place // 4 % 4, place % 4
                source = (((y * 2 + x % 2) * 2 + c) * 4 + z) * 2 + x // 2
                pairs[slot].append((source, group // 3))
                local = (group // 128) * 256 + (group % 32) * 8
                order[z, place, slot] = local + np.arange(8)
    return order.reshape(4, 768), pairs


def on_device(
    tokens,
    memory,
    lengths,
    patch_counts,
    self_qkv,
    self_out,
    cross_query,
    cross_kv,
    cross_out,
    ffn_in,
    ffn_out,
    norm_gains,
    norm_shifts,
    proj_biases,
    ffn_bias,
    cotangent,
):
    y, xl, c, z, xh = (lax.axis_index(axis) for axis in AXES)
    x = xh * 2 + xl
    width = tokens.shape[2]
    rows = 2 * tokens.shape[1]
    page_rows = RING * rows
    length = lax.dynamic_index_in_dim(lengths, xh, 0, keepdims=False)
    count = lax.dynamic_slice(patch_counts, (xh,), (1,))
    valid = (z * rows + jnp.arange(rows) < length)[:, None]

    def swap_cores(part):
        return lax.ppermute(part, "c", FLIP)

    by_core = jnp.asarray(eight_order()).reshape(2, 512)
    eights = shuffle_matrix(by_core.reshape(-1))
    sides = shuffle_matrix(
        jnp.concatenate([lax.dynamic_index_in_dim(by_core, side, 0, keepdims=False) for side in (c, 1 - c)])
    )

    def own_eights(grads):
        return product(grads, sides).astype(BF)

    def relay(chunks, axis, pairs):
        return lax.ppermute(chunks[3], axis, pairs(1)), lax.ppermute(chunks[4], axis, pairs(3))

    def add_on(chunks, got):
        plus, minus, half = chunks[1], chunks[2], chunks[3].shape[0]
        got_a, got_b = (part.astype(F32) for part in got)
        plus = jnp.concatenate([(plus[:half].astype(F32) + got_a).astype(BF), plus[half:]], axis=0)
        minus = jnp.concatenate([minus[:half], (minus[half:].astype(F32) + got_b).astype(BF)], axis=0)
        return plus, minus

    def send_on(sums, axis, pairs):
        return lax.ppermute(sums[0], axis, pairs(1)), lax.ppermute(sums[1], axis, pairs(3))

    def finish(chunks, got):
        return (chunks[0] + got[0].astype(F32) + got[1].astype(F32)).astype(BF)

    X_RING, Y_RING = (("xl", "xh"), x_pairs), ("y", ring_pairs)

    def then_y(part):
        part = part.reshape(4, 32, part.shape[1])
        return ring_sum(
            lambda target: lax.dynamic_index_in_dim(part, target, 0, keepdims=False), y, "y", ring_pairs
        ).astype(BF)

    def then_x(part):
        each = part.shape[0] // 16
        part = part.reshape(2, 4, 2, each, part.shape[1])

        def cut(target):
            piece = lax.dynamic_slice(
                part, (target % 2, 0, target // 2, 0, 0), (1, 4, 1, each, part.shape[4])
            )
            return piece.reshape(4 * each, part.shape[4])

        return ring_sum(cut, x, ("xl", "xh"), x_pairs).astype(BF)

    def sum_z(parts):
        lines = [part.reshape(4, -1, 1024) for part in parts]
        line = jnp.concatenate(lines, axis=1)
        total = ring_sum(
            lambda target: lax.dynamic_index_in_dim(line, target, 0, keepdims=False), z, "z", ring_pairs
        )
        done, at = [], 0
        for part, own in zip(parts, lines):
            done.append(total[at : at + own.shape[1]].reshape(-1, part.shape[-1]))
            at += own.shape[1]
        return done

    mine = lax.dynamic_index_in_dim(tokens, xh, 0, keepdims=False)
    other = lax.dynamic_index_in_dim(tokens, 1 - xh, 0, keepdims=False)
    other = lax.ppermute(other, "xh", FLIP)
    early_rows = [mine] + [lax.ppermute(mine, "z", ring_pairs(step)) for step in STEPS]
    late_row = after(other, *early_rows)
    late_rows = [late_row] + [lax.ppermute(late_row, "z", ring_pairs(step)) for step in STEPS]
    own_memory = swap_in(after(memory, *early_rows), xh)
    own_tokens = jnp.concatenate(
        [jnp.where(xh == 0, mine, late_row), jnp.where(xh == 0, late_row, mine)], axis=0
    )

    def head_cols(matrix, third):
        return lax.dynamic_slice(matrix, (0, third * width + z * 256), (matrix.shape[0], 256))

    heads_qkv = jnp.concatenate([head_cols(self_qkv, third) for third in range(3)], axis=1)
    bias_q = lax.dynamic_slice(proj_biases, (0, z * 256), (1, 256))
    bias_v = lax.dynamic_slice(proj_biases, (1, z * 256), (1, 256))
    bias_qkv = jnp.concatenate([bias_q, jnp.zeros_like(bias_q), bias_v], axis=1)
    joined, low_one, normal_one = project_heads(
        z, xh, early_rows, late_rows, heads_qkv, bias_qkv, norm_gains[0:1], norm_shifts[0:1]
    )
    heads_mix, self_level = attend(page_rows, page_rows, 2, True, joined, joined, joined, (0, 2, 4))

    page_memory = lax.all_gather(after(own_memory, *late_rows), "z", axis=0, tiled=True)
    patch_bias = jnp.concatenate([jnp.zeros_like(proj_biases[4]), proj_biases[4]])
    page_kv = (product(page_memory, cross_kv) + patch_bias).astype(BF)

    grad_low = jnp.where(valid, swap_in(after(cotangent, heads_mix), xh), 0)
    mixture = heads_to_rows(heads_mix, z, (page_kv,))
    after_self = own_tokens.astype(F32) + product(mixture, self_out) + proj_biases[2]
    normal_two, inverse_two = unit(after_self)
    low_two = (normal_two * norm_gains[1] + norm_shifts[1]).astype(BF)
    cross_queries = (product(low_two, cross_query) + proj_biases[3]).astype(BF)
    cross_mix, cross_level = attend(
        rows, page_rows, 8, False, cross_queries, page_kv, page_kv, (0, 0, 8), count
    )
    after_cross = after_self + product(cross_mix, cross_out) + proj_biases[5]
    normal_three, inverse_three = unit(after_cross)
    low_three = (normal_three * norm_gains[2] + norm_shifts[2]).astype(BF)
    before = product(low_three, ffn_in) + ffn_bias
    below = 0.5 * (1.0 + lax.erf(before * np.float32(np.sqrt(0.5))))
    hidden = (before * below).astype(BF)
    slope = below + before * jnp.exp(-0.5 * before * before) * np.float32(1 / np.sqrt(2 * np.pi))
    result = after_cross + product(hidden, ffn_out) + proj_biases[6]
    layer_rows = jnp.where(valid, result, 0.0).astype(BF)

    order, owner_pairs = qkv_order()
    head_order = lax.dynamic_index_in_dim(jnp.asarray(order), z, 0, keepdims=False)
    head_shuffle, sides = lax.optimization_barrier((shuffle_matrix(head_order), sides))

    out_grads = own_eights(grad_low)
    early = jnp.concatenate([cross_mix, low_two, mixture, low_three, out_grads[:, 512:]], axis=1)
    early_got = swap_cores(early)
    hidden_got = swap_cores(hidden)
    grad_before = (back_product(grad_low, ffn_out) * slope).astype(BF)
    before_sums = column_sums(grad_before)
    in_keep, in_send = split_wides(c, grad_before)
    in_got = swap_cores(in_send)
    grad_three = back_product(grad_before, ffn_in)
    grad_after_cross = grad_low.astype(F32) + unit_back(
        normal_three, inverse_three, grad_three, norm_gains[2]
    )
    cross_low = grad_after_cross.astype(BF)
    cross_grads = own_eights(cross_low)
    cross_got = swap_cores(cross_grads[:, 512:])
    grad_cross_mix = back_product(cross_low, cross_out).astype(BF)
    ffn_in_chunks = outer_chunks(
        y, 512, 512, [((in_keep, 0), (in_got, 0), (early, 3 * width), (early_got, 3 * width), 2)]
    )
    ffn_out_chunks = outer_chunks(
        x,
        128,
        width,
        [
            ((out_grads, 0), (early_got, 4 * width), (hidden, 0), (hidden_got, 0), 4),
            ((cross_grads, 0), (cross_got, 0), (early, 0), (early_got, 0), 1),
        ],
    )
    ffn_out_got = relay(ffn_out_chunks, *X_RING)
    ffn_in_got = relay(ffn_in_chunks, *Y_RING)

    grad_cross_mix, layer_rows, *got = lax.optimization_barrier(
        (grad_cross_mix, layer_rows, *ffn_out_got, *ffn_in_got)
    )
    ffn_out_sums, ffn_in_sums = add_on(ffn_out_chunks, got[:2]), add_on(ffn_in_chunks, got[2:])
    grad_cross_mix, *sums = lax.optimization_barrier((grad_cross_mix, *ffn_out_sums, *ffn_in_sums))
    ffn_out_got, ffn_in_got = send_on(sums[:2], *X_RING), send_on(sums[2:], *Y_RING)
    cross_query_low, patch_grads = attend_back(
        rows,
        page_rows,
        8,
        False,
        cross_queries,
        page_kv,
        page_kv,
        (0, 0, 8),
        cross_mix,
        grad_cross_mix,
        cross_level,
        count,
    )
    cross_query_low, patch_grads, layer_rows, *got = lax.optimization_barrier(
        (cross_query_low, patch_grads, layer_rows, *ffn_out_got, *ffn_in_got)
    )
    layer_out = swap_out(layer_rows, xh)
    ffn_out_part, ffn_in_part = finish(ffn_out_chunks, got[:2]), finish(ffn_in_chunks, got[2:])
    owned_grad = lax.psum_scatter(patch_grads, "z", scatter_dimension=1, tiled=True)
    grad_two = back_product(cross_query_low, cross_query)
    grad_after_self = grad_after_cross + unit_back(normal_two, inverse_two, grad_two, norm_gains[1])

    self_low = grad_after_self.astype(BF)
    grad_mix_rows = back_product(self_low, self_out).astype(BF)
    grads_here = after(patch_grads, grad_mix_rows)
    kv_send = patch_outer(1 - c, grads_here, page_memory, BF)
    grad_mixture = rows_to_heads(grad_mix_rows, z, (kv_send,))
    kv_got = swap_cores(kv_send)
    kv_rows = (patch_outer(c, grads_here, page_memory, BF).astype(F32) + kv_got.astype(F32)).astype(BF)
    kv_quarters = kv_rows.reshape(RING, 256, width)

    def kv_chunk(hop):
        return lax.dynamic_index_in_dim(kv_quarters, around(hop, y), 0, keepdims=False)

    kv_got = [lax.ppermute(kv_chunk(step), "y", ring_pairs(step)) for step in STEPS]
    query_grads, self_grads = own_eights(cross_query_low), own_eights(self_low)
    sent = swap_cores(jnp.concatenate([query_grads[:, 512:], self_grads[:, 512:]], axis=1))
    two_chunks = outer_chunks(
        x,
        128,
        width,
        [
            ((query_grads, 0), (sent, 0), (early, width), (early_got, width), 1),
            ((self_grads, 0), (sent, 512), (early, 2 * width), (early_got, 2 * width), 1),
        ],
        extra=ffn_in_part,
    )
    two_got = relay(two_chunks, *X_RING)
    ffn_out_part = then_y(ffn_out_part)
    owned_both = jnp.concatenate([owned_grad[0], owned_grad[1]], axis=1)
    memory_rows = back_product(owned_both, cross_kv).astype(BF)
    grad_mixture, layer_out, memory_rows, kv_rows = lax.optimization_barrier(
        (grad_mixture, layer_out, memory_rows, kv_rows, *two_chunks)
    )[:4]
    memory_grad = swap_out(memory_rows, xh)
    head_dq, head_dkv = attend_back(
        page_rows, page_rows, 2, True, joined, joined, joined, (0, 2, 4), heads_mix, grad_mixture, self_level
    )
    head_dq, head_dkv, memory_grad, *got = lax.optimization_barrier((head_dq, head_dkv, memory_grad, *two_got))
    head_dq, head_dkv, *sums = lax.optimization_barrier((head_dq, head_dkv, *add_on(two_chunks, got)))
    two_got = send_on(sums, *X_RING)
    head_dv = head_dkv[1]
    grad_joined = jnp.concatenate([head_dq, head_dkv[0], head_dv], axis=1)
    grad_one = back_product(grad_joined, heads_qkv)
    grad_one_low, *kv_got = lax.optimization_barrier((grad_one.astype(BF), *kv_got))
    kv_part = sum((got.astype(F32) for got in kv_got), kv_chunk(0).astype(F32)).astype(BF)

    def token_chunk(hop, first=0, height=rows):
        return lax.dynamic_slice(grad_one_low, (around(hop, z) * rows + first, 0), (height, width))

    half = rows // 2
    token_chunks = (
        token_chunk(0).astype(F32),
        token_chunk(1),
        token_chunk(3),
        token_chunk(2, 0, half),
        token_chunk(2, half, half),
    )
    Z_RING = ("z", ring_pairs)
    token_sums = add_on(token_chunks, relay(token_chunks, *Z_RING))
    got = send_on(token_sums, *Z_RING)
    grad_own = token_chunks[0] + got[0].astype(F32) + got[1].astype(F32)
    grad_own, own_tokens = lax.optimization_barrier((grad_own, own_tokens))
    two_part = finish(two_chunks, two_got)
    own_normal, own_inverse = unit(own_tokens.astype(F32))
    token_rows = grad_after_self + unit_back(own_normal, own_inverse, grad_own, norm_gains[0])
    token_grad = swap_out(token_rows.astype(BF), xh)

    shuffled = product(grad_joined, head_shuffle).astype(BF)

    def core_half(target):
        return outer(lax.dynamic_slice(shuffled, (0, target * 384), (page_rows, 384)), low_one)

    def at_heads(sums):
        return lax.dynamic_update_slice(jnp.zeros((width,), F32), sums, (z * 256,))

    vectors = [
        column_sums(grad_one * normal_one.astype(F32)),
        column_sums(grad_two * normal_two),
        column_sums(grad_three * normal_three),
        column_sums(grad_one),
        column_sums(grad_two),
        column_sums(grad_three),
        at_heads(column_sums(head_dq)),
        at_heads(column_sums(head_dv)),
        column_sums(grad_after_self),
        column_sums(cross_query_low),
        column_sums(patch_grads[1]),
        column_sums(grad_after_cross),
        column_sums(grad_low),
    ]
    small = jnp.concatenate([jnp.stack(vectors), before_sums.reshape(width, 4).T], axis=0)
    small = lax.dot_general(
        small, eights.astype(F32), (((1,), (0,)), ((), ())), precision=lax.Precision.HIGHEST
    )
    small = small.reshape(17, 2, 16, 4, 8).transpose(1, 2, 3, 0, 4).reshape(2, 16, 4, 17 * 8)
    small = jnp.pad(small, ((0, 0), (0, 0), (0, 0), (0, 256 - 17 * 8))).reshape(2, 16, width).astype(BF)
    small_keep = lax.dynamic_index_in_dim(small, c, 0, keepdims=False)
    small_send = lax.dynamic_index_in_dim(small, 1 - c, 0, keepdims=False)
    core_got = swap_cores(jnp.concatenate([core_half(1 - c).astype(BF), small_send], axis=0)).astype(F32)
    core_sum = (core_half(c) + core_got[:384]).astype(BF)
    small_sum = (small_keep.astype(F32) + core_got[384:]).astype(BF)
    core_sum, small_sum, two_part = lax.optimization_barrier((core_sum, small_sum, two_part))
    two_part, ffn_in_part = two_part[:, : 2 * width].reshape(4, 32, 2 * width), two_part[:, 2 * width :]
    small_sum = jnp.pad(small_sum.reshape(4, 4, 1, width), ((0, 0), (0, 0), (0, 7), (0, 0)))
    core_sum = jnp.concatenate([core_sum.reshape(4, 4, 24, width), small_sum], axis=2)
    kv_lines = kv_part.reshape(2, 4, 2, 16, width)

    def x_chunk(target):
        piece = lax.dynamic_slice(kv_lines, (target % 2, 0, target // 2, 0, 0), (1, 4, 1, 16, width))
        lines = lax.dynamic_index_in_dim(core_sum, target, 0, keepdims=False)
        return jnp.concatenate([lines.reshape(128, width), piece.reshape(64, width)], axis=0)

    x_sum = ring_sum(x_chunk, x, ("xl", "xh"), x_pairs).astype(BF)
    cross_kv_part = x_sum[128:]
    y_lines = jnp.concatenate([x_sum[:128].reshape(4, 32, width), two_part], axis=2)
    y_sum = ring_sum(
        lambda target: lax.dynamic_index_in_dim(y_lines, target, 0, keepdims=False), y, "y", ring_pairs
    )
    two_part, y_sum = y_sum[:, width:].astype(BF), y_sum[:, :width]
    small_part = jnp.pad(y_sum[24].astype(BF).reshape(4, 256), ((0, 0), (0, 768)))
    grad_qkv = jnp.concatenate(
        [lax.ppermute(y_sum[8 * slot : 8 * slot + 8], AXES, owner_pairs[slot]) for slot in range(3)], axis=0
    )

    ffn_out_rows, ffn_in_rows, two_rows, cross_kv_rows, small = sum_z(
        [ffn_out_part, ffn_in_part, two_part, cross_kv_part, small_part]
    )
    ffn_out_rows, cross_out_rows = ffn_out_rows[:, : 4 * width], ffn_out_rows[:, 4 * width :]
    cross_query_rows, self_out_rows = two_rows[:, :width], two_rows[:, width:]
    small = small[0, : 17 * 8].reshape(17, 8)

    return (
        layer_out,
        token_grad,
        memory_grad,
        grad_qkv.T,
        self_out_rows.T,
        cross_query_rows.T,
        cross_kv_rows.T,
        cross_out_rows.T,
        ffn_in_rows.T,
        ffn_out_rows.T,
        small[:3],
        small[3:6],
        small[6:13],
        small[13:].T.reshape(-1),
    )


def solution(mesh):
    split = jax.sharding.Mesh(mesh.devices.reshape(MESH_SHAPE), AXES)
    page, blk = AXES[:3], AXES[3:]
    blocks, cols = P(page, blk, None), P(None, AXES)
    in_specs = (blocks, blocks, P(page), P(page)) + (P(),) * 11 + (blocks,)
    out_specs = (blocks,) * 3 + (cols,) * 10 + (P(AXES),)
    return jax.shard_map(
        on_device, mesh=split, in_specs=in_specs, out_specs=out_specs, check_vma=False
    )
```

```python
import functools

import jax
import jax.numpy as jnp
import numpy as np
from jax import lax
from jax.experimental import pallas as pl
from jax.experimental.pallas import tpu as pltpu
from jax.sharding import PartitionSpec as P

EPS = 1e-05

BF = jnp.bfloat16
F32 = jnp.float32
NEG = -1e30
TILE = 256
PAIR = 128
HINT = pl.CostEstimate(flops=1 << 20, bytes_accessed=1 << 16, transcendentals=0)


def dot_tt(a, b):
    return lax.dot_general(a, b, (((1,), (1,)), ((), ())), preferred_element_type=F32)


def dot_nn(a, b):
    return lax.dot_general(a, b, (((1,), (0,)), ((), ())), preferred_element_type=F32)


def two_heads(rows):
    lanes = lax.broadcasted_iota(jnp.int32, rows.shape, 1)
    none = jnp.zeros_like(rows)
    return jnp.concatenate([jnp.where(lanes < 64, rows, none), jnp.where(lanes < 64, none, rows)], axis=0)


def later_key():
    keys = lax.broadcasted_iota(jnp.int32, (TILE, 2 * TILE), 0)
    return keys > lax.broadcasted_iota(jnp.int32, (TILE, 2 * TILE), 1) % TILE


def own_halves(both):
    return jnp.concatenate([both[:64, :TILE], both[64:, TILE:]], axis=0).T


def span(tile):
    return pl.ds(tile * TILE, TILE)


def forward_tiles(key_tiles, causal, q_ref, k_ref, o_ref, lse_ref, vt_ref, s_ref):
    for i in range(q_ref.shape[0] // TILE):
        tiles = i + 1 if causal else key_tiles
        queries = two_heads(q_ref[span(i), :] * 0.125)
        kept = s_ref.at[i % 2]
        top = None
        for j in range(tiles):
            scores = dot_tt(k_ref[span(j), :], queries)
            if causal and j == i:
                scores = jnp.where(later_key(), NEG, scores)
            kept[span(j), :] = scores
            tile_top = jnp.max(scores, axis=0, keepdims=True)
            top = tile_top if top is None else jnp.maximum(top, tile_top)
        total, mixed = None, None
        for j in range(tiles):
            shares = jnp.exp(kept[span(j), :] - top)
            tile_sum = jnp.sum(shares, axis=0, keepdims=True)
            tile_mix = dot_nn(vt_ref[:, span(j)], shares.astype(BF))
            total = tile_sum if total is None else total + tile_sum
            mixed = tile_mix if mixed is None else mixed + tile_mix
        level = top + jnp.log(total)
        lse_ref[0, 0:1, span(i)] = level[:, :TILE]
        lse_ref[0, 1:2, span(i)] = level[:, TILE:]
        o_ref[span(i), :] = own_halves(mixed / total).astype(o_ref.dtype)


def pair_columns(pair, first=0):
    return pl.ds(pl.multiple_of(pair * PAIR + first, PAIR), PAIR)


def every_pair(pairs, count_ref, tiles, run):
    def loop(live):
        @pl.loop(0, pairs // 2)
        def _(couple):
            run(2 * couple, 0, live)
            run(2 * couple + 1, 1, live)

    if count_ref is None:
        loop(tiles)
    else:
        pl.when(count_ref[0] > TILE)(lambda: loop(tiles))
        pl.when(count_ref[0] <= TILE)(lambda: loop(1))


def forward_kernel(pairs, causal, firsts, *refs):
    count_ref = None if causal else refs[0]
    refs = refs if causal else refs[1:]
    q_ref, k_ref, v_ref, o_ref, lse_ref, vt_ref, s_ref = refs

    def run(pair, slot, tiles):
        q, k, v = (ref.at[:, pair_columns(pair, at)] for ref, at in zip((q_ref, k_ref, v_ref), firsts))
        vt, kept = vt_ref.at[slot], s_ref.at[slot]
        vt[:, : tiles * TILE] = v[: tiles * TILE, :].T
        out, level = o_ref.at[:, pair_columns(pair)], lse_ref.at[pl.ds(pair, 1)]
        forward_tiles(tiles, causal, q, k, out, level, vt, kept)

    every_pair(pairs, count_ref, k_ref.shape[0] // TILE, run)


def backward_tiles(
    key_tiles, causal, q_ref, k_ref, v_ref, o_ref, do_ref, lse_ref, dq_ref, kt_ref, dk_ref, dv_ref
):
    ones = jnp.ones((8, PAIR), F32)
    for i in range(q_ref.shape[0] // TILE):
        tiles = i + 1 if causal else key_tiles
        queries = two_heads(q_ref[span(i), :] * 0.125)
        pulled = two_heads(do_ref[span(i), :])
        out = o_ref[span(i), :].astype(F32)
        weighed = pulled.astype(F32) * jnp.concatenate([out, out], axis=0)
        dots = lax.dot_general(
            ones,
            weighed,
            (((1,), (1,)), ((), ())),
            preferred_element_type=F32,
            precision=lax.Precision.HIGHEST,
        )[0:1, :]
        level = jnp.concatenate([lse_ref[0, 0:1, span(i)], lse_ref[0, 1:2, span(i)]], axis=1)
        drawn = None
        for j in range(tiles):
            shares = jnp.exp(dot_tt(k_ref[span(j), :], queries) - level)
            if causal and j == i:
                shares = jnp.where(later_key(), 0.0, shares)
            grad_shares = dot_tt(v_ref[span(j), :], pulled)
            grad_scores = (shares * (grad_shares - dots)).astype(BF)
            dv_part = dot_nn(shares.astype(BF), pulled)
            dk_part = dot_nn(grad_scores, queries)
            if i == (j if causal else 0):
                dv_ref[span(j), :] = dv_part
                dk_ref[span(j), :] = dk_part
            else:
                dv_ref[span(j), :] += dv_part
                dk_ref[span(j), :] += dk_part
            tile_drawn = dot_nn(kt_ref[:, span(j)], grad_scores)
            drawn = tile_drawn if drawn is None else drawn + tile_drawn
        dq_ref[span(i), :] = (own_halves(drawn) * 0.125).astype(dq_ref.dtype)


def backward_kernel(pairs, causal, firsts, *refs):
    count_ref = None if causal else refs[0]
    refs = refs if causal else refs[1:]
    q_ref, k_ref, v_ref, o_ref, do_ref, lse_ref, *outs, kt_ref, dk_ref, dv_ref = refs
    dq_ref, dkv_ref = outs[0], outs[-1]
    width = pairs * PAIR
    first = dkv_ref.shape[1] - 2 * width

    def run(pair, slot, tiles):
        q, k, v = (ref.at[:, pair_columns(pair, at)] for ref, at in zip((q_ref, k_ref, v_ref), firsts))
        cols, live = pair_columns(pair), tiles * TILE
        kt, dk, dv = kt_ref.at[slot], dk_ref.at[slot], dv_ref.at[slot]
        kt[:, :live] = k[:live, :].T
        if live < k.shape[0]:
            dk[...] = jnp.zeros_like(dk)
            dv[...] = jnp.zeros_like(dv)
        out, grads, level = o_ref.at[:, cols], do_ref.at[:, cols], lse_ref.at[pl.ds(pair, 1)]
        backward_tiles(
            tiles, causal, q, k, v, out, grads, level, dq_ref.at[:, cols], kt, dk, dv
        )
        dkv_ref[:, pair_columns(pair, first)] = dk[...].astype(BF)
        dkv_ref[:, pair_columns(pair, first + width)] = dv[...].astype(BF)

    every_pair(pairs, count_ref, k_ref.shape[0] // TILE, run)


SCALAR = pl.BlockSpec(memory_space=pltpu.SMEM)
HERE = pl.BlockSpec(memory_space=pltpu.VMEM)


def attend(q_rows, key_rows, pairs, causal, q, k, v, firsts, count=None):
    return pl.pallas_call(
        functools.partial(forward_kernel, pairs, causal, firsts),
        in_specs=([] if causal else [SCALAR]) + [HERE] * 3,
        out_specs=[HERE] * 2,
        out_shape=[
            jax.ShapeDtypeStruct((q_rows, pairs * PAIR), BF),
            jax.ShapeDtypeStruct((pairs, 2, q_rows), F32),
        ],
        scratch_shapes=[pltpu.VMEM((2, PAIR, key_rows), BF), pltpu.VMEM((2, 2, key_rows, 2 * TILE), F32)],
        compiler_params=pltpu.CompilerParams(vmem_limit_bytes=32 * 1024 * 1024),
        cost_estimate=HINT,
    )(*(() if causal else (count,)), q, k, v)


def attend_back(q_rows, key_rows, pairs, causal, q, k, v, firsts, o, do, lse, count=None):
    width = pairs * PAIR
    shapes = [jax.ShapeDtypeStruct((q_rows, width), BF), jax.ShapeDtypeStruct((key_rows, 2 * width), BF)]
    if causal:
        shapes = [jax.ShapeDtypeStruct((q_rows, 3 * width), BF)]
    return pl.pallas_call(
        functools.partial(backward_kernel, pairs, causal, firsts),
        in_specs=([] if causal else [SCALAR]) + [HERE] * 6,
        out_specs=[HERE] * len(shapes),
        out_shape=shapes,
        scratch_shapes=[
            pltpu.VMEM((2, PAIR, key_rows), BF),
            pltpu.VMEM((2, key_rows, PAIR), F32),
            pltpu.VMEM((2, key_rows, PAIR), F32),
        ],
        compiler_params=pltpu.CompilerParams(vmem_limit_bytes=32 * 1024 * 1024),
        cost_estimate=HINT,
    )(*(() if causal else (count,)), q, k, v, o, do, lse)

AXES = ("y", "xl", "c", "z", "xh")
MESH_SHAPE = (4, 2, 2, 4, 2)
RING = 4


def ring_pairs(step):
    return [(i, (i + step) % RING) for i in range(RING)]


def x_slot(x):
    return (x % 2) * 2 + x // 2


def x_pairs(step):
    return [(x_slot(x), x_slot((x + step) % RING)) for x in range(RING)]


FLIP = [(0, 1), (1, 0)]
STEPS = (1, 3, 2)


def around(step, coord):
    return lax.rem(coord + step, RING)


def swap_in(blocks, side):
    own = lax.dynamic_index_in_dim(blocks, side, 0, keepdims=False)
    got = lax.ppermute(lax.dynamic_index_in_dim(blocks, 1 - side, 0, keepdims=False), "xh", FLIP)
    return jnp.concatenate([jnp.where(side == 0, own, got), jnp.where(side == 0, got, own)], axis=0)


def swap_out(rows, side):
    blocks = rows.reshape(2, rows.shape[0] // 2, rows.shape[1])
    own = lax.dynamic_index_in_dim(blocks, side, 0, keepdims=False)
    got = lax.ppermute(lax.dynamic_index_in_dim(blocks, 1 - side, 0, keepdims=False), "xh", FLIP)
    return jnp.stack([jnp.where(side == 0, own, got), jnp.where(side == 0, got, own)])


def exchange(pick, z, behind=()):
    got = [lax.ppermute(pick(around(step, z)), "z", ring_pairs(step)) for step in STEPS]
    got = lax.optimization_barrier((*got, *behind))[: len(STEPS)]
    return [(z, pick(z))] + [(around(RING - step, z), part) for step, part in zip(STEPS, got)]


def rows_to_heads(rows, z, behind=()):
    height, width = rows.shape[0], rows.shape[1] // RING
    full = jnp.zeros((RING * height, width), rows.dtype)
    pick = lambda target: lax.dynamic_slice(rows, (0, target * width), (height, width))
    for source, part in exchange(pick, z, behind):
        full = lax.dynamic_update_slice(full, part, (source * height, 0))
    return full


def ring_sum(pick, coord, axis, pairs):
    total = pick(coord).astype(F32)
    for step in STEPS:
        got = lax.ppermute(pick(around(step, coord)).astype(BF), axis, pairs(step))
        total = total + got.astype(F32)
    return total


def after(value, *others):
    return lax.optimization_barrier((value, *others))[0]


def product(left, right):
    return jnp.dot(left, right, preferred_element_type=F32)


def back_product(grads, matrix):
    return lax.dot_general(grads, matrix, (((1,), (1,)), ((), ())), preferred_element_type=F32)


def outer(grads, inputs):
    return lax.dot_general(grads, inputs, (((0,), (0,)), ((), ())), preferred_element_type=F32)


def unit(rows):
    centred = rows - jnp.mean(rows, axis=-1, keepdims=True)
    inverse = lax.rsqrt(jnp.mean(centred * centred, axis=-1, keepdims=True) + EPS)
    return centred * inverse, inverse


def unit_back(normal, inverse, grads, gain):
    scaled = grads * gain
    mean = jnp.mean(scaled, axis=-1, keepdims=True)
    along = jnp.mean(scaled * normal, axis=-1, keepdims=True)
    return inverse * (scaled - mean - normal * along)


def chunks_kernel(width, block, segments, coord_ref, *refs):
    outs, turned_ref = refs[-6:-1], refs[-1]
    own_ref, plus_ref, minus_ref, far_a_ref, far_b_ref = outs
    tokens = refs[0].shape[0]
    half, each = width // 2, width // 4
    lane = 0

    def put(pick, lanes):
        own_ref[:, lanes] = pick(0, 0, width).astype(F32)
        plus_ref[:, lanes] = pick(1, 0, width).astype(BF)
        minus_ref[:, lanes] = pick(3, 0, width).astype(BF)
        far_a_ref[:, lanes] = pick(2, 0, half).astype(BF)
        far_b_ref[:, lanes] = pick(2, half, half).astype(BF)

    for at, (grads_at, got_grads_at, inputs_at, got_inputs_at, blocks) in enumerate(segments):
        grads_ref, got_grads_ref, inputs_ref, got_inputs_ref = refs[4 * at : 4 * at + 4]
        for hop in range(RING):
            column = around(hop, coord_ref[0]) * width
            rows = slice(hop * width, hop * width + width)
            turned_ref[at, rows, :tokens] = grads_ref[:, pl.ds(pl.multiple_of(grads_at + column, 128), width)].T
            turned_ref[at, rows, tokens:] = got_grads_ref[
                :, pl.ds(pl.multiple_of(got_grads_at + column, 128), width)
            ].T
        for number in range(blocks):
            mine = inputs_ref[:, inputs_at + number * block : inputs_at + number * block + block]
            got = got_inputs_ref[:, got_inputs_at + number * block : got_inputs_at + number * block + block]

            def pick(hop, first, rows, at=at, mine=mine, got=got):
                turned = turned_ref.at[at, hop * width + first : hop * width + first + rows, :]
                return dot_nn(turned[:, :tokens], mine) + dot_nn(turned[:, tokens:], got)

            put(pick, slice(lane, lane + block))
            lane += block

    if lane < own_ref.shape[1]:
        extra_ref = refs[4 * len(segments)]

        def pick(hop, first, rows):
            target = around(hop, coord_ref[0])
            zs = range(first // each, (first + rows) // each)
            return jnp.concatenate([extra_ref[target % 2, zz, target // 2] for zz in zs], axis=0)

        put(pick, slice(lane, own_ref.shape[1]))


def outer_chunks(coord, width, block, segments, extra=None):
    cols = RING * width
    tokens = segments[0][0][0].shape[0]
    operands = [array for segment in segments for array, _ in segment[:4]]
    places = tuple(tuple(first for _, first in segment[:4]) + (segment[4],) for segment in segments)
    lanes = sum(segment[4] for segment in segments) * block
    if extra is not None:
        operands.append(extra.reshape(2, 4, 2, width // 4, extra.shape[1]))
        lanes += extra.shape[1]
    shape = lambda rows, dtype: jax.ShapeDtypeStruct((rows, lanes), dtype)
    return pl.pallas_call(
        functools.partial(chunks_kernel, width, block, places),
        in_specs=[SCALAR] + [HERE] * len(operands),
        out_specs=[HERE] * 5,
        out_shape=[shape(width, F32), shape(width, BF), shape(width, BF)] + [shape(width // 2, BF)] * 2,
        scratch_shapes=[pltpu.VMEM((len(segments), cols, 2 * tokens), BF)],
        compiler_params=pltpu.CompilerParams(vmem_limit_bytes=40 * 1024 * 1024),
        cost_estimate=HINT,
    )(coord.reshape(1), *operands)


def project_kernel(place_ref, *refs):
    early, late = refs[:RING], refs[RING : 2 * RING]
    matrix_ref, bias_ref, gain_ref, shift_ref, joined_ref, low_ref, normal_ref = refs[2 * RING :]

    def run(at):
        first = jnp.where(place_ref[1] == 0, early[at][...], late[at][...])
        second = jnp.where(place_ref[1] == 0, late[at][...], early[at][...])
        normal, _ = unit(jnp.concatenate([first, second], axis=0).astype(F32))
        low = (normal * gain_ref[...] + shift_ref[...]).astype(BF)
        low_ref[...] = low
        normal_ref[...] = normal.astype(BF)
        joined_ref[...] = (dot_nn(low, matrix_ref[...]) + bias_ref[...]).astype(BF)

    for at in range(RING):
        pl.when(pl.program_id(0) == at)(functools.partial(run, at))


def project_heads(z, side, early, late, matrix, bias, gain, shift):
    half, width = early[0].shape
    rows = 2 * half

    def row_block(j, place):
        hop = jnp.where(j == 0, 0, jnp.where(j == 1, STEPS[0], jnp.where(j == 2, STEPS[1], STEPS[2])))
        return (lax.rem(place[0] + RING - hop, RING), 0)

    whole = lambda shape: pl.BlockSpec(shape, lambda j, place: (0, 0))
    return pl.pallas_call(
        project_kernel,
        grid_spec=pltpu.PrefetchScalarGridSpec(
            num_scalar_prefetch=1,
            grid=(RING,),
            in_specs=[whole((half, width))] * 8
            + [whole((width, 768)), whole((1, 768)), whole((1, width)), whole((1, width))],
            out_specs=[
                pl.BlockSpec((rows, 768), row_block),
                pl.BlockSpec((rows, width), row_block),
                pl.BlockSpec((rows, width), row_block),
            ],
        ),
        out_shape=[
            jax.ShapeDtypeStruct((RING * rows, 768), BF),
            jax.ShapeDtypeStruct((RING * rows, width), BF),
            jax.ShapeDtypeStruct((RING * rows, width), BF),
        ],
        compiler_params=pltpu.CompilerParams(vmem_limit_bytes=40 * 1024 * 1024),
        cost_estimate=HINT,
    )(jnp.stack([z, side]), *early, *late, matrix, bias, gain, shift)


def split_kernel(core_ref, grads_ref, keep_ref, send_ref):
    for at in range(grads_ref.shape[1] // 512):
        first = grads_ref[:, 512 * at : 512 * at + 256]
        second = grads_ref[:, 512 * at + 256 : 512 * at + 512]
        keep_ref[:, 256 * at : 256 * at + 256] = jnp.where(core_ref[0] == 0, first, second)
        send_ref[:, 256 * at : 256 * at + 256] = jnp.where(core_ref[0] == 0, second, first)


def split_wides(core, grads):
    rows, cols = grads.shape
    put = pl.BlockSpec((rows // 2, cols // 2), lambda j: (j, 0))
    return pl.pallas_call(
        split_kernel,
        grid=(2,),
        in_specs=[SCALAR, pl.BlockSpec((rows // 2, cols), lambda j: (j, 0))],
        out_specs=[put, put],
        out_shape=[jax.ShapeDtypeStruct((rows, cols // 2), BF)] * 2,
        compiler_params=pltpu.CompilerParams(vmem_limit_bytes=32 * 1024 * 1024),
        cost_estimate=HINT,
    )(core.reshape(1), grads)


def patch_halves_kernel(side_ref, grads_ref, inputs_ref, send_ref, keep_ref):
    for out_ref, side in ((send_ref, 1 - side_ref[0]), (keep_ref, side_ref[0])):
        for group in range(8):
            column = pl.multiple_of((group * 2 + side) * 128, 128)
            part = outer(grads_ref[:, pl.ds(column, 128)], inputs_ref[...])
            out_ref[group * 128 : group * 128 + 128, :] = part.astype(BF)


def patch_halves(side, grads, inputs):
    patches, width = inputs.shape
    return pl.pallas_call(
        patch_halves_kernel,
        in_specs=[SCALAR, HERE, HERE],
        out_specs=[HERE, HERE],
        out_shape=[jax.ShapeDtypeStruct((1024, width), BF)] * 2,
        compiler_params=pltpu.CompilerParams(vmem_limit_bytes=32 * 1024 * 1024),
        cost_estimate=HINT,
    )(side.reshape(1), grads, inputs)


def column_sums(rows):
    return jnp.sum(rows.astype(F32), axis=0)


def eight_order():
    cols = np.arange(1024).reshape(4, 2, 2, 4, 2, 8)
    return cols.transpose(2, 4, 1, 0, 3, 5).reshape(-1)


def shuffle_matrix(order):
    cols = order.shape[0]
    return (lax.broadcasted_iota(jnp.int32, (cols, cols), 0) == order[None, :]).astype(BF)


def qkv_order():
    order = np.zeros((4, 32, 3, 8), np.int32)
    pairs = [[], [], []]
    for z in range(4):
        groups = [third * 128 + z * 32 + k for third in range(3) for k in range(32)]
        for slot in range(3):
            chosen = [g for g in groups if g % 3 == slot]
            for place, group in enumerate(chosen):
                c, x, y = place // 16, place // 4 % 4, place % 4
                source = (((y * 2 + x % 2) * 2 + c) * 4 + z) * 2 + x // 2
                pairs[slot].append((source, group // 3))
                local = (group // 128) * 256 + (group % 32) * 8
                order[z, place, slot] = local + np.arange(8)
    return order.reshape(4, 768), pairs


def on_device(
    tokens,
    memory,
    lengths,
    patch_counts,
    self_qkv,
    self_out,
    cross_query,
    cross_kv,
    cross_out,
    ffn_in,
    ffn_out,
    norm_gains,
    norm_shifts,
    proj_biases,
    ffn_bias,
    cotangent,
):
    y, xl, c, z, xh = (lax.axis_index(axis) for axis in AXES)
    x = xh * 2 + xl
    width = tokens.shape[2]
    rows = 2 * tokens.shape[1]
    page_rows = RING * rows
    length = lax.dynamic_index_in_dim(lengths, xh, 0, keepdims=False)
    count = lax.dynamic_slice(patch_counts, (xh,), (1,))
    valid = (z * rows + jnp.arange(rows) < length)[:, None]

    def swap_cores(part):
        return lax.ppermute(part, "c", FLIP)

    by_core = jnp.asarray(eight_order()).reshape(2, 512)
    eights = shuffle_matrix(by_core.reshape(-1))
    sides = shuffle_matrix(
        jnp.concatenate([lax.dynamic_index_in_dim(by_core, side, 0, keepdims=False) for side in (c, 1 - c)])
    )

    def own_eights(grads):
        return product(grads, sides).astype(BF)

    def relay(chunks, axis, pairs):
        return lax.ppermute(chunks[3], axis, pairs(1)), lax.ppermute(chunks[4], axis, pairs(3))

    def add_on(chunks, got):
        plus, minus, half = chunks[1], chunks[2], chunks[3].shape[0]
        got_a, got_b = (part.astype(F32) for part in got)
        plus = jnp.concatenate([(plus[:half].astype(F32) + got_a).astype(BF), plus[half:]], axis=0)
        minus = jnp.concatenate([minus[:half], (minus[half:].astype(F32) + got_b).astype(BF)], axis=0)
        return plus, minus

    def send_on(sums, axis, pairs):
        return lax.ppermute(sums[0], axis, pairs(1)), lax.ppermute(sums[1], axis, pairs(3))

    def finish(chunks, got):
        return (chunks[0] + got[0].astype(F32) + got[1].astype(F32)).astype(BF)

    X_RING, Y_RING = (("xl", "xh"), x_pairs), ("y", ring_pairs)

    def then_y(part):
        part = part.reshape(4, 32, part.shape[1])
        return ring_sum(
            lambda target: lax.dynamic_index_in_dim(part, target, 0, keepdims=False), y, "y", ring_pairs
        ).astype(BF)

    def then_x(part):
        each = part.shape[0] // 16
        part = part.reshape(2, 4, 2, each, part.shape[1])

        def cut(target):
            piece = lax.dynamic_slice(
                part, (target % 2, 0, target // 2, 0, 0), (1, 4, 1, each, part.shape[4])
            )
            return piece.reshape(4 * each, part.shape[4])

        return ring_sum(cut, x, ("xl", "xh"), x_pairs).astype(BF)

    def sum_z(parts):
        lines = [part.reshape(4, -1, 1024) for part in parts]
        line = jnp.concatenate(lines, axis=1)
        total = ring_sum(
            lambda target: lax.dynamic_index_in_dim(line, target, 0, keepdims=False), z, "z", ring_pairs
        )
        done, at = [], 0
        for part, own in zip(parts, lines):
            done.append(total[at : at + own.shape[1]].reshape(-1, part.shape[-1]))
            at += own.shape[1]
        return done

    mine = lax.dynamic_index_in_dim(tokens, xh, 0, keepdims=False)
    other = lax.dynamic_index_in_dim(tokens, 1 - xh, 0, keepdims=False)
    other = lax.ppermute(other, "xh", FLIP)
    early_rows = [mine] + [lax.ppermute(mine, "z", ring_pairs(step)) for step in STEPS]
    late_row = after(other, *early_rows)
    late_rows = [late_row] + [lax.ppermute(late_row, "z", ring_pairs(step)) for step in STEPS]
    own_memory = swap_in(after(memory, *early_rows), xh)
    own_tokens = jnp.concatenate(
        [jnp.where(xh == 0, mine, late_row), jnp.where(xh == 0, late_row, mine)], axis=0
    )

    def head_cols(matrix, third):
        return lax.dynamic_slice(matrix, (0, third * width + z * 256), (matrix.shape[0], 256))

    heads_qkv = jnp.concatenate([head_cols(self_qkv, third) for third in range(3)], axis=1)
    bias_q = lax.dynamic_slice(proj_biases, (0, z * 256), (1, 256))
    bias_v = lax.dynamic_slice(proj_biases, (1, z * 256), (1, 256))
    bias_qkv = jnp.concatenate([bias_q, jnp.zeros_like(bias_q), bias_v], axis=1)
    joined, low_one, normal_one = project_heads(
        z, xh, early_rows, late_rows, heads_qkv, bias_qkv, norm_gains[0:1], norm_shifts[0:1]
    )
    heads_mix, self_level = attend(page_rows, page_rows, 2, True, joined, joined, joined, (0, 256, 512))

    memory_here = after(own_memory, *late_rows)
    before_got, behind_got = (lax.ppermute(memory_here, "z", ring_pairs(step)) for step in (1, 3))
    heads_mix, before_got, behind_got = lax.optimization_barrier((heads_mix, before_got, behind_got))
    far_got = (
        lax.ppermute(behind_got[: rows // 2], "z", ring_pairs(3)),
        lax.ppermute(before_got[rows // 2 :], "z", ring_pairs(1)),
    )
    mix_pick = lambda target: lax.dynamic_slice(heads_mix, (target * rows, 0), (rows, 256))
    mix_got = exchange(mix_pick, z, far_got)
    far_got = lax.optimization_barrier((*far_got, *(part for _, part in mix_got[1:])))[:2]
    page_memory = jnp.zeros((page_rows, width), BF)
    for hop, first, part in (
        (0, 0, memory_here),
        (1, 0, behind_got),
        (3, 0, before_got),
        (2, 0, far_got[0]),
        (2, rows // 2, far_got[1]),
    ):
        page_memory = lax.dynamic_update_slice(page_memory, part, (around(hop, z) * rows + first, 0))
    patch_bias = jnp.concatenate([jnp.zeros_like(proj_biases[4]), proj_biases[4]])
    page_kv = (product(page_memory, cross_kv) + patch_bias).astype(BF)

    grad_low = jnp.where(valid, swap_in(after(cotangent, heads_mix), xh), 0)
    mixture = jnp.zeros((rows, width), BF)
    for source, part in mix_got:
        mixture = lax.dynamic_update_slice(mixture, part, (0, source * 256))
    after_self = own_tokens.astype(F32) + product(mixture, self_out) + proj_biases[2]
    normal_two, inverse_two = unit(after_self)
    low_two = (normal_two * norm_gains[1] + norm_shifts[1]).astype(BF)
    cross_queries = (product(low_two, cross_query) + proj_biases[3]).astype(BF)
    cross_mix, cross_level = attend(
        rows, page_rows, 8, False, cross_queries, page_kv, page_kv, (0, 0, 1024), count
    )
    after_cross = after_self + product(cross_mix, cross_out) + proj_biases[5]
    normal_three, inverse_three = unit(after_cross)
    low_three = (normal_three * norm_gains[2] + norm_shifts[2]).astype(BF)
    before = product(low_three, ffn_in) + ffn_bias
    below = 0.5 * (1.0 + lax.erf(before * np.float32(np.sqrt(0.5))))
    hidden = (before * below).astype(BF)
    slope = below + before * jnp.exp(-0.5 * before * before) * np.float32(1 / np.sqrt(2 * np.pi))
    result = after_cross + product(hidden, ffn_out) + proj_biases[6]
    layer_rows = jnp.where(valid, result, 0.0).astype(BF)

    order, owner_pairs = qkv_order()
    head_order = lax.dynamic_index_in_dim(jnp.asarray(order), z, 0, keepdims=False)
    head_shuffle, sides = lax.optimization_barrier((shuffle_matrix(head_order), sides))

    out_grads = own_eights(grad_low)
    early = jnp.concatenate([cross_mix, low_two, mixture, low_three, out_grads[:, 512:]], axis=1)
    early_got = swap_cores(early)
    hidden_got = swap_cores(hidden)
    grad_before = (back_product(grad_low, ffn_out) * slope).astype(BF)
    before_sums = column_sums(grad_before)
    in_keep, in_send = split_wides(c, grad_before)
    in_got = swap_cores(in_send)
    grad_three = back_product(grad_before, ffn_in)
    grad_after_cross = grad_low.astype(F32) + unit_back(
        normal_three, inverse_three, grad_three, norm_gains[2]
    )
    cross_low = grad_after_cross.astype(BF)
    cross_grads = own_eights(cross_low)
    cross_got = swap_cores(cross_grads[:, 512:])
    grad_cross_mix = back_product(cross_low, cross_out).astype(BF)
    ffn_in_chunks = outer_chunks(
        y, 512, 512, [((in_keep, 0), (in_got, 0), (early, 3 * width), (early_got, 3 * width), 2)]
    )
    ffn_out_chunks = outer_chunks(
        x,
        128,
        width,
        [
            ((out_grads, 0), (early_got, 4 * width), (hidden, 0), (hidden_got, 0), 4),
            ((cross_grads, 0), (cross_got, 0), (early, 0), (early_got, 0), 1),
        ],
    )
    ffn_out_got = relay(ffn_out_chunks, *X_RING)
    ffn_in_got = relay(ffn_in_chunks, *Y_RING)

    grad_cross_mix, layer_rows, *got = lax.optimization_barrier(
        (grad_cross_mix, layer_rows, *ffn_out_got, *ffn_in_got)
    )
    ffn_out_sums, ffn_in_sums = add_on(ffn_out_chunks, got[:2]), add_on(ffn_in_chunks, got[2:])
    grad_cross_mix, *sums = lax.optimization_barrier((grad_cross_mix, *ffn_out_sums, *ffn_in_sums))
    ffn_out_got, ffn_in_got = send_on(sums[:2], *X_RING), send_on(sums[2:], *Y_RING)
    cross_query_low, patch_grads = attend_back(
        rows,
        page_rows,
        8,
        False,
        cross_queries,
        page_kv,
        page_kv,
        (0, 0, 1024),
        cross_mix,
        grad_cross_mix,
        cross_level,
        count,
    )
    cross_query_low, patch_grads, layer_rows, *got = lax.optimization_barrier(
        (cross_query_low, patch_grads, layer_rows, *ffn_out_got, *ffn_in_got)
    )
    layer_out = swap_out(layer_rows, xh)
    ffn_out_part, ffn_in_part = finish(ffn_out_chunks, got[:2]), finish(ffn_in_chunks, got[2:])
    grad_two = back_product(cross_query_low, cross_query)
    grad_after_self = grad_after_cross + unit_back(normal_two, inverse_two, grad_two, norm_gains[1])

    self_low = grad_after_self.astype(BF)
    grad_mix_rows = back_product(self_low, self_out).astype(BF)
    grads_here = after(patch_grads, grad_mix_rows)
    kv_send, kv_keep = patch_halves(c, grads_here, page_memory)
    grad_mixture = rows_to_heads(grad_mix_rows, z, (kv_send,))
    grads_here = after(patch_grads, grad_mixture)
    grad_memory_low = back_product(grads_here, cross_kv).astype(BF)
    kv_rows = (kv_keep.astype(F32) + swap_cores(kv_send).astype(F32)).astype(BF)
    kv_quarters = kv_rows.reshape(RING, 256, width)

    def kv_chunk(hop):
        return lax.dynamic_index_in_dim(kv_quarters, around(hop, y), 0, keepdims=False)

    kv_own, kv_sends = kv_chunk(0), [kv_chunk(step) for step in STEPS]
    out_quarters = ffn_out_part.reshape(RING, 32, 5 * width)
    out_own, *out_sends = (
        lax.dynamic_index_in_dim(out_quarters, around(hop, y), 0, keepdims=False) for hop in (0,) + STEPS
    )
    query_grads, self_grads = own_eights(cross_query_low), own_eights(self_low)
    sent = swap_cores(jnp.concatenate([query_grads[:, 512:], self_grads[:, 512:]], axis=1))
    sent, *out_sends = lax.optimization_barrier((sent, *out_sends))
    out_got = [lax.ppermute(chunk, "y", ring_pairs(step)) for step, chunk in zip(STEPS, out_sends)]
    two_chunks = outer_chunks(
        x,
        128,
        width,
        [
            ((query_grads, 0), (sent, 0), (early, width), (early_got, width), 1),
            ((self_grads, 0), (sent, 512), (early, 2 * width), (early_got, 2 * width), 1),
        ],
        extra=ffn_in_part,
    )
    two_chunks = lax.optimization_barrier((*two_chunks, *out_got))
    two_chunks, out_got = two_chunks[:5], two_chunks[5:]
    ffn_out_part = sum((got.astype(F32) for got in out_got), out_own.astype(F32)).astype(BF)
    grad_mixture, layer_out, *held = lax.optimization_barrier(
        (grad_mixture, layer_out, *kv_sends, *two_chunks)
    )
    kv_sends, two_chunks = held[:3], held[3:]

    two_got = relay(two_chunks, *X_RING)
    kv_got = [lax.ppermute(chunk, "y", ring_pairs(step)) for step, chunk in zip(STEPS, kv_sends)]
    (grad_joined,) = attend_back(
        page_rows, page_rows, 2, True, joined, joined, joined, (0, 256, 512), heads_mix, grad_mixture, self_level
    )
    grad_joined, *two_got = lax.optimization_barrier((grad_joined, *two_got))
    grad_one = back_product(grad_joined, heads_qkv)
    shuffled = product(grad_joined, head_shuffle).astype(BF)
    grad_one, shuffled, *kv_got = lax.optimization_barrier((grad_one, shuffled, *kv_got))

    def core_half(target):
        return outer(lax.dynamic_slice(shuffled, (0, target * 384), (page_rows, 384)), low_one)

    core_keep = core_half(c)
    core_send = core_half(1 - c).astype(BF)
    grad_one, grad_one_low, grad_memory_low, core_keep, core_send, *held = lax.optimization_barrier(
        (grad_one, grad_one.astype(BF), grad_memory_low, core_keep, core_send, *two_got, *kv_got)
    )
    two_got, kv_got = held[:2], held[2:]

    core_got = swap_cores(core_send).astype(F32)
    two_got = send_on(add_on(two_chunks, two_got), *X_RING)

    def page_chunk(hop, first=0, height=rows):
        at = (around(hop, z) * rows + first, 0)
        return jnp.concatenate(
            [lax.dynamic_slice(part, at, (height, width)) for part in (grad_one_low, grad_memory_low)], axis=1
        )

    half = rows // 2
    page_chunks = (
        page_chunk(0),
        page_chunk(1),
        page_chunk(3),
        page_chunk(2, 0, half),
        page_chunk(2, half, half),
    )
    Z_RING = ("z", ring_pairs)
    page_got = relay(page_chunks, *Z_RING)
    before_sums = after(before_sums, core_send)

    def at_heads(sums):
        return lax.dynamic_update_slice(jnp.zeros((width,), F32), sums, (z * 256,))

    vectors = [
        column_sums(grad_one * normal_one.astype(F32)),
        column_sums(grad_two * normal_two),
        column_sums(grad_three * normal_three),
        column_sums(grad_one),
        column_sums(grad_two),
        column_sums(grad_three),
        at_heads(column_sums(grad_joined[:, :256])),
        at_heads(column_sums(grad_joined[:, 512:])),
        column_sums(grad_after_self),
        column_sums(cross_query_low),
        column_sums(patch_grads[:, width:]),
        column_sums(grad_after_cross),
        column_sums(grad_low),
    ]
    small = jnp.concatenate([jnp.stack(vectors), before_sums.reshape(width, 4).T], axis=0)
    small = lax.dot_general(
        small, eights.astype(F32), (((1,), (0,)), ((), ())), precision=lax.Precision.HIGHEST
    )
    small = small.reshape(17, 2, 16, 4, 8).transpose(1, 2, 3, 0, 4).reshape(2, 16, 4, 17 * 8)
    small = jnp.pad(small, ((0, 0), (0, 0), (0, 0), (0, 256 - 17 * 8))).reshape(2, 16, width).astype(BF)
    small_keep = lax.dynamic_index_in_dim(small, c, 0, keepdims=False)
    small_send = lax.dynamic_index_in_dim(small, 1 - c, 0, keepdims=False)
    small_sum = (small_keep.astype(F32) + swap_cores(small_send).astype(F32)).astype(BF)
    core_sum = (core_keep + core_got).astype(BF)
    kv_part = sum((got.astype(F32) for got in kv_got), kv_own.astype(F32)).astype(BF)
    core_sum, small_sum, kv_part, *held = lax.optimization_barrier(
        (core_sum, small_sum, kv_part, *two_got, *page_got)
    )
    two_got, page_got = held[:2], held[2:]

    page_got = send_on(add_on(page_chunks, page_got), *Z_RING)
    small_sum = jnp.pad(small_sum.reshape(4, 4, 1, width), ((0, 0), (0, 0), (0, 7), (0, 0)))
    core_sum = jnp.concatenate([core_sum.reshape(4, 4, 24, width), small_sum], axis=2)
    kv_lines = kv_part.reshape(2, 4, 2, 16, width)

    def x_chunk(target):
        piece = lax.dynamic_slice(kv_lines, (target % 2, 0, target // 2, 0, 0), (1, 4, 1, 16, width))
        lines = lax.dynamic_index_in_dim(core_sum, target, 0, keepdims=False)
        return jnp.concatenate([lines.reshape(128, width), piece.reshape(64, width)], axis=0)

    x_sum = ring_sum(x_chunk, x, ("xl", "xh"), x_pairs).astype(BF)
    two_part = finish(two_chunks, two_got)
    x_sum, two_part, own_tokens, *page_got = lax.optimization_barrier((x_sum, two_part, own_tokens, *page_got))

    two_part, ffn_in_part = two_part[:, : 2 * width].reshape(4, 32, 2 * width), two_part[:, 2 * width :]
    cross_kv_part = x_sum[128:]
    y_lines = jnp.concatenate([x_sum[:128].reshape(4, 32, width), two_part], axis=2)
    y_sum = ring_sum(
        lambda target: lax.dynamic_index_in_dim(y_lines, target, 0, keepdims=False), y, "y", ring_pairs
    )
    grad_own, memory_rows = (
        sum(part[:, at : at + width].astype(F32) for part in (page_chunks[0], *page_got)) for at in (0, width)
    )
    own_normal, own_inverse = unit(own_tokens.astype(F32))
    token_rows = grad_after_self + unit_back(own_normal, own_inverse, grad_own, norm_gains[0])
    both_grads = swap_out(jnp.concatenate([token_rows, memory_rows], axis=1).astype(BF), xh)
    token_grad, memory_grad = both_grads[..., :width], both_grads[..., width:]

    two_part, y_sum = y_sum[:, width:].astype(BF), y_sum[:, :width]
    small_part = jnp.pad(y_sum[24].astype(BF).reshape(4, 256), ((0, 0), (0, 768)))
    order, owner_pairs = qkv_order()
    grad_qkv = jnp.concatenate(
        [lax.ppermute(y_sum[8 * slot : 8 * slot + 8], AXES, owner_pairs[slot]) for slot in range(3)], axis=0
    )

    ffn_out_rows, ffn_in_rows, two_rows, cross_kv_rows, small = sum_z(
        [ffn_out_part, ffn_in_part, two_part, cross_kv_part, small_part]
    )
    ffn_out_rows, cross_out_rows = ffn_out_rows[:, : 4 * width], ffn_out_rows[:, 4 * width :]
    cross_query_rows, self_out_rows = two_rows[:, :width], two_rows[:, width:]
    small = small[0, : 17 * 8].reshape(17, 8)

    return (
        layer_out,
        token_grad,
        memory_grad,
        grad_qkv.T,
        self_out_rows.T,
        cross_query_rows.T,
        cross_kv_rows.T,
        cross_out_rows.T,
        ffn_in_rows.T,
        ffn_out_rows.T,
        small[:3],
        small[3:6],
        small[6:13],
        small[13:].T.reshape(-1),
    )


def solution(mesh):
    split = jax.sharding.Mesh(mesh.devices.reshape(MESH_SHAPE), AXES)
    page, blk = AXES[:3], AXES[3:]
    blocks, cols = P(page, blk, None), P(None, AXES)
    in_specs = (blocks, blocks, P(page), P(page)) + (P(),) * 11 + (blocks,)
    out_specs = (blocks,) * 3 + (cols,) * 10 + (P(AXES),)
    return jax.shard_map(
        on_device, mesh=split, in_specs=in_specs, out_specs=out_specs, check_vma=False
    )
```

```python
import functools

import jax
import jax.numpy as jnp
import numpy as np
from jax import lax
from jax.experimental import pallas as pl
from jax.experimental.pallas import tpu as pltpu
from jax.sharding import PartitionSpec as P

EPS = 1e-05

BF = jnp.bfloat16
F32 = jnp.float32
NEG = -1e30
TILE = 256
PAIR = 128
HINT = pl.CostEstimate(flops=1 << 20, bytes_accessed=1 << 16, transcendentals=0)


def dot_tt(a, b):
    return lax.dot_general(a, b, (((1,), (1,)), ((), ())), preferred_element_type=F32)


def dot_nn(a, b):
    return lax.dot_general(a, b, (((1,), (0,)), ((), ())), preferred_element_type=F32)


def two_heads(rows):
    lanes = lax.broadcasted_iota(jnp.int32, rows.shape, 1)
    none = jnp.zeros_like(rows)
    return jnp.concatenate([jnp.where(lanes < 64, rows, none), jnp.where(lanes < 64, none, rows)], axis=0)


def later_key():
    keys = lax.broadcasted_iota(jnp.int32, (TILE, 2 * TILE), 0)
    return keys > lax.broadcasted_iota(jnp.int32, (TILE, 2 * TILE), 1) % TILE


def own_halves(both):
    return jnp.concatenate([both[:64, :TILE], both[64:, TILE:]], axis=0).T


def span(tile):
    return pl.ds(tile * TILE, TILE)


def forward_tiles(key_tiles, causal, q_ref, k_ref, o_ref, lse_ref, vt_ref, s_ref):
    for i in range(q_ref.shape[0] // TILE):
        tiles = i + 1 if causal else key_tiles
        queries = two_heads(q_ref[span(i), :] * 0.125)
        kept = s_ref.at[i % 2]
        top = None
        for j in range(tiles):
            scores = dot_tt(k_ref[span(j), :], queries)
            if causal and j == i:
                scores = jnp.where(later_key(), NEG, scores)
            kept[span(j), :] = scores
            tile_top = jnp.max(scores, axis=0, keepdims=True)
            top = tile_top if top is None else jnp.maximum(top, tile_top)
        total, mixed = None, None
        for j in range(tiles):
            shares = jnp.exp(kept[span(j), :] - top)
            tile_sum = jnp.sum(shares, axis=0, keepdims=True)
            tile_mix = dot_nn(vt_ref[:, span(j)], shares.astype(BF))
            total = tile_sum if total is None else total + tile_sum
            mixed = tile_mix if mixed is None else mixed + tile_mix
        level = top + jnp.log(total)
        lse_ref[0, 0:1, span(i)] = level[:, :TILE]
        lse_ref[0, 1:2, span(i)] = level[:, TILE:]
        o_ref[span(i), :] = own_halves(mixed / total).astype(o_ref.dtype)


def pair_columns(pair, first=0):
    return pl.ds(pl.multiple_of(pair * PAIR + first, PAIR), PAIR)


def every_pair(pairs, count_ref, tiles, run):
    def loop(live):
        @pl.loop(0, pairs // 2)
        def _(couple):
            run(2 * couple, 0, live)
            run(2 * couple + 1, 1, live)

    if count_ref is None:
        loop(tiles)
    else:
        pl.when(count_ref[0] > TILE)(lambda: loop(tiles))
        pl.when(count_ref[0] <= TILE)(lambda: loop(1))


def forward_kernel(pairs, causal, firsts, *refs):
    count_ref = None if causal else refs[0]
    refs = refs if causal else refs[1:]
    q_ref, k_ref, v_ref, o_ref, lse_ref, vt_ref, s_ref = refs

    def run(pair, slot, tiles):
        q, k, v = (ref.at[:, pair_columns(pair, at)] for ref, at in zip((q_ref, k_ref, v_ref), firsts))
        vt, kept = vt_ref.at[slot], s_ref.at[slot]
        vt[:, : tiles * TILE] = v[: tiles * TILE, :].T
        out, level = o_ref.at[:, pair_columns(pair)], lse_ref.at[pl.ds(pair, 1)]
        forward_tiles(tiles, causal, q, k, out, level, vt, kept)

    every_pair(pairs, count_ref, k_ref.shape[0] // TILE, run)


def backward_tiles(
    key_tiles, causal, q_ref, k_ref, v_ref, o_ref, do_ref, lse_ref, dq_ref, kt_ref, dk_ref, dv_ref
):
    ones = jnp.ones((8, PAIR), F32)
    for i in range(q_ref.shape[0] // TILE):
        tiles = i + 1 if causal else key_tiles
        queries = two_heads(q_ref[span(i), :] * 0.125)
        pulled = two_heads(do_ref[span(i), :])
        out = o_ref[span(i), :].astype(F32)
        weighed = pulled.astype(F32) * jnp.concatenate([out, out], axis=0)
        dots = lax.dot_general(
            ones,
            weighed,
            (((1,), (1,)), ((), ())),
            preferred_element_type=F32,
            precision=lax.Precision.HIGHEST,
        )[0:1, :]
        level = jnp.concatenate([lse_ref[0, 0:1, span(i)], lse_ref[0, 1:2, span(i)]], axis=1)
        drawn = None
        for j in range(tiles):
            shares = jnp.exp(dot_tt(k_ref[span(j), :], queries) - level)
            if causal and j == i:
                shares = jnp.where(later_key(), 0.0, shares)
            grad_shares = dot_tt(v_ref[span(j), :], pulled)
            grad_scores = (shares * (grad_shares - dots)).astype(BF)
            dv_part = dot_nn(shares.astype(BF), pulled)
            dk_part = dot_nn(grad_scores, queries)
            if i == (j if causal else 0):
                dv_ref[span(j), :] = dv_part
                dk_ref[span(j), :] = dk_part
            else:
                dv_ref[span(j), :] += dv_part
                dk_ref[span(j), :] += dk_part
            tile_drawn = dot_nn(kt_ref[:, span(j)], grad_scores)
            drawn = tile_drawn if drawn is None else drawn + tile_drawn
        dq_ref[span(i), :] = (own_halves(drawn) * 0.125).astype(dq_ref.dtype)


def backward_kernel(pairs, causal, firsts, *refs):
    count_ref = None if causal else refs[0]
    refs = refs if causal else refs[1:]
    q_ref, k_ref, v_ref, o_ref, do_ref, lse_ref, *outs, kt_ref, dk_ref, dv_ref = refs
    dq_ref, dkv_ref = outs[0], outs[-1]
    width = pairs * PAIR
    first = dkv_ref.shape[1] - 2 * width

    def run(pair, slot, tiles):
        q, k, v = (ref.at[:, pair_columns(pair, at)] for ref, at in zip((q_ref, k_ref, v_ref), firsts))
        cols, live = pair_columns(pair), tiles * TILE
        kt, dk, dv = kt_ref.at[slot], dk_ref.at[slot], dv_ref.at[slot]
        kt[:, :live] = k[:live, :].T
        if live < k.shape[0]:
            dk[...] = jnp.zeros_like(dk)
            dv[...] = jnp.zeros_like(dv)
        out, grads, level = o_ref.at[:, cols], do_ref.at[:, cols], lse_ref.at[pl.ds(pair, 1)]
        backward_tiles(
            tiles, causal, q, k, v, out, grads, level, dq_ref.at[:, cols], kt, dk, dv
        )
        dkv_ref[:, pair_columns(pair, first)] = dk[...].astype(BF)
        dkv_ref[:, pair_columns(pair, first + width)] = dv[...].astype(BF)

    every_pair(pairs, count_ref, k_ref.shape[0] // TILE, run)


SCALAR = pl.BlockSpec(memory_space=pltpu.SMEM)
HERE = pl.BlockSpec(memory_space=pltpu.VMEM)


def attend(q_rows, key_rows, pairs, causal, q, k, v, firsts, count=None):
    return pl.pallas_call(
        functools.partial(forward_kernel, pairs, causal, firsts),
        in_specs=([] if causal else [SCALAR]) + [HERE] * 3,
        out_specs=[HERE] * 2,
        out_shape=[
            jax.ShapeDtypeStruct((q_rows, pairs * PAIR), BF),
            jax.ShapeDtypeStruct((pairs, 2, q_rows), F32),
        ],
        scratch_shapes=[pltpu.VMEM((2, PAIR, key_rows), BF), pltpu.VMEM((2, 2, key_rows, 2 * TILE), F32)],
        compiler_params=pltpu.CompilerParams(vmem_limit_bytes=32 * 1024 * 1024),
        cost_estimate=HINT,
    )(*(() if causal else (count,)), q, k, v)


def attend_back(q_rows, key_rows, pairs, causal, q, k, v, firsts, o, do, lse, count=None):
    width = pairs * PAIR
    shapes = [jax.ShapeDtypeStruct((q_rows, width), BF), jax.ShapeDtypeStruct((key_rows, 2 * width), BF)]
    if causal:
        shapes = [jax.ShapeDtypeStruct((q_rows, 3 * width), BF)]
    return pl.pallas_call(
        functools.partial(backward_kernel, pairs, causal, firsts),
        in_specs=([] if causal else [SCALAR]) + [HERE] * 6,
        out_specs=[HERE] * len(shapes),
        out_shape=shapes,
        scratch_shapes=[
            pltpu.VMEM((2, PAIR, key_rows), BF),
            pltpu.VMEM((2, key_rows, PAIR), F32),
            pltpu.VMEM((2, key_rows, PAIR), F32),
        ],
        compiler_params=pltpu.CompilerParams(vmem_limit_bytes=32 * 1024 * 1024),
        cost_estimate=HINT,
    )(*(() if causal else (count,)), q, k, v, o, do, lse)

AXES = ("y", "xl", "c", "z", "xh")
MESH_SHAPE = (4, 2, 2, 4, 2)
RING = 4


def ring_pairs(step):
    return [(i, (i + step) % RING) for i in range(RING)]


def x_slot(x):
    return (x % 2) * 2 + x // 2


def x_pairs(step):
    return [(x_slot(x), x_slot((x + step) % RING)) for x in range(RING)]


FLIP = [(0, 1), (1, 0)]
STEPS = (1, 3, 2)


def around(step, coord):
    return lax.rem(coord + step, RING)


def swap_in(blocks, side):
    own = lax.dynamic_index_in_dim(blocks, side, 0, keepdims=False)
    got = lax.ppermute(lax.dynamic_index_in_dim(blocks, 1 - side, 0, keepdims=False), "xh", FLIP)
    return jnp.concatenate([jnp.where(side == 0, own, got), jnp.where(side == 0, got, own)], axis=0)


def swap_out(rows, side):
    blocks = rows.reshape(2, rows.shape[0] // 2, rows.shape[1])
    own = lax.dynamic_index_in_dim(blocks, side, 0, keepdims=False)
    got = lax.ppermute(lax.dynamic_index_in_dim(blocks, 1 - side, 0, keepdims=False), "xh", FLIP)
    return jnp.stack([jnp.where(side == 0, own, got), jnp.where(side == 0, got, own)])


def exchange(pick, z, behind=()):
    got = [lax.ppermute(pick(around(step, z)), "z", ring_pairs(step)) for step in STEPS]
    got = lax.optimization_barrier((*got, *behind))[: len(STEPS)]
    return [(z, pick(z))] + [(around(RING - step, z), part) for step, part in zip(STEPS, got)]


def rows_to_heads(rows, z, behind=()):
    height, width = rows.shape[0], rows.shape[1] // RING
    full = jnp.zeros((RING * height, width), rows.dtype)
    pick = lambda target: lax.dynamic_slice(rows, (0, target * width), (height, width))
    for source, part in exchange(pick, z, behind):
        full = lax.dynamic_update_slice(full, part, (source * height, 0))
    return full


def ring_sum(pick, coord, axis, pairs):
    total = pick(coord).astype(F32)
    for step in STEPS:
        got = lax.ppermute(pick(around(step, coord)).astype(BF), axis, pairs(step))
        total = total + got.astype(F32)
    return total


def after(value, *others):
    return lax.optimization_barrier((value, *others))[0]


def product(left, right):
    return jnp.dot(left, right, preferred_element_type=F32)


def back_product(grads, matrix):
    return lax.dot_general(grads, matrix, (((1,), (1,)), ((), ())), preferred_element_type=F32)


def outer(grads, inputs):
    return lax.dot_general(grads, inputs, (((0,), (0,)), ((), ())), preferred_element_type=F32)


def unit(rows):
    centred = rows - jnp.mean(rows, axis=-1, keepdims=True)
    inverse = lax.rsqrt(jnp.mean(centred * centred, axis=-1, keepdims=True) + EPS)
    return centred * inverse, inverse


def unit_back(normal, inverse, grads, gain):
    scaled = grads * gain
    mean = jnp.mean(scaled, axis=-1, keepdims=True)
    along = jnp.mean(scaled * normal, axis=-1, keepdims=True)
    return inverse * (scaled - mean - normal * along)


def chunks_kernel(width, block, segments, coord_ref, *refs):
    outs, turned_ref = refs[-6:-1], refs[-1]
    own_ref, plus_ref, minus_ref, far_a_ref, far_b_ref = outs
    tokens = refs[0].shape[0]
    half, each = width // 2, width // 4
    lane = 0

    def put(pick, lanes):
        own_ref[:, lanes] = pick(0, 0, width).astype(F32)
        plus_ref[:, lanes] = pick(1, 0, width).astype(BF)
        minus_ref[:, lanes] = pick(3, 0, width).astype(BF)
        far_a_ref[:, lanes] = pick(2, 0, half).astype(BF)
        far_b_ref[:, lanes] = pick(2, half, half).astype(BF)

    for at, (grads_at, got_grads_at, inputs_at, got_inputs_at, blocks) in enumerate(segments):
        grads_ref, got_grads_ref, inputs_ref, got_inputs_ref = refs[4 * at : 4 * at + 4]
        for hop in range(RING):
            column = around(hop, coord_ref[0]) * width
            rows = slice(hop * width, hop * width + width)
            turned_ref[at, rows, :tokens] = grads_ref[:, pl.ds(pl.multiple_of(grads_at + column, 128), width)].T
            turned_ref[at, rows, tokens:] = got_grads_ref[
                :, pl.ds(pl.multiple_of(got_grads_at + column, 128), width)
            ].T
        for number in range(blocks):
            mine = inputs_ref[:, inputs_at + number * block : inputs_at + number * block + block]
            got = got_inputs_ref[:, got_inputs_at + number * block : got_inputs_at + number * block + block]

            def pick(hop, first, rows, at=at, mine=mine, got=got):
                turned = turned_ref.at[at, hop * width + first : hop * width + first + rows, :]
                return dot_nn(turned[:, :tokens], mine) + dot_nn(turned[:, tokens:], got)

            put(pick, slice(lane, lane + block))
            lane += block

    if lane < own_ref.shape[1]:
        extra_ref = refs[4 * len(segments)]

        def pick(hop, first, rows):
            target = around(hop, coord_ref[0])
            zs = range(first // each, (first + rows) // each)
            return jnp.concatenate([extra_ref[target % 2, zz, target // 2] for zz in zs], axis=0)

        put(pick, slice(lane, own_ref.shape[1]))


def outer_chunks(coord, width, block, segments, extra=None):
    cols = RING * width
    tokens = segments[0][0][0].shape[0]
    operands = [array for segment in segments for array, _ in segment[:4]]
    places = tuple(tuple(first for _, first in segment[:4]) + (segment[4],) for segment in segments)
    lanes = sum(segment[4] for segment in segments) * block
    if extra is not None:
        operands.append(extra.reshape(2, 4, 2, width // 4, extra.shape[1]))
        lanes += extra.shape[1]
    shape = lambda rows, dtype: jax.ShapeDtypeStruct((rows, lanes), dtype)
    return pl.pallas_call(
        functools.partial(chunks_kernel, width, block, places),
        in_specs=[SCALAR] + [HERE] * len(operands),
        out_specs=[HERE] * 5,
        out_shape=[shape(width, F32), shape(width, BF), shape(width, BF)] + [shape(width // 2, BF)] * 2,
        scratch_shapes=[pltpu.VMEM((len(segments), cols, 2 * tokens), BF)],
        compiler_params=pltpu.CompilerParams(vmem_limit_bytes=40 * 1024 * 1024),
        cost_estimate=HINT,
    )(coord.reshape(1), *operands)


def project_kernel(place_ref, *refs):
    early, late = refs[:RING], refs[RING : 2 * RING]
    matrix_ref, bias_ref, gain_ref, shift_ref, joined_ref, low_ref, normal_ref = refs[2 * RING :]

    def run(at):
        first = jnp.where(place_ref[1] == 0, early[at][...], late[at][...])
        second = jnp.where(place_ref[1] == 0, late[at][...], early[at][...])
        normal, _ = unit(jnp.concatenate([first, second], axis=0).astype(F32))
        low = (normal * gain_ref[...] + shift_ref[...]).astype(BF)
        low_ref[...] = low
        normal_ref[...] = normal.astype(BF)
        joined_ref[...] = (dot_nn(low, matrix_ref[...]) + bias_ref[...]).astype(BF)

    for at in range(RING):
        pl.when(pl.program_id(0) == at)(functools.partial(run, at))


def project_heads(z, side, early, late, matrix, bias, gain, shift):
    half, width = early[0].shape
    rows = 2 * half

    def row_block(j, place):
        hop = jnp.where(j == 0, 0, jnp.where(j == 1, STEPS[0], jnp.where(j == 2, STEPS[1], STEPS[2])))
        return (lax.rem(place[0] + RING - hop, RING), 0)

    whole = lambda shape: pl.BlockSpec(shape, lambda j, place: (0, 0))
    return pl.pallas_call(
        project_kernel,
        grid_spec=pltpu.PrefetchScalarGridSpec(
            num_scalar_prefetch=1,
            grid=(RING,),
            in_specs=[whole((half, width))] * 8
            + [whole((width, 768)), whole((1, 768)), whole((1, width)), whole((1, width))],
            out_specs=[
                pl.BlockSpec((rows, 768), row_block),
                pl.BlockSpec((rows, width), row_block),
                pl.BlockSpec((rows, width), row_block),
            ],
        ),
        out_shape=[
            jax.ShapeDtypeStruct((RING * rows, 768), BF),
            jax.ShapeDtypeStruct((RING * rows, width), BF),
            jax.ShapeDtypeStruct((RING * rows, width), BF),
        ],
        compiler_params=pltpu.CompilerParams(vmem_limit_bytes=40 * 1024 * 1024),
        cost_estimate=HINT,
    )(jnp.stack([z, side]), *early, *late, matrix, bias, gain, shift)


def split_kernel(core_ref, grads_ref, keep_ref, send_ref):
    for at in range(grads_ref.shape[1] // 512):
        first = grads_ref[:, 512 * at : 512 * at + 256]
        second = grads_ref[:, 512 * at + 256 : 512 * at + 512]
        keep_ref[:, 256 * at : 256 * at + 256] = jnp.where(core_ref[0] == 0, first, second)
        send_ref[:, 256 * at : 256 * at + 256] = jnp.where(core_ref[0] == 0, second, first)


def split_wides(core, grads):
    rows, cols = grads.shape
    put = pl.BlockSpec((rows // 2, cols // 2), lambda j: (j, 0))
    return pl.pallas_call(
        split_kernel,
        grid=(2,),
        in_specs=[SCALAR, pl.BlockSpec((rows // 2, cols), lambda j: (j, 0))],
        out_specs=[put, put],
        out_shape=[jax.ShapeDtypeStruct((rows, cols // 2), BF)] * 2,
        compiler_params=pltpu.CompilerParams(vmem_limit_bytes=32 * 1024 * 1024),
        cost_estimate=HINT,
    )(core.reshape(1), grads)


def patch_halves_kernel(side_ref, grads_ref, inputs_ref, send_ref, keep_ref):
    for out_ref, side in ((send_ref, 1 - side_ref[0]), (keep_ref, side_ref[0])):
        for group in range(8):
            column = pl.multiple_of((group * 2 + side) * 128, 128)
            part = outer(grads_ref[:, pl.ds(column, 128)], inputs_ref[...])
            out_ref[group * 128 : group * 128 + 128, :] = part.astype(BF)


def patch_halves(side, grads, inputs):
    patches, width = inputs.shape
    return pl.pallas_call(
        patch_halves_kernel,
        in_specs=[SCALAR, HERE, HERE],
        out_specs=[HERE, HERE],
        out_shape=[jax.ShapeDtypeStruct((1024, width), BF)] * 2,
        compiler_params=pltpu.CompilerParams(vmem_limit_bytes=32 * 1024 * 1024),
        cost_estimate=HINT,
    )(side.reshape(1), grads, inputs)


def page_kernel(place_ref, joined_ref, heads_ref, patch_ref, cross_ref, normal_ref, *refs):
    own_ref, plus_ref, minus_ref, far_a_ref, far_b_ref, sums_ref, head_sums_ref = refs
    rows, width = own_ref.shape[0], cross_ref.shape[0]
    half = rows // 2
    sums, head_sums = [0.0, 0.0, 0.0], 0.0
    for hop in range(RING):
        here = pl.ds(pl.multiple_of(around(hop, place_ref[0]) * rows, rows), rows)
        one = dot_tt(joined_ref[here, :], heads_ref[...])
        sums[0] += jnp.sum(one * normal_ref[here, :].astype(F32), axis=0, keepdims=True)
        sums[1] += jnp.sum(one, axis=0, keepdims=True)
        sums[2] += jnp.sum(patch_ref[here, width:].astype(F32), axis=0, keepdims=True)
        head_sums += jnp.sum(joined_ref[here, :].astype(F32), axis=0, keepdims=True)
        two = dot_tt(patch_ref[here, :], cross_ref[...])
        for part, lanes in ((one, slice(0, width)), (two, slice(width, 2 * width))):
            if hop == 2:
                far_a_ref[:, lanes] = part[:half].astype(BF)
                far_b_ref[:, lanes] = part[half:].astype(BF)
            else:
                out_ref = {0: own_ref, 1: plus_ref, 3: minus_ref}[hop]
                out_ref[:, lanes] = part.astype(out_ref.dtype)
    sums_ref[...] = jnp.concatenate(sums, axis=0)
    head_sums_ref[...] = head_sums


def page_back(z, joined, heads, patch_grads, cross_kv, normal):
    page_rows, width = normal.shape
    rows = page_rows // RING
    chunk = lambda height, dtype: jax.ShapeDtypeStruct((height, 2 * width), dtype)
    return pl.pallas_call(
        page_kernel,
        in_specs=[SCALAR] + [HERE] * 5,
        out_specs=[HERE] * 7,
        out_shape=[
            chunk(rows, F32),
            chunk(rows, BF),
            chunk(rows, BF),
            chunk(rows // 2, BF),
            chunk(rows // 2, BF),
            jax.ShapeDtypeStruct((3, width), F32),
            jax.ShapeDtypeStruct((1, joined.shape[1]), F32),
        ],
        compiler_params=pltpu.CompilerParams(vmem_limit_bytes=40 * 1024 * 1024),
        cost_estimate=HINT,
    )(z.reshape(1), joined, heads, patch_grads, cross_kv, normal)


def relay_add_kernel(plus_ref, minus_ref, got_a_ref, got_b_ref, plus_out_ref, minus_out_ref):
    half = got_a_ref.shape[0]
    plus_out_ref[:half] = (plus_ref[:half].astype(F32) + got_a_ref[...].astype(F32)).astype(BF)
    plus_out_ref[half:] = plus_ref[half:]
    minus_out_ref[:half] = minus_ref[:half]
    minus_out_ref[half:] = (minus_ref[half:].astype(F32) + got_b_ref[...].astype(F32)).astype(BF)


def relay_add(plus, minus, got_a, got_b):
    return pl.pallas_call(
        relay_add_kernel,
        in_specs=[HERE] * 4,
        out_specs=[HERE] * 2,
        out_shape=[jax.ShapeDtypeStruct(plus.shape, BF)] * 2,
        compiler_params=pltpu.CompilerParams(vmem_limit_bytes=32 * 1024 * 1024),
        cost_estimate=HINT,
    )(plus, minus, got_a, got_b)


def last_kernel(*refs):
    parts, outs = refs[:RING], refs[RING:]
    total = sum(ref[...].astype(F32) for ref in parts)
    ffn_out, cross_out, ffn_in, cross_query, self_out, cross_kv, gains, shifts, biases, ffn_bias = outs
    width = total.shape[1]
    for at in range(4):
        ffn_out[:, at * width : at * width + width] = total[8 * at : 8 * at + 8]
    cross_out[...] = total[32:40]
    ffn_in[...] = total[40:72]
    cross_query[...] = total[72:80]
    self_out[...] = total[80:88]
    cross_kv[...] = total[88:104]
    line = total[104:112, :256]
    spot = lax.broadcasted_iota(jnp.int32, (24, 256), 1)
    picked = jnp.where(spot // 8 == lax.broadcasted_iota(jnp.int32, (24, 256), 0), line[0:1], 0.0)
    spot = lax.broadcasted_iota(jnp.int32, (256, 128), 0)
    lane = lax.broadcasted_iota(jnp.int32, (256, 128), 1)
    exact = functools.partial(jnp.dot, precision=lax.Precision.HIGHEST, preferred_element_type=F32)
    table = exact(picked, (spot % 8 == lane).astype(F32))
    gains[...] = table[0:3, :8]
    shifts[...] = table[3:6, :8]
    biases[...] = table[6:13, :8]
    ffn_bias[...] = exact(line, (spot == 104 + lane % 4 * 8 + lane // 4).astype(F32))[0:1, :32]


def last_sums(*parts):
    width = parts[0].shape[1]
    shapes = [(8, 4 * width), (8, width), (32, width), (8, width), (8, width), (16, width)]
    shapes += [(3, 8), (3, 8), (7, 8), (1, 32)]
    return pl.pallas_call(
        last_kernel,
        in_specs=[HERE] * RING,
        out_specs=[HERE] * len(shapes),
        out_shape=[jax.ShapeDtypeStruct(shape, F32) for shape in shapes],
        compiler_params=pltpu.CompilerParams(vmem_limit_bytes=32 * 1024 * 1024),
        cost_estimate=HINT,
    )(*parts)


def sum_kernel(*refs):
    total = refs[0][...].astype(F32)
    for ref in refs[1:-1]:
        total = total + ref[...].astype(F32)
    refs[-1][...] = total.astype(refs[-1].dtype)


def sum_low(*parts):
    return pl.pallas_call(
        sum_kernel,
        in_specs=[HERE] * len(parts),
        out_specs=HERE,
        out_shape=jax.ShapeDtypeStruct(parts[0].shape, BF),
        compiler_params=pltpu.CompilerParams(vmem_limit_bytes=32 * 1024 * 1024),
        cost_estimate=HINT,
    )(*parts)


def column_sums(rows):
    return jnp.sum(rows.astype(F32), axis=0)


def eight_order():
    cols = np.arange(1024).reshape(4, 2, 2, 4, 2, 8)
    return cols.transpose(2, 4, 1, 0, 3, 5).reshape(-1)


def shuffle_matrix(order):
    cols = order.shape[0]
    return (lax.broadcasted_iota(jnp.int32, (cols, cols), 0) == order[None, :]).astype(BF)


def qkv_order():
    order = np.zeros((4, 32, 3, 8), np.int32)
    sends, odd_sends = [], []
    odd_from, odd_to = np.zeros(128, np.int32), np.full(128, -1, np.int32)
    for z in range(4):
        owners = {}
        for group in (third * 128 + z * 32 + k for third in range(3) for k in range(32)):
            owners.setdefault(group // 3, []).append(group)
        by_size = {size: [owner for owner in sorted(owners) if len(owners[owner]) == size] for size in (1, 2, 3)}
        for place, owner in enumerate(by_size[3] + by_size[2]):
            c, x, y = place // 16, place // 4 % 4, place % 4
            source = (((y * 2 + x % 2) * 2 + c) * 4 + z) * 2 + x // 2
            sends.append((source, owner))
            groups = {group % 3: group for group in owners[owner]}
            if len(groups) == 2:
                odd_owner = by_size[1][place - len(by_size[3])]
                (odd,) = owners[odd_owner]
                (odd_from[source],) = {0, 1, 2} - set(groups)
                odd_to[odd_owner] = odd % 3
                odd_sends.append((source, odd_owner))
                groups[int(odd_from[source])] = odd
            for slot, group in groups.items():
                order[z, place, slot] = (group // 128) * 256 + (group % 32) * 8 + np.arange(8)
    return order.reshape(4, 768), sends, odd_sends, odd_from, odd_to


def on_device(
    tokens,
    memory,
    lengths,
    patch_counts,
    self_qkv,
    self_out,
    cross_query,
    cross_kv,
    cross_out,
    ffn_in,
    ffn_out,
    norm_gains,
    norm_shifts,
    proj_biases,
    ffn_bias,
    cotangent,
):
    y, xl, c, z, xh = (lax.axis_index(axis) for axis in AXES)
    x = xh * 2 + xl
    width = tokens.shape[2]
    rows = 2 * tokens.shape[1]
    page_rows = RING * rows
    length = lax.dynamic_index_in_dim(lengths, xh, 0, keepdims=False)
    count = lax.dynamic_slice(patch_counts, (xh,), (1,))
    valid = (z * rows + jnp.arange(rows) < length)[:, None]

    def swap_cores(part):
        return lax.ppermute(part, "c", FLIP)

    by_core = jnp.asarray(eight_order()).reshape(2, 512)
    eights = shuffle_matrix(by_core.reshape(-1))
    sides = shuffle_matrix(
        jnp.concatenate([lax.dynamic_index_in_dim(by_core, side, 0, keepdims=False) for side in (c, 1 - c)])
    )

    def own_eights(grads):
        return product(grads, sides).astype(BF)

    def relay(chunks, axis, pairs):
        return lax.ppermute(chunks[3], axis, pairs(1)), lax.ppermute(chunks[4], axis, pairs(3))

    def add_on(chunks, got):
        return relay_add(chunks[1], chunks[2], *got)

    def send_on(sums, axis, pairs):
        return lax.ppermute(sums[0], axis, pairs(1)), lax.ppermute(sums[1], axis, pairs(3))

    def finish(chunks, got):
        return sum_low(chunks[0], *got)

    X_RING, Y_RING = (("xl", "xh"), x_pairs), ("y", ring_pairs)

    def then_y(part):
        part = part.reshape(4, 32, part.shape[1])
        return ring_sum(
            lambda target: lax.dynamic_index_in_dim(part, target, 0, keepdims=False), y, "y", ring_pairs
        ).astype(BF)

    def then_x(part):
        each = part.shape[0] // 16
        part = part.reshape(2, 4, 2, each, part.shape[1])

        def cut(target):
            piece = lax.dynamic_slice(
                part, (target % 2, 0, target // 2, 0, 0), (1, 4, 1, each, part.shape[4])
            )
            return piece.reshape(4 * each, part.shape[4])

        return ring_sum(cut, x, ("xl", "xh"), x_pairs).astype(BF)

    mine = lax.dynamic_index_in_dim(tokens, xh, 0, keepdims=False)
    other = lax.dynamic_index_in_dim(tokens, 1 - xh, 0, keepdims=False)
    other = lax.ppermute(other, "xh", FLIP)
    early_rows = [mine] + [lax.ppermute(mine, "z", ring_pairs(step)) for step in STEPS]
    late_row = after(other, *early_rows)
    late_rows = [late_row] + [lax.ppermute(late_row, "z", ring_pairs(step)) for step in STEPS]
    own_memory = swap_in(after(memory, *early_rows), xh)
    def side_by_side(own, other):
        return jnp.concatenate([jnp.where(xh == 0, own, other), jnp.where(xh == 0, other, own)], axis=0)

    own_tokens = side_by_side(mine, late_row)

    def head_cols(matrix, third):
        return lax.dynamic_slice(matrix, (0, third * width + z * 256), (matrix.shape[0], 256))

    heads_qkv = jnp.concatenate([head_cols(self_qkv, third) for third in range(3)], axis=1)
    bias_q = lax.dynamic_slice(proj_biases, (0, z * 256), (1, 256))
    bias_v = lax.dynamic_slice(proj_biases, (1, z * 256), (1, 256))
    bias_qkv = jnp.concatenate([bias_q, jnp.zeros_like(bias_q), bias_v], axis=1)
    joined, low_one, normal_one = project_heads(
        z, xh, early_rows, late_rows, heads_qkv, bias_qkv, norm_gains[0:1], norm_shifts[0:1]
    )
    heads_mix, self_level = attend(page_rows, page_rows, 2, True, joined, joined, joined, (0, 256, 512))

    memory_here = after(own_memory, *late_rows)
    before_got, behind_got = (lax.ppermute(memory_here, "z", ring_pairs(step)) for step in (1, 3))
    heads_mix, before_got, behind_got = lax.optimization_barrier((heads_mix, before_got, behind_got))
    far_got = (
        lax.ppermute(behind_got[: rows // 2], "z", ring_pairs(3)),
        lax.ppermute(before_got[rows // 2 :], "z", ring_pairs(1)),
    )
    mix_pick = lambda target: lax.dynamic_slice(heads_mix, (target * rows, 0), (rows, 256))
    mix_got = exchange(mix_pick, z, far_got)
    far_got = lax.optimization_barrier((*far_got, *(part for _, part in mix_got[1:])))[:2]
    page_memory = jnp.zeros((page_rows, width), BF)
    for hop, first, part in (
        (0, 0, memory_here),
        (1, 0, behind_got),
        (3, 0, before_got),
        (2, 0, far_got[0]),
        (2, rows // 2, far_got[1]),
    ):
        page_memory = lax.dynamic_update_slice(page_memory, part, (around(hop, z) * rows + first, 0))
    patch_bias = jnp.concatenate([jnp.zeros_like(proj_biases[4]), proj_biases[4]])
    page_kv = (product(page_memory, cross_kv) + patch_bias).astype(BF)

    grad_low = jnp.where(valid, swap_in(after(cotangent, heads_mix), xh), 0)
    mixture = jnp.zeros((rows, width), BF)
    for source, part in mix_got:
        mixture = lax.dynamic_update_slice(mixture, part, (0, source * 256))
    after_self = own_tokens.astype(F32) + product(mixture, self_out) + proj_biases[2]
    normal_two, inverse_two = unit(after_self)
    low_two = (normal_two * norm_gains[1] + norm_shifts[1]).astype(BF)
    cross_queries = (product(low_two, cross_query) + proj_biases[3]).astype(BF)
    cross_mix, cross_level = attend(
        rows, page_rows, 8, False, cross_queries, page_kv, page_kv, (0, 0, 1024), count
    )
    after_cross = after_self + product(cross_mix, cross_out) + proj_biases[5]
    normal_three, inverse_three = unit(after_cross)
    low_three = (normal_three * norm_gains[2] + norm_shifts[2]).astype(BF)
    before = product(low_three, ffn_in) + ffn_bias
    below = 0.5 * (1.0 + lax.erf(before * np.float32(np.sqrt(0.5))))
    hidden = (before * below).astype(BF)
    slope = below + before * jnp.exp(-0.5 * before * before) * np.float32(1 / np.sqrt(2 * np.pi))
    result = after_cross + product(hidden, ffn_out) + proj_biases[6]
    layer_rows = jnp.where(valid, result, 0.0).astype(BF)

    order, sends, odd_sends, odd_from, odd_to = qkv_order()
    head_order = lax.dynamic_index_in_dim(jnp.asarray(order), z, 0, keepdims=False)
    head_shuffle, sides = lax.optimization_barrier((shuffle_matrix(head_order), sides))

    out_grads = own_eights(grad_low)
    early = jnp.concatenate([cross_mix, low_two, mixture, low_three, out_grads[:, 512:]], axis=1)
    early_got = swap_cores(early)
    hidden_got = swap_cores(hidden)
    grad_before = (back_product(grad_low, ffn_out) * slope).astype(BF)
    before_sums = column_sums(grad_before)
    in_keep, in_send = split_wides(c, grad_before)
    in_got = swap_cores(in_send)
    grad_three = back_product(grad_before, ffn_in)
    grad_after_cross = grad_low.astype(F32) + unit_back(
        normal_three, inverse_three, grad_three, norm_gains[2]
    )
    cross_low = grad_after_cross.astype(BF)
    cross_grads = own_eights(cross_low)
    cross_got = swap_cores(cross_grads[:, 512:])
    grad_cross_mix = back_product(cross_low, cross_out).astype(BF)
    ffn_in_chunks = outer_chunks(
        y, 512, 512, [((in_keep, 0), (in_got, 0), (early, 3 * width), (early_got, 3 * width), 2)]
    )
    ffn_out_chunks = outer_chunks(
        x,
        128,
        width,
        [
            ((out_grads, 0), (early_got, 4 * width), (hidden, 0), (hidden_got, 0), 4),
            ((cross_grads, 0), (cross_got, 0), (early, 0), (early_got, 0), 1),
        ],
    )
    ffn_out_got = relay(ffn_out_chunks, *X_RING)
    ffn_in_got = relay(ffn_in_chunks, *Y_RING)

    grad_cross_mix, layer_rows, *got = lax.optimization_barrier(
        (grad_cross_mix, layer_rows, *ffn_out_got, *ffn_in_got)
    )
    ffn_out_sums, ffn_in_sums = add_on(ffn_out_chunks, got[:2]), add_on(ffn_in_chunks, got[2:])
    grad_cross_mix, *sums = lax.optimization_barrier((grad_cross_mix, *ffn_out_sums, *ffn_in_sums))
    ffn_out_got, ffn_in_got = send_on(sums[:2], *X_RING), send_on(sums[2:], *Y_RING)
    cross_query_low, patch_grads = attend_back(
        rows,
        page_rows,
        8,
        False,
        cross_queries,
        page_kv,
        page_kv,
        (0, 0, 1024),
        cross_mix,
        grad_cross_mix,
        cross_level,
        count,
    )
    cross_query_low, patch_grads, layer_rows, *got = lax.optimization_barrier(
        (cross_query_low, patch_grads, layer_rows, *ffn_out_got, *ffn_in_got)
    )
    layer_out = swap_out(layer_rows, xh)
    ffn_out_part, ffn_in_part = finish(ffn_out_chunks, got[:2]), finish(ffn_in_chunks, got[2:])
    grad_two = back_product(cross_query_low, cross_query)
    grad_after_self = grad_after_cross + unit_back(normal_two, inverse_two, grad_two, norm_gains[1])

    self_low = grad_after_self.astype(BF)
    grad_mix_rows = back_product(self_low, self_out).astype(BF)
    grads_here = after(patch_grads, grad_mix_rows)
    kv_send, kv_keep = patch_halves(c, grads_here, page_memory)
    grad_mixture = rows_to_heads(grad_mix_rows, z, (kv_send,))
    grads_here = after(patch_grads, grad_mixture)
    kv_rows = sum_low(kv_keep, swap_cores(kv_send))
    kv_quarters = kv_rows.reshape(RING, 256, width)

    def kv_chunk(hop):
        return lax.dynamic_index_in_dim(kv_quarters, around(hop, y), 0, keepdims=False)

    kv_own, kv_sends = kv_chunk(0), [kv_chunk(step) for step in STEPS]
    out_quarters = ffn_out_part.reshape(RING, 32, 5 * width)
    out_own, *out_sends = (
        lax.dynamic_index_in_dim(out_quarters, around(hop, y), 0, keepdims=False) for hop in (0,) + STEPS
    )
    query_grads, self_grads = own_eights(cross_query_low), own_eights(self_low)
    sent = swap_cores(jnp.concatenate([query_grads[:, 512:], self_grads[:, 512:]], axis=1))
    sent, *out_sends = lax.optimization_barrier((sent, *out_sends))
    out_got = [lax.ppermute(chunk, "y", ring_pairs(step)) for step, chunk in zip(STEPS, out_sends)]
    two_chunks = outer_chunks(
        x,
        128,
        width,
        [
            ((query_grads, 0), (sent, 0), (early, width), (early_got, width), 1),
            ((self_grads, 0), (sent, 512), (early, 2 * width), (early_got, 2 * width), 1),
        ],
        extra=ffn_in_part,
    )
    two_chunks = lax.optimization_barrier((*two_chunks, *out_got))
    two_chunks, out_got = two_chunks[:5], two_chunks[5:]
    grad_mixture, layer_out, *held = lax.optimization_barrier(
        (grad_mixture, layer_out, *kv_sends, *two_chunks)
    )
    kv_sends, two_chunks = held[:3], held[3:]

    two_got = relay(two_chunks, *X_RING)
    kv_got = [lax.ppermute(chunk, "y", ring_pairs(step)) for step, chunk in zip(STEPS, kv_sends)]
    (grad_joined,) = attend_back(
        page_rows, page_rows, 2, True, joined, joined, joined, (0, 256, 512), heads_mix, grad_mixture, self_level
    )
    grad_joined, grads_here, *two_got = lax.optimization_barrier((grad_joined, grads_here, *two_got))
    *page_chunks, page_sums, head_sums = page_back(z, grad_joined, heads_qkv, grads_here, cross_kv, normal_one)
    shuffled = product(grad_joined, head_shuffle).astype(BF)
    shuffled, page_sums, head_sums, *held = lax.optimization_barrier(
        (shuffled, page_sums, head_sums, *page_chunks, *kv_got)
    )
    page_chunks, kv_got = held[:5], held[5:]

    def core_half(target):
        return outer(lax.dynamic_slice(shuffled, (0, target * 384), (page_rows, 384)), low_one)

    core_keep = core_half(c)
    core_send = core_half(1 - c).astype(BF)
    core_keep, core_send, *held = lax.optimization_barrier(
        (core_keep, core_send, *page_chunks, *two_got, *kv_got, *out_got)
    )
    page_chunks, held = held[:5], held[5:]
    two_got, kv_got, out_got = held[:2], held[2:5], held[5:]
    ffn_out_part = sum_low(out_own, *out_got)

    core_got = swap_cores(core_send).astype(F32)
    two_got = send_on(add_on(two_chunks, two_got), *X_RING)

    Z_RING = ("z", ring_pairs)
    page_got = relay(page_chunks, *Z_RING)
    before_sums = after(before_sums, core_send)

    def at_heads(sums):
        return lax.dynamic_update_slice(jnp.zeros((width,), F32), sums, (z * 256,))

    vectors = [
        page_sums[0],
        column_sums(grad_two * normal_two),
        column_sums(grad_three * normal_three),
        page_sums[1],
        column_sums(grad_two),
        column_sums(grad_three),
        at_heads(head_sums[0, :256]),
        at_heads(head_sums[0, 512:]),
        column_sums(grad_after_self),
        column_sums(cross_query_low),
        page_sums[2],
        column_sums(grad_after_cross),
        column_sums(grad_low),
    ]
    small = jnp.concatenate([jnp.stack(vectors), before_sums.reshape(width, 4).T], axis=0)
    small = lax.dot_general(
        small, eights.astype(F32), (((1,), (0,)), ((), ())), precision=lax.Precision.HIGHEST
    )
    small = small.reshape(17, 2, 16, 4, 8).transpose(1, 2, 3, 0, 4).reshape(2, 16, 4, 17 * 8)
    small = jnp.pad(small, ((0, 0), (0, 0), (0, 0), (0, 256 - 17 * 8))).reshape(2, 16, width).astype(BF)
    small_keep = lax.dynamic_index_in_dim(small, c, 0, keepdims=False)
    small_send = lax.dynamic_index_in_dim(small, 1 - c, 0, keepdims=False)
    small_sum = (small_keep.astype(F32) + swap_cores(small_send).astype(F32)).astype(BF)
    core_sum = (core_keep + core_got).astype(BF)
    kv_part = sum_low(kv_own, *kv_got)
    core_sum, small_sum, kv_part, *held = lax.optimization_barrier(
        (core_sum, small_sum, kv_part, *two_got, *page_got)
    )
    two_got, page_got = held[:2], held[2:]

    page_got = send_on(add_on(page_chunks, page_got), *Z_RING)
    small_sum = jnp.pad(small_sum.reshape(4, 4, 1, width), ((0, 0), (0, 0), (0, 7), (0, 0)))
    core_sum = jnp.concatenate([core_sum.reshape(4, 4, 24, width), small_sum], axis=2)
    kv_lines = kv_part.reshape(2, 4, 2, 16, width)

    def x_chunk(target):
        piece = lax.dynamic_slice(kv_lines, (target % 2, 0, target // 2, 0, 0), (1, 4, 1, 16, width))
        lines = lax.dynamic_index_in_dim(core_sum, target, 0, keepdims=False)
        return jnp.concatenate([lines.reshape(128, width), piece.reshape(64, width)], axis=0)

    x_sum = ring_sum(x_chunk, x, ("xl", "xh"), x_pairs).astype(BF)
    two_part = finish(two_chunks, two_got)
    x_sum, two_part, mine, late_row, *page_got = lax.optimization_barrier(
        (x_sum, two_part, mine, late_row, *page_got)
    )
    own_tokens = side_by_side(mine, late_row)

    two_part, ffn_in_part = two_part[:, : 2 * width].reshape(4, 32, 2 * width), two_part[:, 2 * width :]
    cross_kv_part = x_sum[128:]
    y_lines = jnp.concatenate([x_sum[:128].reshape(4, 32, width), two_part], axis=2)
    y_sum = ring_sum(
        lambda target: lax.dynamic_index_in_dim(y_lines, target, 0, keepdims=False), y, "y", ring_pairs
    )
    grad_own, memory_rows = (
        sum(part[:, at : at + width].astype(F32) for part in (page_chunks[0], *page_got)) for at in (0, width)
    )
    own_normal, own_inverse = unit(own_tokens.astype(F32))
    token_rows = grad_after_self + unit_back(own_normal, own_inverse, grad_own, norm_gains[0])
    both_grads = swap_out(jnp.concatenate([token_rows, memory_rows], axis=1).astype(BF), xh)
    token_grad, memory_grad = both_grads[..., :width], both_grads[..., width:]

    two_part, y_sum = y_sum[:, width:].astype(BF), y_sum[:, :width]
    small_part = jnp.pad(y_sum[24].astype(BF).reshape(4, 1, 256), ((0, 0), (0, 7), (0, 768)))
    me = (((y * 2 + xl) * 2 + c) * 4 + z) * 2 + xh
    odd_at = lax.dynamic_index_in_dim(jnp.asarray(odd_from), me, 0, keepdims=False) * 8
    odd_got = lax.ppermute(lax.dynamic_slice(y_sum, (odd_at, 0), (8, width)), AXES, odd_sends)
    odd_here = jnp.arange(24) // 8 == lax.dynamic_index_in_dim(jnp.asarray(odd_to), me, 0, keepdims=False)
    grad_qkv = lax.ppermute(y_sum[:24], AXES, sends)
    grad_qkv = jnp.where(odd_here[:, None], jnp.concatenate([odd_got] * 3, axis=0), grad_qkv)

    lines = []
    for part in (ffn_out_part, ffn_in_part, two_part, cross_kv_part, small_part):
        part = part.reshape(4, -1, part.shape[-1])
        lines += [part[..., at : at + width] for at in range(0, part.shape[-1], width)]
    lines = jnp.concatenate(lines, axis=1)
    z_line = lambda hop: lax.dynamic_index_in_dim(lines, around(hop, z), 0, keepdims=False)
    z_got = [lax.ppermute(z_line(step), "z", ring_pairs(step)) for step in STEPS]
    ffn_out_rows, cross_out_rows, ffn_in_rows, cross_query_rows, self_out_rows, cross_kv_rows, *small = last_sums(
        z_line(0), *z_got
    )

    return (
        layer_out,
        token_grad,
        memory_grad,
        grad_qkv.T,
        self_out_rows.T,
        cross_query_rows.T,
        cross_kv_rows.T,
        cross_out_rows.T,
        ffn_in_rows.T,
        ffn_out_rows.T,
        *small[:3],
        small[3].reshape(-1),
    )


def solution(mesh):
    split = jax.sharding.Mesh(mesh.devices.reshape(MESH_SHAPE), AXES)
    page, blk = AXES[:3], AXES[3:]
    blocks, cols = P(page, blk, None), P(None, AXES)
    in_specs = (blocks, blocks, P(page), P(page)) + (P(),) * 11 + (blocks,)
    out_specs = (blocks,) * 3 + (cols,) * 10 + (P(AXES),)
    return jax.shard_map(
        on_device, mesh=split, in_specs=in_specs, out_specs=out_specs, check_vma=False
    )
```

```python
import functools

import jax
import jax.numpy as jnp
import numpy as np
from jax import lax
from jax.experimental import pallas as pl
from jax.experimental.pallas import tpu as pltpu
from jax.sharding import PartitionSpec as P

EPS = 1e-05

BF = jnp.bfloat16
F32 = jnp.float32
NEG = -1e30
TILE = 256
PAIR = 128
HINT = pl.CostEstimate(flops=1 << 20, bytes_accessed=1 << 16, transcendentals=0)


def dot_tt(a, b):
    return lax.dot_general(a, b, (((1,), (1,)), ((), ())), preferred_element_type=F32)


def dot_nn(a, b):
    return lax.dot_general(a, b, (((1,), (0,)), ((), ())), preferred_element_type=F32)


def two_heads(rows):
    lanes = lax.broadcasted_iota(jnp.int32, rows.shape, 1)
    none = jnp.zeros_like(rows)
    return jnp.concatenate([jnp.where(lanes < 64, rows, none), jnp.where(lanes < 64, none, rows)], axis=0)


def later_key():
    keys = lax.broadcasted_iota(jnp.int32, (TILE, 2 * TILE), 0)
    return keys > lax.broadcasted_iota(jnp.int32, (TILE, 2 * TILE), 1) % TILE


def own_halves(both):
    return jnp.concatenate([both[:64, :TILE], both[64:, TILE:]], axis=0).T


def span(tile):
    return pl.ds(tile * TILE, TILE)


def forward_tiles(key_tiles, causal, q_ref, k_ref, o_ref, lse_ref, vt_ref, s_ref):
    for i in range(q_ref.shape[0] // TILE):
        tiles = i + 1 if causal else key_tiles
        queries = two_heads(q_ref[span(i), :] * 0.125)
        kept = s_ref.at[i % 2]
        top = None
        for j in range(tiles):
            scores = dot_tt(k_ref[span(j), :], queries)
            if causal and j == i:
                scores = jnp.where(later_key(), NEG, scores)
            kept[span(j), :] = scores
            tile_top = jnp.max(scores, axis=0, keepdims=True)
            top = tile_top if top is None else jnp.maximum(top, tile_top)
        total, mixed = None, None
        for j in range(tiles):
            shares = jnp.exp(kept[span(j), :] - top)
            tile_sum = jnp.sum(shares, axis=0, keepdims=True)
            tile_mix = dot_nn(vt_ref[:, span(j)], shares.astype(BF))
            total = tile_sum if total is None else total + tile_sum
            mixed = tile_mix if mixed is None else mixed + tile_mix
        level = top + jnp.log(total)
        lse_ref[0, 0:1, span(i)] = level[:, :TILE]
        lse_ref[0, 1:2, span(i)] = level[:, TILE:]
        o_ref[span(i), :] = own_halves(mixed / total).astype(o_ref.dtype)


def pair_columns(pair, first=0):
    return pl.ds(pl.multiple_of(pair * PAIR + first, PAIR), PAIR)


def every_pair(pairs, count_ref, tiles, run):
    def loop(live):
        @pl.loop(0, pairs // 2)
        def _(couple):
            run(2 * couple, 0, live)
            run(2 * couple + 1, 1, live)

    if count_ref is None:
        loop(tiles)
    else:
        pl.when(count_ref[0] > TILE)(lambda: loop(tiles))
        pl.when(count_ref[0] <= TILE)(lambda: loop(1))


def forward_kernel(pairs, causal, firsts, *refs):
    count_ref = None if causal else refs[0]
    refs = refs if causal else refs[1:]
    q_ref, k_ref, v_ref, o_ref, lse_ref, vt_ref, s_ref = refs

    def run(pair, slot, tiles):
        q, k, v = (ref.at[:, pair_columns(pair, at)] for ref, at in zip((q_ref, k_ref, v_ref), firsts))
        vt, kept = vt_ref.at[slot], s_ref.at[slot]
        vt[:, : tiles * TILE] = v[: tiles * TILE, :].T
        out, level = o_ref.at[:, pair_columns(pair)], lse_ref.at[pl.ds(pair, 1)]
        forward_tiles(tiles, causal, q, k, out, level, vt, kept)

    every_pair(pairs, count_ref, k_ref.shape[0] // TILE, run)


def backward_tiles(
    key_tiles, causal, q_ref, k_ref, v_ref, o_ref, do_ref, lse_ref, dq_ref, kt_ref, dk_ref, dv_ref
):
    ones = jnp.ones((8, PAIR), F32)
    for i in range(q_ref.shape[0] // TILE):
        tiles = i + 1 if causal else key_tiles
        queries = two_heads(q_ref[span(i), :] * 0.125)
        pulled = two_heads(do_ref[span(i), :])
        out = o_ref[span(i), :].astype(F32)
        weighed = pulled.astype(F32) * jnp.concatenate([out, out], axis=0)
        dots = lax.dot_general(
            ones,
            weighed,
            (((1,), (1,)), ((), ())),
            preferred_element_type=F32,
            precision=lax.Precision.HIGHEST,
        )[0:1, :]
        level = jnp.concatenate([lse_ref[0, 0:1, span(i)], lse_ref[0, 1:2, span(i)]], axis=1)
        drawn = None
        for j in range(tiles):
            shares = jnp.exp(dot_tt(k_ref[span(j), :], queries) - level)
            if causal and j == i:
                shares = jnp.where(later_key(), 0.0, shares)
            grad_shares = dot_tt(v_ref[span(j), :], pulled)
            grad_scores = (shares * (grad_shares - dots)).astype(BF)
            dv_part = dot_nn(shares.astype(BF), pulled)
            dk_part = dot_nn(grad_scores, queries)
            if i == (j if causal else 0):
                dv_ref[span(j), :] = dv_part
                dk_ref[span(j), :] = dk_part
            else:
                dv_ref[span(j), :] += dv_part
                dk_ref[span(j), :] += dk_part
            tile_drawn = dot_nn(kt_ref[:, span(j)], grad_scores)
            drawn = tile_drawn if drawn is None else drawn + tile_drawn
        dq_ref[span(i), :] = (own_halves(drawn) * 0.125).astype(dq_ref.dtype)


def backward_kernel(pairs, causal, firsts, *refs):
    count_ref = None if causal else refs[0]
    refs = refs if causal else refs[1:]
    q_ref, k_ref, v_ref, o_ref, do_ref, lse_ref, *outs, kt_ref, dk_ref, dv_ref = refs
    dq_ref, dkv_ref = outs[0], outs[-1]
    width = pairs * PAIR
    first = dkv_ref.shape[1] - 2 * width

    def run(pair, slot, tiles):
        q, k, v = (ref.at[:, pair_columns(pair, at)] for ref, at in zip((q_ref, k_ref, v_ref), firsts))
        cols, live = pair_columns(pair), tiles * TILE
        kt, dk, dv = kt_ref.at[slot], dk_ref.at[slot], dv_ref.at[slot]
        kt[:, :live] = k[:live, :].T
        if live < k.shape[0]:
            dk[...] = jnp.zeros_like(dk)
            dv[...] = jnp.zeros_like(dv)
        out, grads, level = o_ref.at[:, cols], do_ref.at[:, cols], lse_ref.at[pl.ds(pair, 1)]
        backward_tiles(
            tiles, causal, q, k, v, out, grads, level, dq_ref.at[:, cols], kt, dk, dv
        )
        dkv_ref[:, pair_columns(pair, first)] = dk[...].astype(BF)
        dkv_ref[:, pair_columns(pair, first + width)] = dv[...].astype(BF)

    every_pair(pairs, count_ref, k_ref.shape[0] // TILE, run)


SCALAR = pl.BlockSpec(memory_space=pltpu.SMEM)
HERE = pl.BlockSpec(memory_space=pltpu.VMEM)


def attend(q_rows, key_rows, pairs, causal, q, k, v, firsts, count=None):
    return pl.pallas_call(
        functools.partial(forward_kernel, pairs, causal, firsts),
        in_specs=([] if causal else [SCALAR]) + [HERE] * 3,
        out_specs=[HERE] * 2,
        out_shape=[
            jax.ShapeDtypeStruct((q_rows, pairs * PAIR), BF),
            jax.ShapeDtypeStruct((pairs, 2, q_rows), F32),
        ],
        scratch_shapes=[pltpu.VMEM((2, PAIR, key_rows), BF), pltpu.VMEM((2, 2, key_rows, 2 * TILE), F32)],
        compiler_params=pltpu.CompilerParams(vmem_limit_bytes=32 * 1024 * 1024),
        cost_estimate=HINT,
    )(*(() if causal else (count,)), q, k, v)


def attend_back(q_rows, key_rows, pairs, causal, q, k, v, firsts, o, do, lse, count=None):
    width = pairs * PAIR
    shapes = [jax.ShapeDtypeStruct((q_rows, width), BF), jax.ShapeDtypeStruct((key_rows, 2 * width), BF)]
    if causal:
        shapes = [jax.ShapeDtypeStruct((q_rows, 3 * width), BF)]
    return pl.pallas_call(
        functools.partial(backward_kernel, pairs, causal, firsts),
        in_specs=([] if causal else [SCALAR]) + [HERE] * 6,
        out_specs=[HERE] * len(shapes),
        out_shape=shapes,
        scratch_shapes=[
            pltpu.VMEM((2, PAIR, key_rows), BF),
            pltpu.VMEM((2, key_rows, PAIR), F32),
            pltpu.VMEM((2, key_rows, PAIR), F32),
        ],
        compiler_params=pltpu.CompilerParams(vmem_limit_bytes=32 * 1024 * 1024),
        cost_estimate=HINT,
    )(*(() if causal else (count,)), q, k, v, o, do, lse)

AXES = ("y", "xl", "c", "z", "xh")
MESH_SHAPE = (4, 2, 2, 4, 2)
RING = 4


def ring_pairs(step):
    return [(i, (i + step) % RING) for i in range(RING)]


def x_slot(x):
    return (x % 2) * 2 + x // 2


def x_pairs(step):
    return [(x_slot(x), x_slot((x + step) % RING)) for x in range(RING)]


FLIP = [(0, 1), (1, 0)]
STEPS = (1, 3, 2)


def around(step, coord):
    return lax.rem(coord + step, RING)


def swap_in(blocks, side):
    own = lax.dynamic_index_in_dim(blocks, side, 0, keepdims=False)
    got = lax.ppermute(lax.dynamic_index_in_dim(blocks, 1 - side, 0, keepdims=False), "xh", FLIP)
    return jnp.concatenate([jnp.where(side == 0, own, got), jnp.where(side == 0, got, own)], axis=0)


def swap_out(rows, side):
    blocks = rows.reshape(2, rows.shape[0] // 2, rows.shape[1])
    own = lax.dynamic_index_in_dim(blocks, side, 0, keepdims=False)
    got = lax.ppermute(lax.dynamic_index_in_dim(blocks, 1 - side, 0, keepdims=False), "xh", FLIP)
    return jnp.stack([jnp.where(side == 0, own, got), jnp.where(side == 0, got, own)])


def exchange(pick, z, behind=()):
    got = [lax.ppermute(pick(around(step, z)), "z", ring_pairs(step)) for step in STEPS]
    got = lax.optimization_barrier((*got, *behind))[: len(STEPS)]
    return [(z, pick(z))] + [(around(RING - step, z), part) for step, part in zip(STEPS, got)]


def rows_to_heads(rows, z, behind=()):
    height, width = rows.shape[0], rows.shape[1] // RING
    full = jnp.zeros((RING * height, width), rows.dtype)
    pick = lambda target: lax.dynamic_slice(rows, (0, target * width), (height, width))
    for source, part in exchange(pick, z, behind):
        full = lax.dynamic_update_slice(full, part, (source * height, 0))
    return full


def ring_sum(pick, coord, axis, pairs):
    total = pick(coord).astype(F32)
    for step in STEPS:
        got = lax.ppermute(pick(around(step, coord)).astype(BF), axis, pairs(step))
        total = total + got.astype(F32)
    return total


def after(value, *others):
    return lax.optimization_barrier((value, *others))[0]


def product(left, right):
    return jnp.dot(left, right, preferred_element_type=F32)


def back_product(grads, matrix):
    return lax.dot_general(grads, matrix, (((1,), (1,)), ((), ())), preferred_element_type=F32)


def outer(grads, inputs):
    return lax.dot_general(grads, inputs, (((0,), (0,)), ((), ())), preferred_element_type=F32)


def unit(rows):
    centred = rows - jnp.mean(rows, axis=-1, keepdims=True)
    inverse = lax.rsqrt(jnp.mean(centred * centred, axis=-1, keepdims=True) + EPS)
    return centred * inverse, inverse


def unit_back(normal, inverse, grads, gain):
    scaled = grads * gain
    mean = jnp.mean(scaled, axis=-1, keepdims=True)
    along = jnp.mean(scaled * normal, axis=-1, keepdims=True)
    return inverse * (scaled - mean - normal * along)


def chunks_kernel(width, block, segments, coord_ref, *refs):
    outs, turned_ref = refs[-6:-1], refs[-1]
    own_ref, plus_ref, minus_ref, far_a_ref, far_b_ref = outs
    tokens = refs[0].shape[0]
    half, each = width // 2, width // 4
    lane = 0

    def put(pick, lanes):
        own_ref[:, lanes] = pick(0, 0, width).astype(F32)
        plus_ref[:, lanes] = pick(1, 0, width).astype(BF)
        minus_ref[:, lanes] = pick(3, 0, width).astype(BF)
        far_a_ref[:, lanes] = pick(2, 0, half).astype(BF)
        far_b_ref[:, lanes] = pick(2, half, half).astype(BF)

    for at, (grads_at, got_grads_at, inputs_at, got_inputs_at, blocks) in enumerate(segments):
        grads_ref, got_grads_ref, inputs_ref, got_inputs_ref = refs[4 * at : 4 * at + 4]
        for hop in range(RING):
            column = around(hop, coord_ref[0]) * width
            rows = slice(hop * width, hop * width + width)
            turned_ref[at, rows, :tokens] = grads_ref[:, pl.ds(pl.multiple_of(grads_at + column, 128), width)].T
            turned_ref[at, rows, tokens:] = got_grads_ref[
                :, pl.ds(pl.multiple_of(got_grads_at + column, 128), width)
            ].T
        for number in range(blocks):
            mine = inputs_ref[:, inputs_at + number * block : inputs_at + number * block + block]
            got = got_inputs_ref[:, got_inputs_at + number * block : got_inputs_at + number * block + block]

            def pick(hop, first, rows, at=at, mine=mine, got=got):
                turned = turned_ref.at[at, hop * width + first : hop * width + first + rows, :]
                return dot_nn(turned[:, :tokens], mine) + dot_nn(turned[:, tokens:], got)

            put(pick, slice(lane, lane + block))
            lane += block

    if lane < own_ref.shape[1]:
        extra_ref = refs[4 * len(segments)]

        def pick(hop, first, rows):
            target = around(hop, coord_ref[0])
            zs = range(first // each, (first + rows) // each)
            return jnp.concatenate([extra_ref[target % 2, zz, target // 2] for zz in zs], axis=0)

        put(pick, slice(lane, own_ref.shape[1]))


def outer_chunks(coord, width, block, segments, extra=None):
    cols = RING * width
    tokens = segments[0][0][0].shape[0]
    operands = [array for segment in segments for array, _ in segment[:4]]
    places = tuple(tuple(first for _, first in segment[:4]) + (segment[4],) for segment in segments)
    lanes = sum(segment[4] for segment in segments) * block
    if extra is not None:
        operands.append(extra.reshape(2, 4, 2, width // 4, extra.shape[1]))
        lanes += extra.shape[1]
    shape = lambda rows, dtype: jax.ShapeDtypeStruct((rows, lanes), dtype)
    return pl.pallas_call(
        functools.partial(chunks_kernel, width, block, places),
        in_specs=[SCALAR] + [HERE] * len(operands),
        out_specs=[HERE] * 5,
        out_shape=[shape(width, F32), shape(width, BF), shape(width, BF)] + [shape(width // 2, BF)] * 2,
        scratch_shapes=[pltpu.VMEM((len(segments), cols, 2 * tokens), BF)],
        compiler_params=pltpu.CompilerParams(vmem_limit_bytes=40 * 1024 * 1024),
        cost_estimate=HINT,
    )(coord.reshape(1), *operands)


def project_kernel(place_ref, *refs):
    early, late = refs[:RING], refs[RING : 2 * RING]
    matrix_ref, bias_ref, gain_ref, shift_ref, joined_ref, low_ref, normal_ref = refs[2 * RING :]

    def run(at):
        first = jnp.where(place_ref[1] == 0, early[at][...], late[at][...])
        second = jnp.where(place_ref[1] == 0, late[at][...], early[at][...])
        normal, _ = unit(jnp.concatenate([first, second], axis=0).astype(F32))
        low = (normal * gain_ref[...] + shift_ref[...]).astype(BF)
        low_ref[...] = low
        normal_ref[...] = normal.astype(BF)
        joined_ref[...] = (dot_nn(low, matrix_ref[...]) + bias_ref[...]).astype(BF)

    for at in range(RING):
        pl.when(pl.program_id(0) == at)(functools.partial(run, at))


def project_heads(z, side, early, late, matrix, bias, gain, shift):
    half, width = early[0].shape
    rows = 2 * half

    def row_block(j, place):
        hop = jnp.where(j == 0, 0, jnp.where(j == 1, STEPS[0], jnp.where(j == 2, STEPS[1], STEPS[2])))
        return (lax.rem(place[0] + RING - hop, RING), 0)

    whole = lambda shape: pl.BlockSpec(shape, lambda j, place: (0, 0))
    return pl.pallas_call(
        project_kernel,
        grid_spec=pltpu.PrefetchScalarGridSpec(
            num_scalar_prefetch=1,
            grid=(RING,),
            in_specs=[whole((half, width))] * 8
            + [whole((width, 768)), whole((1, 768)), whole((1, width)), whole((1, width))],
            out_specs=[
                pl.BlockSpec((rows, 768), row_block),
                pl.BlockSpec((rows, width), row_block),
                pl.BlockSpec((rows, width), row_block),
            ],
        ),
        out_shape=[
            jax.ShapeDtypeStruct((RING * rows, 768), BF),
            jax.ShapeDtypeStruct((RING * rows, width), BF),
            jax.ShapeDtypeStruct((RING * rows, width), BF),
        ],
        compiler_params=pltpu.CompilerParams(vmem_limit_bytes=40 * 1024 * 1024),
        cost_estimate=HINT,
    )(jnp.stack([z, side]), *early, *late, matrix, bias, gain, shift)


def split_kernel(core_ref, grads_ref, keep_ref, send_ref):
    for at in range(grads_ref.shape[1] // 512):
        first = grads_ref[:, 512 * at : 512 * at + 256]
        second = grads_ref[:, 512 * at + 256 : 512 * at + 512]
        keep_ref[:, 256 * at : 256 * at + 256] = jnp.where(core_ref[0] == 0, first, second)
        send_ref[:, 256 * at : 256 * at + 256] = jnp.where(core_ref[0] == 0, second, first)


def split_wides(core, grads):
    rows, cols = grads.shape
    put = pl.BlockSpec((rows // 2, cols // 2), lambda j: (j, 0))
    return pl.pallas_call(
        split_kernel,
        grid=(2,),
        in_specs=[SCALAR, pl.BlockSpec((rows // 2, cols), lambda j: (j, 0))],
        out_specs=[put, put],
        out_shape=[jax.ShapeDtypeStruct((rows, cols // 2), BF)] * 2,
        compiler_params=pltpu.CompilerParams(vmem_limit_bytes=32 * 1024 * 1024),
        cost_estimate=HINT,
    )(core.reshape(1), grads)


def patch_halves_kernel(side_ref, grads_ref, inputs_ref, send_ref, keep_ref):
    for out_ref, side in ((send_ref, 1 - side_ref[0]), (keep_ref, side_ref[0])):
        for group in range(8):
            column = pl.multiple_of((group * 2 + side) * 128, 128)
            part = outer(grads_ref[:, pl.ds(column, 128)], inputs_ref[...])
            out_ref[group * 128 : group * 128 + 128, :] = part.astype(BF)


def patch_halves(side, grads, inputs):
    patches, width = inputs.shape
    return pl.pallas_call(
        patch_halves_kernel,
        in_specs=[SCALAR, HERE, HERE],
        out_specs=[HERE, HERE],
        out_shape=[jax.ShapeDtypeStruct((1024, width), BF)] * 2,
        compiler_params=pltpu.CompilerParams(vmem_limit_bytes=32 * 1024 * 1024),
        cost_estimate=HINT,
    )(side.reshape(1), grads, inputs)


def page_kernel(place_ref, joined_ref, heads_ref, patch_ref, cross_ref, normal_ref, *refs):
    own_ref, plus_ref, minus_ref, far_a_ref, far_b_ref, sums_ref, head_sums_ref = refs
    rows, width = own_ref.shape[0], cross_ref.shape[0]
    half = rows // 2
    sums, head_sums = [0.0, 0.0, 0.0], 0.0
    for hop in range(RING):
        here = pl.ds(pl.multiple_of(around(hop, place_ref[0]) * rows, rows), rows)
        one = dot_tt(joined_ref[here, :], heads_ref[...])
        sums[0] += jnp.sum(one * normal_ref[here, :].astype(F32), axis=0, keepdims=True)
        sums[1] += jnp.sum(one, axis=0, keepdims=True)
        sums[2] += jnp.sum(patch_ref[here, width:].astype(F32), axis=0, keepdims=True)
        head_sums += jnp.sum(joined_ref[here, :].astype(F32), axis=0, keepdims=True)
        two = dot_tt(patch_ref[here, :], cross_ref[...])
        for part, lanes in ((one, slice(0, width)), (two, slice(width, 2 * width))):
            if hop == 2:
                far_a_ref[:, lanes] = part[:half].astype(BF)
                far_b_ref[:, lanes] = part[half:].astype(BF)
            else:
                out_ref = {0: own_ref, 1: plus_ref, 3: minus_ref}[hop]
                out_ref[:, lanes] = part.astype(out_ref.dtype)
    sums_ref[...] = jnp.concatenate(sums, axis=0)
    head_sums_ref[...] = head_sums


def page_back(z, joined, heads, patch_grads, cross_kv, normal):
    page_rows, width = normal.shape
    rows = page_rows // RING
    chunk = lambda height, dtype: jax.ShapeDtypeStruct((height, 2 * width), dtype)
    return pl.pallas_call(
        page_kernel,
        in_specs=[SCALAR] + [HERE] * 5,
        out_specs=[HERE] * 7,
        out_shape=[
            chunk(rows, F32),
            chunk(rows, BF),
            chunk(rows, BF),
            chunk(rows // 2, BF),
            chunk(rows // 2, BF),
            jax.ShapeDtypeStruct((3, width), F32),
            jax.ShapeDtypeStruct((1, joined.shape[1]), F32),
        ],
        compiler_params=pltpu.CompilerParams(vmem_limit_bytes=40 * 1024 * 1024),
        cost_estimate=HINT,
    )(z.reshape(1), joined, heads, patch_grads, cross_kv, normal)


def relay_add_kernel(plus_ref, minus_ref, got_a_ref, got_b_ref, plus_out_ref, minus_out_ref):
    half = got_a_ref.shape[0]
    plus_out_ref[:half] = (plus_ref[:half].astype(F32) + got_a_ref[...].astype(F32)).astype(BF)
    plus_out_ref[half:] = plus_ref[half:]
    minus_out_ref[:half] = minus_ref[:half]
    minus_out_ref[half:] = (minus_ref[half:].astype(F32) + got_b_ref[...].astype(F32)).astype(BF)


def relay_add(plus, minus, got_a, got_b):
    return pl.pallas_call(
        relay_add_kernel,
        in_specs=[HERE] * 4,
        out_specs=[HERE] * 2,
        out_shape=[jax.ShapeDtypeStruct(plus.shape, BF)] * 2,
        compiler_params=pltpu.CompilerParams(vmem_limit_bytes=32 * 1024 * 1024),
        cost_estimate=HINT,
    )(plus, minus, got_a, got_b)


def vectors_kernel(place_ref, *refs):
    *row_refs, heads_ref, bias_ref, keep_ref, send_ref = refs
    width = bias_ref.shape[1]
    quarter = width // 4
    at_heads = lax.broadcasted_iota(jnp.int32, (1, width), 1) // quarter == place_ref[0]
    own = [ref[...] for ref in row_refs]
    for place, first in ((6, 0), (7, 2 * quarter)):
        part = heads_ref[:, first : first + quarter]
        own.insert(place, jnp.where(at_heads, jnp.concatenate([part] * 4, axis=1), 0.0))
    group = lax.broadcasted_iota(jnp.int32, (32, width), 0)
    col = lax.broadcasted_iota(jnp.int32, (32, width), 1)

    def of_group(owner, y):
        return group == owner // 8 % 2 * 16 + (owner % 2 * 2 + owner // 16 % 2) * 4 + y

    eights = of_group(col // 8, col // 256)
    picked = [jnp.where(eights, row.astype(BF).astype(F32), 0.0).astype(BF) for row in own]
    for y in range(4):
        bias = bias_ref[y : y + 1, :].astype(BF).astype(F32)
        picked.append(jnp.where(of_group(col // 32, y), bias, 0.0).astype(BF))
    col = lax.broadcasted_iota(jnp.int32, (width, 128), 0)
    lane = lax.broadcasted_iota(jnp.int32, (width, 128), 1)
    narrow = (lane == col // 16 % 4 * 8 + col % 8).astype(F32).astype(BF)
    wide = (lane == col // 64 % 4 * 32 + col % 32).astype(F32).astype(BF)
    rows = dot_nn(jnp.concatenate(picked[:13], axis=0), narrow).astype(BF)
    bias = dot_nn(jnp.concatenate(picked[13:], axis=0), wide).astype(BF)
    bias = bias[:32] + bias[32:64] + bias[64:96] + bias[96:]
    lane = lax.broadcasted_iota(jnp.int32, (128, width), 0)
    spot = lax.broadcasted_iota(jnp.int32, (128, width), 1)
    packed = dot_nn(bias, (spot == lane // 32 * 256 + 104 + lane % 32).astype(F32).astype(BF))
    for place in range(13):
        here = (spot == lane // 8 * 256 + place * 8 + lane % 8) & (lane < 32)
        packed += dot_nn(rows[32 * place : 32 * place + 32], here.astype(F32).astype(BF))
    packed = packed.astype(BF)
    keep_ref[...] = jnp.where(place_ref[1] == 0, packed[:16], packed[16:])
    send_ref[...] = jnp.where(place_ref[1] == 0, packed[16:], packed[:16])


def pack_vectors(z, core, rows, head_sums, bias):
    width = bias.shape[1]
    return pl.pallas_call(
        vectors_kernel,
        in_specs=[SCALAR] + [HERE] * (len(rows) + 2),
        out_specs=[HERE] * 2,
        out_shape=[jax.ShapeDtypeStruct((16, width), BF)] * 2,
        compiler_params=pltpu.CompilerParams(vmem_limit_bytes=32 * 1024 * 1024),
        cost_estimate=HINT,
    )(jnp.stack([z, core]), *(row.reshape(1, width) for row in rows), head_sums, bias)


def last_kernel(*refs):
    parts, outs = refs[:RING], refs[RING:]
    total = sum(ref[...].astype(F32) for ref in parts)
    ffn_out, cross_out, ffn_in, cross_query, self_out, cross_kv, gains, shifts, biases, ffn_bias = outs
    width = total.shape[1]
    for at in range(4):
        ffn_out[:, at * width : at * width + width] = total[8 * at : 8 * at + 8]
    cross_out[...] = total[32:40]
    ffn_in[...] = total[40:72]
    cross_query[...] = total[72:80]
    self_out[...] = total[80:88]
    cross_kv[...] = total[88:104]
    line = total[104:112, :256]
    spot = lax.broadcasted_iota(jnp.int32, (24, 256), 1)
    picked = jnp.where(spot // 8 == lax.broadcasted_iota(jnp.int32, (24, 256), 0), line[0:1], 0.0)
    spot = lax.broadcasted_iota(jnp.int32, (256, 128), 0)
    lane = lax.broadcasted_iota(jnp.int32, (256, 128), 1)
    exact = functools.partial(jnp.dot, precision=lax.Precision.HIGHEST, preferred_element_type=F32)
    table = exact(picked, (spot % 8 == lane).astype(F32))
    gains[...] = table[0:3, :8]
    shifts[...] = table[3:6, :8]
    biases[...] = table[6:13, :8]
    ffn_bias[...] = exact(line, (spot == 104 + lane).astype(F32))[0:1, :32]


def last_sums(*parts):
    width = parts[0].shape[1]
    shapes = [(8, 4 * width), (8, width), (32, width), (8, width), (8, width), (16, width)]
    shapes += [(3, 8), (3, 8), (7, 8), (1, 32)]
    return pl.pallas_call(
        last_kernel,
        in_specs=[HERE] * RING,
        out_specs=[HERE] * len(shapes),
        out_shape=[jax.ShapeDtypeStruct(shape, F32) for shape in shapes],
        compiler_params=pltpu.CompilerParams(vmem_limit_bytes=32 * 1024 * 1024),
        cost_estimate=HINT,
    )(*parts)


def sum_kernel(*refs):
    total = refs[0][...].astype(F32)
    for ref in refs[1:-1]:
        total = total + ref[...].astype(F32)
    refs[-1][...] = total.astype(refs[-1].dtype)


def sum_low(*parts):
    return pl.pallas_call(
        sum_kernel,
        in_specs=[HERE] * len(parts),
        out_specs=HERE,
        out_shape=jax.ShapeDtypeStruct(parts[0].shape, BF),
        compiler_params=pltpu.CompilerParams(vmem_limit_bytes=32 * 1024 * 1024),
        cost_estimate=HINT,
    )(*parts)


def column_sums(rows):
    return jnp.sum(rows.astype(F32), axis=0)


def eight_order():
    cols = np.arange(1024).reshape(4, 2, 2, 4, 2, 8)
    return cols.transpose(2, 4, 1, 0, 3, 5).reshape(-1)


def shuffle_matrix(order):
    cols = order.shape[0]
    return (lax.broadcasted_iota(jnp.int32, (cols, cols), 0) == order[None, :]).astype(BF)


def qkv_order():
    order = np.zeros((4, 32, 3, 8), np.int32)
    sends, odd_sends = [], []
    odd_from, odd_to = np.zeros(128, np.int32), np.full(128, -1, np.int32)
    for z in range(4):
        owners = {}
        for group in (third * 128 + z * 32 + k for third in range(3) for k in range(32)):
            owners.setdefault(group // 3, []).append(group)
        by_size = {size: [owner for owner in sorted(owners) if len(owners[owner]) == size] for size in (1, 2, 3)}
        for place, owner in enumerate(by_size[3] + by_size[2]):
            c, x, y = place // 16, place // 4 % 4, place % 4
            source = (((y * 2 + x % 2) * 2 + c) * 4 + z) * 2 + x // 2
            sends.append((source, owner))
            groups = {group % 3: group for group in owners[owner]}
            if len(groups) == 2:
                odd_owner = by_size[1][place - len(by_size[3])]
                (odd,) = owners[odd_owner]
                (odd_from[source],) = {0, 1, 2} - set(groups)
                odd_to[odd_owner] = odd % 3
                odd_sends.append((source, odd_owner))
                groups[int(odd_from[source])] = odd
            for slot, group in groups.items():
                order[z, place, slot] = (group // 128) * 256 + (group % 32) * 8 + np.arange(8)
    return order.reshape(4, 768), sends, odd_sends, odd_from, odd_to


def on_device(
    tokens,
    memory,
    lengths,
    patch_counts,
    self_qkv,
    self_out,
    cross_query,
    cross_kv,
    cross_out,
    ffn_in,
    ffn_out,
    norm_gains,
    norm_shifts,
    proj_biases,
    ffn_bias,
    cotangent,
):
    y, xl, c, z, xh = (lax.axis_index(axis) for axis in AXES)
    x = xh * 2 + xl
    width = tokens.shape[2]
    rows = 2 * tokens.shape[1]
    page_rows = RING * rows
    length = lax.dynamic_index_in_dim(lengths, xh, 0, keepdims=False)
    count = lax.dynamic_slice(patch_counts, (xh,), (1,))
    valid = (z * rows + jnp.arange(rows) < length)[:, None]

    def swap_cores(part):
        return lax.ppermute(part, "c", FLIP)

    by_core = jnp.asarray(eight_order()).reshape(2, 512)
    sides = shuffle_matrix(
        jnp.concatenate([lax.dynamic_index_in_dim(by_core, side, 0, keepdims=False) for side in (c, 1 - c)])
    )

    def own_eights(grads):
        return product(grads, sides).astype(BF)

    def relay(chunks, axis, pairs):
        return lax.ppermute(chunks[3], axis, pairs(1)), lax.ppermute(chunks[4], axis, pairs(3))

    def add_on(chunks, got):
        return relay_add(chunks[1], chunks[2], *got)

    def send_on(sums, axis, pairs):
        return lax.ppermute(sums[0], axis, pairs(1)), lax.ppermute(sums[1], axis, pairs(3))

    def finish(chunks, got):
        return sum_low(chunks[0], *got)

    X_RING, Y_RING = (("xl", "xh"), x_pairs), ("y", ring_pairs)

    def then_y(part):
        part = part.reshape(4, 32, part.shape[1])
        return ring_sum(
            lambda target: lax.dynamic_index_in_dim(part, target, 0, keepdims=False), y, "y", ring_pairs
        ).astype(BF)

    def then_x(part):
        each = part.shape[0] // 16
        part = part.reshape(2, 4, 2, each, part.shape[1])

        def cut(target):
            piece = lax.dynamic_slice(
                part, (target % 2, 0, target // 2, 0, 0), (1, 4, 1, each, part.shape[4])
            )
            return piece.reshape(4 * each, part.shape[4])

        return ring_sum(cut, x, ("xl", "xh"), x_pairs).astype(BF)

    mine = lax.dynamic_index_in_dim(tokens, xh, 0, keepdims=False)
    other = lax.dynamic_index_in_dim(tokens, 1 - xh, 0, keepdims=False)
    other = lax.ppermute(other, "xh", FLIP)
    early_rows = [mine] + [lax.ppermute(mine, "z", ring_pairs(step)) for step in STEPS]
    late_row = after(other, *early_rows)
    late_rows = [late_row] + [lax.ppermute(late_row, "z", ring_pairs(step)) for step in STEPS]
    own_memory = swap_in(after(memory, *early_rows), xh)
    def side_by_side(own, other):
        return jnp.concatenate([jnp.where(xh == 0, own, other), jnp.where(xh == 0, other, own)], axis=0)

    own_tokens = side_by_side(mine, late_row)

    def head_cols(matrix, third):
        return lax.dynamic_slice(matrix, (0, third * width + z * 256), (matrix.shape[0], 256))

    heads_qkv = jnp.concatenate([head_cols(self_qkv, third) for third in range(3)], axis=1)
    bias_q = lax.dynamic_slice(proj_biases, (0, z * 256), (1, 256))
    bias_v = lax.dynamic_slice(proj_biases, (1, z * 256), (1, 256))
    bias_qkv = jnp.concatenate([bias_q, jnp.zeros_like(bias_q), bias_v], axis=1)
    joined, low_one, normal_one = project_heads(
        z, xh, early_rows, late_rows, heads_qkv, bias_qkv, norm_gains[0:1], norm_shifts[0:1]
    )
    heads_mix, self_level = attend(page_rows, page_rows, 2, True, joined, joined, joined, (0, 256, 512))

    memory_here = after(own_memory, *late_rows)
    before_got, behind_got = (lax.ppermute(memory_here, "z", ring_pairs(step)) for step in (1, 3))
    heads_mix, before_got, behind_got = lax.optimization_barrier((heads_mix, before_got, behind_got))
    far_got = (
        lax.ppermute(behind_got[: rows // 2], "z", ring_pairs(3)),
        lax.ppermute(before_got[rows // 2 :], "z", ring_pairs(1)),
    )
    mix_pick = lambda target: lax.dynamic_slice(heads_mix, (target * rows, 0), (rows, 256))
    mix_got = exchange(mix_pick, z, far_got)
    far_got = lax.optimization_barrier((*far_got, *(part for _, part in mix_got[1:])))[:2]
    page_memory = jnp.zeros((page_rows, width), BF)
    for hop, first, part in (
        (0, 0, memory_here),
        (1, 0, behind_got),
        (3, 0, before_got),
        (2, 0, far_got[0]),
        (2, rows // 2, far_got[1]),
    ):
        page_memory = lax.dynamic_update_slice(page_memory, part, (around(hop, z) * rows + first, 0))
    patch_bias = jnp.concatenate([jnp.zeros_like(proj_biases[4]), proj_biases[4]])
    page_kv = (product(page_memory, cross_kv) + patch_bias).astype(BF)

    grad_low = jnp.where(valid, swap_in(after(cotangent, heads_mix), xh), 0)
    mixture = jnp.zeros((rows, width), BF)
    for source, part in mix_got:
        mixture = lax.dynamic_update_slice(mixture, part, (0, source * 256))
    after_self = own_tokens.astype(F32) + product(mixture, self_out) + proj_biases[2]
    normal_two, inverse_two = unit(after_self)
    low_two = (normal_two * norm_gains[1] + norm_shifts[1]).astype(BF)
    cross_queries = (product(low_two, cross_query) + proj_biases[3]).astype(BF)
    cross_mix, cross_level = attend(
        rows, page_rows, 8, False, cross_queries, page_kv, page_kv, (0, 0, 1024), count
    )
    after_cross = after_self + product(cross_mix, cross_out) + proj_biases[5]
    normal_three, inverse_three = unit(after_cross)
    low_three = (normal_three * norm_gains[2] + norm_shifts[2]).astype(BF)
    before = product(low_three, ffn_in) + ffn_bias
    below = 0.5 * (1.0 + lax.erf(before * np.float32(np.sqrt(0.5))))
    hidden = (before * below).astype(BF)
    slope = below + before * jnp.exp(-0.5 * before * before) * np.float32(1 / np.sqrt(2 * np.pi))
    result = after_cross + product(hidden, ffn_out) + proj_biases[6]
    layer_rows = jnp.where(valid, result, 0.0).astype(BF)

    order, sends, odd_sends, odd_from, odd_to = qkv_order()
    head_order = lax.dynamic_index_in_dim(jnp.asarray(order), z, 0, keepdims=False)
    head_shuffle, sides = lax.optimization_barrier((shuffle_matrix(head_order), sides))

    out_grads = own_eights(grad_low)
    early = jnp.concatenate([cross_mix, low_two, mixture, low_three, out_grads[:, 512:]], axis=1)
    early_got = swap_cores(early)
    hidden_got = swap_cores(hidden)
    grad_before = (back_product(grad_low, ffn_out) * slope).astype(BF)
    before_sums = column_sums(grad_before)
    in_keep, in_send = split_wides(c, grad_before)
    in_got = swap_cores(in_send)
    grad_three = back_product(grad_before, ffn_in)
    grad_after_cross = grad_low.astype(F32) + unit_back(
        normal_three, inverse_three, grad_three, norm_gains[2]
    )
    cross_low = grad_after_cross.astype(BF)
    cross_grads = own_eights(cross_low)
    cross_got = swap_cores(cross_grads[:, 512:])
    grad_cross_mix = back_product(cross_low, cross_out).astype(BF)
    ffn_in_chunks = outer_chunks(
        y, 512, 512, [((in_keep, 0), (in_got, 0), (early, 3 * width), (early_got, 3 * width), 2)]
    )
    ffn_out_chunks = outer_chunks(
        x,
        128,
        width,
        [
            ((out_grads, 0), (early_got, 4 * width), (hidden, 0), (hidden_got, 0), 4),
            ((cross_grads, 0), (cross_got, 0), (early, 0), (early_got, 0), 1),
        ],
    )
    ffn_out_got = relay(ffn_out_chunks, *X_RING)
    ffn_in_got = relay(ffn_in_chunks, *Y_RING)

    grad_cross_mix, layer_rows, *got = lax.optimization_barrier(
        (grad_cross_mix, layer_rows, *ffn_out_got, *ffn_in_got)
    )
    ffn_out_sums, ffn_in_sums = add_on(ffn_out_chunks, got[:2]), add_on(ffn_in_chunks, got[2:])
    grad_cross_mix, *sums = lax.optimization_barrier((grad_cross_mix, *ffn_out_sums, *ffn_in_sums))
    ffn_out_got, ffn_in_got = send_on(sums[:2], *X_RING), send_on(sums[2:], *Y_RING)
    cross_query_low, patch_grads = attend_back(
        rows,
        page_rows,
        8,
        False,
        cross_queries,
        page_kv,
        page_kv,
        (0, 0, 1024),
        cross_mix,
        grad_cross_mix,
        cross_level,
        count,
    )
    cross_query_low, patch_grads, layer_rows, *got = lax.optimization_barrier(
        (cross_query_low, patch_grads, layer_rows, *ffn_out_got, *ffn_in_got)
    )
    layer_out = swap_out(layer_rows, xh)
    ffn_out_part, ffn_in_part = finish(ffn_out_chunks, got[:2]), finish(ffn_in_chunks, got[2:])
    grad_two = back_product(cross_query_low, cross_query)
    grad_after_self = grad_after_cross + unit_back(normal_two, inverse_two, grad_two, norm_gains[1])

    self_low = grad_after_self.astype(BF)
    grad_mix_rows = back_product(self_low, self_out).astype(BF)
    grads_here = after(patch_grads, grad_mix_rows)
    kv_send, kv_keep = patch_halves(c, grads_here, page_memory)
    grad_mixture = rows_to_heads(grad_mix_rows, z, (kv_send,))
    grads_here = after(patch_grads, grad_mixture)
    kv_rows = sum_low(kv_keep, swap_cores(kv_send))
    kv_quarters = kv_rows.reshape(RING, 256, width)

    def kv_chunk(hop):
        return lax.dynamic_index_in_dim(kv_quarters, around(hop, y), 0, keepdims=False)

    kv_own, kv_sends = kv_chunk(0), [kv_chunk(step) for step in STEPS]
    out_quarters = ffn_out_part.reshape(RING, 32, 5 * width)
    out_own, *out_sends = (
        lax.dynamic_index_in_dim(out_quarters, around(hop, y), 0, keepdims=False) for hop in (0,) + STEPS
    )
    query_grads, self_grads = own_eights(cross_query_low), own_eights(self_low)
    sent = swap_cores(jnp.concatenate([query_grads[:, 512:], self_grads[:, 512:]], axis=1))
    sent, *out_sends = lax.optimization_barrier((sent, *out_sends))
    out_got = [lax.ppermute(chunk, "y", ring_pairs(step)) for step, chunk in zip(STEPS, out_sends)]
    two_chunks = outer_chunks(
        x,
        128,
        width,
        [
            ((query_grads, 0), (sent, 0), (early, width), (early_got, width), 1),
            ((self_grads, 0), (sent, 512), (early, 2 * width), (early_got, 2 * width), 1),
        ],
        extra=ffn_in_part,
    )
    two_chunks = lax.optimization_barrier((*two_chunks, *out_got))
    two_chunks, out_got = two_chunks[:5], two_chunks[5:]
    grad_mixture, layer_out, *held = lax.optimization_barrier(
        (grad_mixture, layer_out, *kv_sends, *two_chunks)
    )
    kv_sends, two_chunks = held[:3], held[3:]

    two_got = relay(two_chunks, *X_RING)
    kv_got = [lax.ppermute(chunk, "y", ring_pairs(step)) for step, chunk in zip(STEPS, kv_sends)]
    (grad_joined,) = attend_back(
        page_rows, page_rows, 2, True, joined, joined, joined, (0, 256, 512), heads_mix, grad_mixture, self_level
    )
    grad_joined, grads_here, *two_got = lax.optimization_barrier((grad_joined, grads_here, *two_got))
    *page_chunks, page_sums, head_sums = page_back(z, grad_joined, heads_qkv, grads_here, cross_kv, normal_one)
    shuffled = product(grad_joined, head_shuffle).astype(BF)
    shuffled, page_sums, head_sums, *held = lax.optimization_barrier(
        (shuffled, page_sums, head_sums, *page_chunks, *kv_got)
    )
    page_chunks, kv_got = held[:5], held[5:]

    def core_half(target):
        return outer(lax.dynamic_slice(shuffled, (0, target * 384), (page_rows, 384)), low_one)

    core_keep = core_half(c)
    core_send = core_half(1 - c).astype(BF)
    core_keep, core_send, *held = lax.optimization_barrier(
        (core_keep, core_send, *page_chunks, *two_got, *kv_got, *out_got)
    )
    page_chunks, held = held[:5], held[5:]
    two_got, kv_got, out_got = held[:2], held[2:5], held[5:]
    ffn_out_part = sum_low(out_own, *out_got)

    core_got = swap_cores(core_send).astype(F32)
    two_got = send_on(add_on(two_chunks, two_got), *X_RING)

    Z_RING = ("z", ring_pairs)
    page_got = relay(page_chunks, *Z_RING)
    vectors = [
        page_sums[0],
        column_sums(grad_two * normal_two),
        column_sums(grad_three * normal_three),
        page_sums[1],
        column_sums(grad_two),
        column_sums(grad_three),
        column_sums(grad_after_self),
        column_sums(cross_query_low),
        page_sums[2],
        column_sums(grad_after_cross),
        column_sums(grad_low),
    ]
    small_keep, small_send = pack_vectors(z, c, vectors, head_sums, before_sums.reshape(4, width))
    small_sum = (small_keep.astype(F32) + swap_cores(small_send).astype(F32)).astype(BF)
    core_sum = (core_keep + core_got).astype(BF)
    kv_part = sum_low(kv_own, *kv_got)
    core_sum, small_sum, kv_part, *held = lax.optimization_barrier(
        (core_sum, small_sum, kv_part, *two_got, *page_got)
    )
    two_got, page_got = held[:2], held[2:]

    page_got = send_on(add_on(page_chunks, page_got), *Z_RING)
    small_sum = jnp.pad(small_sum.reshape(4, 4, 1, width), ((0, 0), (0, 0), (0, 7), (0, 0)))
    core_sum = jnp.concatenate([core_sum.reshape(4, 4, 24, width), small_sum], axis=2)
    kv_lines = kv_part.reshape(2, 4, 2, 16, width)

    def x_chunk(target):
        piece = lax.dynamic_slice(kv_lines, (target % 2, 0, target // 2, 0, 0), (1, 4, 1, 16, width))
        lines = lax.dynamic_index_in_dim(core_sum, target, 0, keepdims=False)
        return jnp.concatenate([lines.reshape(128, width), piece.reshape(64, width)], axis=0)

    x_sum = ring_sum(x_chunk, x, ("xl", "xh"), x_pairs).astype(BF)
    two_part = finish(two_chunks, two_got)
    x_sum, two_part, mine, late_row, *page_got = lax.optimization_barrier(
        (x_sum, two_part, mine, late_row, *page_got)
    )
    own_tokens = side_by_side(mine, late_row)

    two_part, ffn_in_part = two_part[:, : 2 * width].reshape(4, 32, 2 * width), two_part[:, 2 * width :]
    cross_kv_part = x_sum[128:]
    y_lines = jnp.concatenate([x_sum[:128].reshape(4, 32, width), two_part], axis=2)
    y_sum = ring_sum(
        lambda target: lax.dynamic_index_in_dim(y_lines, target, 0, keepdims=False), y, "y", ring_pairs
    )
    grad_own, memory_rows = (
        sum(part[:, at : at + width].astype(F32) for part in (page_chunks[0], *page_got)) for at in (0, width)
    )
    own_normal, own_inverse = unit(own_tokens.astype(F32))
    token_rows = grad_after_self + unit_back(own_normal, own_inverse, grad_own, norm_gains[0])
    both_grads = swap_out(jnp.concatenate([token_rows, memory_rows], axis=1).astype(BF), xh)
    token_grad, memory_grad = both_grads[..., :width], both_grads[..., width:]

    two_part, y_sum = y_sum[:, width:].astype(BF), y_sum[:, :width]
    small_part = jnp.pad(y_sum[24].astype(BF).reshape(4, 1, 256), ((0, 0), (0, 7), (0, 768)))
    me = (((y * 2 + xl) * 2 + c) * 4 + z) * 2 + xh
    odd_at = lax.dynamic_index_in_dim(jnp.asarray(odd_from), me, 0, keepdims=False) * 8
    odd_got = lax.ppermute(lax.dynamic_slice(y_sum, (odd_at, 0), (8, width)), AXES, odd_sends)
    odd_here = jnp.arange(24) // 8 == lax.dynamic_index_in_dim(jnp.asarray(odd_to), me, 0, keepdims=False)
    grad_qkv = lax.ppermute(y_sum[:24], AXES, sends)
    grad_qkv = jnp.where(odd_here[:, None], jnp.concatenate([odd_got] * 3, axis=0), grad_qkv)

    lines = []
    for part in (ffn_out_part, ffn_in_part, two_part, cross_kv_part, small_part):
        part = part.reshape(4, -1, part.shape[-1])
        lines += [part[..., at : at + width] for at in range(0, part.shape[-1], width)]
    lines = jnp.concatenate(lines, axis=1)
    z_line = lambda hop: lax.dynamic_index_in_dim(lines, around(hop, z), 0, keepdims=False)
    z_got = [lax.ppermute(z_line(step), "z", ring_pairs(step)) for step in STEPS]
    ffn_out_rows, cross_out_rows, ffn_in_rows, cross_query_rows, self_out_rows, cross_kv_rows, *small = last_sums(
        z_line(0), *z_got
    )

    return (
        layer_out,
        token_grad,
        memory_grad,
        grad_qkv.T,
        self_out_rows.T,
        cross_query_rows.T,
        cross_kv_rows.T,
        cross_out_rows.T,
        ffn_in_rows.T,
        ffn_out_rows.T,
        *small[:3],
        small[3].reshape(-1),
    )


def solution(mesh):
    split = jax.sharding.Mesh(mesh.devices.reshape(MESH_SHAPE), AXES)
    page, blk = AXES[:3], AXES[3:]
    blocks, cols = P(page, blk, None), P(None, AXES)
    in_specs = (blocks, blocks, P(page), P(page)) + (P(),) * 11 + (blocks,)
    out_specs = (blocks,) * 3 + (cols,) * 10 + (P(AXES),)
    return jax.shard_map(
        on_device, mesh=split, in_specs=in_specs, out_specs=out_specs, check_vma=False
    )
```

```python
import functools

import jax
import jax.numpy as jnp
import numpy as np
from jax import lax
from jax.experimental import pallas as pl
from jax.experimental.pallas import tpu as pltpu
from jax.sharding import PartitionSpec as P

EPS = 1e-05

BF = jnp.bfloat16
F32 = jnp.float32
NEG = -1e30
TILE = 256
PAIR = 128
HINT = pl.CostEstimate(flops=1 << 20, bytes_accessed=1 << 16, transcendentals=0)


def dot_tt(a, b):
    return lax.dot_general(a, b, (((1,), (1,)), ((), ())), preferred_element_type=F32)


def dot_nn(a, b):
    return lax.dot_general(a, b, (((1,), (0,)), ((), ())), preferred_element_type=F32)


def two_heads(rows):
    lanes = lax.broadcasted_iota(jnp.int32, rows.shape, 1)
    none = jnp.zeros_like(rows)
    return jnp.concatenate([jnp.where(lanes < 64, rows, none), jnp.where(lanes < 64, none, rows)], axis=0)


def later_key():
    keys = lax.broadcasted_iota(jnp.int32, (TILE, 2 * TILE), 0)
    return keys > lax.broadcasted_iota(jnp.int32, (TILE, 2 * TILE), 1) % TILE


def own_halves(both):
    return jnp.concatenate([both[:64, :TILE], both[64:, TILE:]], axis=0).T


def span(tile):
    return pl.ds(tile * TILE, TILE)


def forward_tiles(key_tiles, causal, q_ref, k_ref, o_ref, lse_ref, vt_ref, s_ref):
    for i in range(q_ref.shape[0] // TILE):
        tiles = i + 1 if causal else key_tiles
        queries = two_heads(q_ref[span(i), :] * 0.125)
        kept = s_ref.at[i % 2]
        top = None
        for j in range(tiles):
            scores = dot_tt(k_ref[span(j), :], queries)
            if causal and j == i:
                scores = jnp.where(later_key(), NEG, scores)
            kept[span(j), :] = scores
            tile_top = jnp.max(scores, axis=0, keepdims=True)
            top = tile_top if top is None else jnp.maximum(top, tile_top)
        total, mixed = None, None
        for j in range(tiles):
            shares = jnp.exp(kept[span(j), :] - top)
            tile_sum = jnp.sum(shares, axis=0, keepdims=True)
            tile_mix = dot_nn(vt_ref[:, span(j)], shares.astype(BF))
            total = tile_sum if total is None else total + tile_sum
            mixed = tile_mix if mixed is None else mixed + tile_mix
        level = top + jnp.log(total)
        lse_ref[0, 0:1, span(i)] = level[:, :TILE]
        lse_ref[0, 1:2, span(i)] = level[:, TILE:]
        o_ref[span(i), :] = own_halves(mixed / total).astype(o_ref.dtype)


def pair_columns(pair, first=0):
    return pl.ds(pl.multiple_of(pair * PAIR + first, PAIR), PAIR)


def every_pair(pairs, count_ref, tiles, run):
    def loop(live):
        @pl.loop(0, pairs // 2)
        def _(couple):
            run(2 * couple, 0, live)
            run(2 * couple + 1, 1, live)

    if count_ref is None:
        loop(tiles)
    else:
        pl.when(count_ref[0] > TILE)(lambda: loop(tiles))
        pl.when(count_ref[0] <= TILE)(lambda: loop(1))


def forward_kernel(pairs, causal, firsts, *refs):
    count_ref = None if causal else refs[0]
    refs = refs if causal else refs[1:]
    q_ref, k_ref, v_ref, o_ref, lse_ref, vt_ref, s_ref = refs

    def run(pair, slot, tiles):
        q, k, v = (ref.at[:, pair_columns(pair, at)] for ref, at in zip((q_ref, k_ref, v_ref), firsts))
        vt, kept = vt_ref.at[slot], s_ref.at[slot]
        vt[:, : tiles * TILE] = v[: tiles * TILE, :].T
        out, level = o_ref.at[:, pair_columns(pair)], lse_ref.at[pl.ds(pair, 1)]
        forward_tiles(tiles, causal, q, k, out, level, vt, kept)

    every_pair(pairs, count_ref, k_ref.shape[0] // TILE, run)


def backward_tiles(
    key_tiles, causal, q_ref, k_ref, v_ref, o_ref, do_ref, lse_ref, dq_ref, kt_ref, dk_ref, dv_ref
):
    ones = jnp.ones((8, PAIR), F32)
    for i in range(q_ref.shape[0] // TILE):
        tiles = i + 1 if causal else key_tiles
        queries = two_heads(q_ref[span(i), :] * 0.125)
        pulled = two_heads(do_ref[span(i), :])
        out = o_ref[span(i), :].astype(F32)
        weighed = pulled.astype(F32) * jnp.concatenate([out, out], axis=0)
        dots = lax.dot_general(
            ones,
            weighed,
            (((1,), (1,)), ((), ())),
            preferred_element_type=F32,
            precision=lax.Precision.HIGHEST,
        )[0:1, :]
        level = jnp.concatenate([lse_ref[0, 0:1, span(i)], lse_ref[0, 1:2, span(i)]], axis=1)
        drawn = None
        for j in range(tiles):
            shares = jnp.exp(dot_tt(k_ref[span(j), :], queries) - level)
            if causal and j == i:
                shares = jnp.where(later_key(), 0.0, shares)
            grad_shares = dot_tt(v_ref[span(j), :], pulled)
            grad_scores = (shares * (grad_shares - dots)).astype(BF)
            dv_part = dot_nn(shares.astype(BF), pulled)
            dk_part = dot_nn(grad_scores, queries)
            if i == (j if causal else 0):
                dv_ref[span(j), :] = dv_part
                dk_ref[span(j), :] = dk_part
            else:
                dv_ref[span(j), :] += dv_part
                dk_ref[span(j), :] += dk_part
            tile_drawn = dot_nn(kt_ref[:, span(j)], grad_scores)
            drawn = tile_drawn if drawn is None else drawn + tile_drawn
        dq_ref[span(i), :] = (own_halves(drawn) * 0.125).astype(dq_ref.dtype)


def backward_kernel(pairs, causal, firsts, *refs):
    count_ref = None if causal else refs[0]
    refs = refs if causal else refs[1:]
    q_ref, k_ref, v_ref, o_ref, do_ref, lse_ref, *outs, kt_ref, dk_ref, dv_ref = refs
    dq_ref, dkv_ref = outs[0], outs[-1]
    width = pairs * PAIR
    first = dkv_ref.shape[1] - 2 * width

    def run(pair, slot, tiles):
        q, k, v = (ref.at[:, pair_columns(pair, at)] for ref, at in zip((q_ref, k_ref, v_ref), firsts))
        cols, live = pair_columns(pair), tiles * TILE
        kt, dk, dv = kt_ref.at[slot], dk_ref.at[slot], dv_ref.at[slot]
        kt[:, :live] = k[:live, :].T
        if live < k.shape[0]:
            dk[...] = jnp.zeros_like(dk)
            dv[...] = jnp.zeros_like(dv)
        out, grads, level = o_ref.at[:, cols], do_ref.at[:, cols], lse_ref.at[pl.ds(pair, 1)]
        backward_tiles(
            tiles, causal, q, k, v, out, grads, level, dq_ref.at[:, cols], kt, dk, dv
        )
        dkv_ref[:, pair_columns(pair, first)] = dk[...].astype(BF)
        dkv_ref[:, pair_columns(pair, first + width)] = dv[...].astype(BF)

    every_pair(pairs, count_ref, k_ref.shape[0] // TILE, run)


SCALAR = pl.BlockSpec(memory_space=pltpu.SMEM)
HERE = pl.BlockSpec(memory_space=pltpu.VMEM)


def attend(q_rows, key_rows, pairs, causal, q, k, v, firsts, count=None):
    return pl.pallas_call(
        functools.partial(forward_kernel, pairs, causal, firsts),
        in_specs=([] if causal else [SCALAR]) + [HERE] * 3,
        out_specs=[HERE] * 2,
        out_shape=[
            jax.ShapeDtypeStruct((q_rows, pairs * PAIR), BF),
            jax.ShapeDtypeStruct((pairs, 2, q_rows), F32),
        ],
        scratch_shapes=[pltpu.VMEM((2, PAIR, key_rows), BF), pltpu.VMEM((2, 2, key_rows, 2 * TILE), F32)],
        compiler_params=pltpu.CompilerParams(vmem_limit_bytes=32 * 1024 * 1024),
        cost_estimate=HINT,
    )(*(() if causal else (count,)), q, k, v)


def attend_back(q_rows, key_rows, pairs, causal, q, k, v, firsts, o, do, lse, count=None):
    width = pairs * PAIR
    shapes = [jax.ShapeDtypeStruct((q_rows, width), BF), jax.ShapeDtypeStruct((key_rows, 2 * width), BF)]
    if causal:
        shapes = [jax.ShapeDtypeStruct((q_rows, 3 * width), BF)]
    return pl.pallas_call(
        functools.partial(backward_kernel, pairs, causal, firsts),
        in_specs=([] if causal else [SCALAR]) + [HERE] * 6,
        out_specs=[HERE] * len(shapes),
        out_shape=shapes,
        scratch_shapes=[
            pltpu.VMEM((2, PAIR, key_rows), BF),
            pltpu.VMEM((2, key_rows, PAIR), F32),
            pltpu.VMEM((2, key_rows, PAIR), F32),
        ],
        compiler_params=pltpu.CompilerParams(vmem_limit_bytes=32 * 1024 * 1024),
        cost_estimate=HINT,
    )(*(() if causal else (count,)), q, k, v, o, do, lse)

AXES = ("y", "xl", "c", "z", "xh")
MESH_SHAPE = (4, 2, 2, 4, 2)
RING = 4


def ring_pairs(step):
    return [(i, (i + step) % RING) for i in range(RING)]


def x_slot(x):
    return (x % 2) * 2 + x // 2


def x_pairs(step):
    return [(x_slot(x), x_slot((x + step) % RING)) for x in range(RING)]


FLIP = [(0, 1), (1, 0)]
STEPS = (1, 3, 2)


def around(step, coord):
    return lax.rem(coord + step, RING)


def swap_in(blocks, side):
    own = lax.dynamic_index_in_dim(blocks, side, 0, keepdims=False)
    got = lax.ppermute(lax.dynamic_index_in_dim(blocks, 1 - side, 0, keepdims=False), "xh", FLIP)
    return jnp.concatenate([jnp.where(side == 0, own, got), jnp.where(side == 0, got, own)], axis=0)


def swap_out(rows, side):
    blocks = rows.reshape(2, rows.shape[0] // 2, rows.shape[1])
    own = lax.dynamic_index_in_dim(blocks, side, 0, keepdims=False)
    got = lax.ppermute(lax.dynamic_index_in_dim(blocks, 1 - side, 0, keepdims=False), "xh", FLIP)
    return jnp.stack([jnp.where(side == 0, own, got), jnp.where(side == 0, got, own)])


def exchange(pick, z, behind=()):
    got = [lax.ppermute(pick(around(step, z)), "z", ring_pairs(step)) for step in STEPS]
    got = lax.optimization_barrier((*got, *behind))[: len(STEPS)]
    return [(z, pick(z))] + [(around(RING - step, z), part) for step, part in zip(STEPS, got)]


def rows_to_heads(rows, z, behind=()):
    height, width = rows.shape[0], rows.shape[1] // RING
    full = jnp.zeros((RING * height, width), rows.dtype)
    pick = lambda target: lax.dynamic_slice(rows, (0, target * width), (height, width))
    for source, part in exchange(pick, z, behind):
        full = lax.dynamic_update_slice(full, part, (source * height, 0))
    return full


def ring_sum(pick, coord, axis, pairs):
    total = pick(coord).astype(F32)
    for step in STEPS:
        got = lax.ppermute(pick(around(step, coord)).astype(BF), axis, pairs(step))
        total = total + got.astype(F32)
    return total


def after(value, *others):
    return lax.optimization_barrier((value, *others))[0]


def product(left, right):
    return jnp.dot(left, right, preferred_element_type=F32)


def back_product(grads, matrix):
    return lax.dot_general(grads, matrix, (((1,), (1,)), ((), ())), preferred_element_type=F32)


def outer(grads, inputs):
    return lax.dot_general(grads, inputs, (((0,), (0,)), ((), ())), preferred_element_type=F32)


def unit(rows):
    centred = rows - jnp.mean(rows, axis=-1, keepdims=True)
    inverse = lax.rsqrt(jnp.mean(centred * centred, axis=-1, keepdims=True) + EPS)
    return centred * inverse, inverse


def unit_back(normal, inverse, grads, gain):
    scaled = grads * gain
    mean = jnp.mean(scaled, axis=-1, keepdims=True)
    along = jnp.mean(scaled * normal, axis=-1, keepdims=True)
    return inverse * (scaled - mean - normal * along)


def chunks_kernel(width, block, segments, coord_ref, *refs):
    outs, turned_ref = refs[-6:-1], refs[-1]
    own_ref, plus_ref, minus_ref, far_a_ref, far_b_ref = outs
    tokens = refs[0].shape[0]
    half, each = width // 2, width // 4
    lane = 0

    def put(pick, lanes):
        own_ref[:, lanes] = pick(0, 0, width).astype(F32)
        plus_ref[:, lanes] = pick(1, 0, width).astype(BF)
        minus_ref[:, lanes] = pick(3, 0, width).astype(BF)
        far_a_ref[:, lanes] = pick(2, 0, half).astype(BF)
        far_b_ref[:, lanes] = pick(2, half, half).astype(BF)

    for at, (grads_at, got_grads_at, inputs_at, got_inputs_at, blocks) in enumerate(segments):
        grads_ref, got_grads_ref, inputs_ref, got_inputs_ref = refs[4 * at : 4 * at + 4]
        for hop in range(RING):
            column = around(hop, coord_ref[0]) * width
            rows = slice(hop * width, hop * width + width)
            turned_ref[at, rows, :tokens] = grads_ref[:, pl.ds(pl.multiple_of(grads_at + column, 128), width)].T
            turned_ref[at, rows, tokens:] = got_grads_ref[
                :, pl.ds(pl.multiple_of(got_grads_at + column, 128), width)
            ].T
        for number in range(blocks):
            mine = inputs_ref[:, inputs_at + number * block : inputs_at + number * block + block]
            got = got_inputs_ref[:, got_inputs_at + number * block : got_inputs_at + number * block + block]

            def pick(hop, first, rows, at=at, mine=mine, got=got):
                turned = turned_ref.at[at, hop * width + first : hop * width + first + rows, :]
                return dot_nn(turned[:, :tokens], mine) + dot_nn(turned[:, tokens:], got)

            put(pick, slice(lane, lane + block))
            lane += block

    if lane < own_ref.shape[1]:
        extra_ref = refs[4 * len(segments)]

        def pick(hop, first, rows):
            target = around(hop, coord_ref[0])
            zs = range(first // each, (first + rows) // each)
            return jnp.concatenate([extra_ref[target % 2, zz, target // 2] for zz in zs], axis=0)

        put(pick, slice(lane, own_ref.shape[1]))


def outer_chunks(coord, width, block, segments, extra=None):
    cols = RING * width
    tokens = segments[0][0][0].shape[0]
    operands = [array for segment in segments for array, _ in segment[:4]]
    places = tuple(tuple(first for _, first in segment[:4]) + (segment[4],) for segment in segments)
    lanes = sum(segment[4] for segment in segments) * block
    if extra is not None:
        operands.append(extra.reshape(2, 4, 2, width // 4, extra.shape[1]))
        lanes += extra.shape[1]
    shape = lambda rows, dtype: jax.ShapeDtypeStruct((rows, lanes), dtype)
    return pl.pallas_call(
        functools.partial(chunks_kernel, width, block, places),
        in_specs=[SCALAR] + [HERE] * len(operands),
        out_specs=[HERE] * 5,
        out_shape=[shape(width, F32), shape(width, BF), shape(width, BF)] + [shape(width // 2, BF)] * 2,
        scratch_shapes=[pltpu.VMEM((len(segments), cols, 2 * tokens), BF)],
        compiler_params=pltpu.CompilerParams(vmem_limit_bytes=40 * 1024 * 1024),
        cost_estimate=HINT,
    )(coord.reshape(1), *operands)


def project_kernel(place_ref, *refs):
    early, late = refs[:RING], refs[RING : 2 * RING]
    matrix_ref, bias_ref, gain_ref, shift_ref, joined_ref, low_ref, normal_ref = refs[2 * RING :]

    def run(at):
        first = jnp.where(place_ref[1] == 0, early[at][...], late[at][...])
        second = jnp.where(place_ref[1] == 0, late[at][...], early[at][...])
        normal, _ = unit(jnp.concatenate([first, second], axis=0).astype(F32))
        low = (normal * gain_ref[...] + shift_ref[...]).astype(BF)
        low_ref[...] = low
        normal_ref[...] = normal.astype(BF)
        joined_ref[...] = (dot_nn(low, matrix_ref[...]) + bias_ref[...]).astype(BF)

    for at in range(RING):
        pl.when(pl.program_id(0) == at)(functools.partial(run, at))


def project_heads(z, side, early, late, matrix, bias, gain, shift):
    half, width = early[0].shape
    rows = 2 * half

    def row_block(j, place):
        hop = jnp.where(j == 0, 0, jnp.where(j == 1, STEPS[0], jnp.where(j == 2, STEPS[1], STEPS[2])))
        return (lax.rem(place[0] + RING - hop, RING), 0)

    whole = lambda shape: pl.BlockSpec(shape, lambda j, place: (0, 0))
    return pl.pallas_call(
        project_kernel,
        grid_spec=pltpu.PrefetchScalarGridSpec(
            num_scalar_prefetch=1,
            grid=(RING,),
            in_specs=[whole((half, width))] * 8
            + [whole((width, 768)), whole((1, 768)), whole((1, width)), whole((1, width))],
            out_specs=[
                pl.BlockSpec((rows, 768), row_block),
                pl.BlockSpec((rows, width), row_block),
                pl.BlockSpec((rows, width), row_block),
            ],
        ),
        out_shape=[
            jax.ShapeDtypeStruct((RING * rows, 768), BF),
            jax.ShapeDtypeStruct((RING * rows, width), BF),
            jax.ShapeDtypeStruct((RING * rows, width), BF),
        ],
        compiler_params=pltpu.CompilerParams(vmem_limit_bytes=40 * 1024 * 1024),
        cost_estimate=HINT,
    )(jnp.stack([z, side]), *early, *late, matrix, bias, gain, shift)


def split_kernel(core_ref, grads_ref, keep_ref, send_ref):
    for at in range(grads_ref.shape[1] // 512):
        first = grads_ref[:, 512 * at : 512 * at + 256]
        second = grads_ref[:, 512 * at + 256 : 512 * at + 512]
        keep_ref[:, 256 * at : 256 * at + 256] = jnp.where(core_ref[0] == 0, first, second)
        send_ref[:, 256 * at : 256 * at + 256] = jnp.where(core_ref[0] == 0, second, first)


def split_wides(core, grads):
    rows, cols = grads.shape
    put = pl.BlockSpec((rows // 2, cols // 2), lambda j: (j, 0))
    return pl.pallas_call(
        split_kernel,
        grid=(2,),
        in_specs=[SCALAR, pl.BlockSpec((rows // 2, cols), lambda j: (j, 0))],
        out_specs=[put, put],
        out_shape=[jax.ShapeDtypeStruct((rows, cols // 2), BF)] * 2,
        compiler_params=pltpu.CompilerParams(vmem_limit_bytes=32 * 1024 * 1024),
        cost_estimate=HINT,
    )(core.reshape(1), grads)


def patch_halves_kernel(side_ref, grads_ref, inputs_ref, send_ref, keep_ref):
    for out_ref, side in ((send_ref, 1 - side_ref[0]), (keep_ref, side_ref[0])):
        for group in range(8):
            column = pl.multiple_of((group * 2 + side) * 128, 128)
            part = outer(grads_ref[:, pl.ds(column, 128)], inputs_ref[...])
            out_ref[group * 128 : group * 128 + 128, :] = part.astype(BF)


def patch_halves(side, grads, inputs):
    patches, width = inputs.shape
    return pl.pallas_call(
        patch_halves_kernel,
        in_specs=[SCALAR, HERE, HERE],
        out_specs=[HERE, HERE],
        out_shape=[jax.ShapeDtypeStruct((1024, width), BF)] * 2,
        compiler_params=pltpu.CompilerParams(vmem_limit_bytes=32 * 1024 * 1024),
        cost_estimate=HINT,
    )(side.reshape(1), grads, inputs)


def page_kernel(place_ref, joined_ref, heads_ref, patch_ref, cross_ref, normal_ref, *refs):
    own_ref, plus_ref, minus_ref, far_a_ref, far_b_ref, sums_ref, head_sums_ref = refs
    rows, width = own_ref.shape[0], cross_ref.shape[0]
    half = rows // 2
    sums, head_sums = [0.0, 0.0, 0.0], 0.0
    for hop in range(RING):
        here = pl.ds(pl.multiple_of(around(hop, place_ref[0]) * rows, rows), rows)
        one = dot_tt(joined_ref[here, :], heads_ref[...])
        sums[0] += jnp.sum(one * normal_ref[here, :].astype(F32), axis=0, keepdims=True)
        sums[1] += jnp.sum(one, axis=0, keepdims=True)
        sums[2] += jnp.sum(patch_ref[here, width:].astype(F32), axis=0, keepdims=True)
        head_sums += jnp.sum(joined_ref[here, :].astype(F32), axis=0, keepdims=True)
        two = dot_tt(patch_ref[here, :], cross_ref[...])
        for part, lanes in ((one, slice(0, width)), (two, slice(width, 2 * width))):
            if hop == 2:
                far_a_ref[:, lanes] = part[:half].astype(BF)
                far_b_ref[:, lanes] = part[half:].astype(BF)
            else:
                out_ref = {0: own_ref, 1: plus_ref, 3: minus_ref}[hop]
                out_ref[:, lanes] = part.astype(out_ref.dtype)
    sums_ref[...] = jnp.concatenate(sums, axis=0)
    head_sums_ref[...] = head_sums


def page_back(z, joined, heads, patch_grads, cross_kv, normal):
    page_rows, width = normal.shape
    rows = page_rows // RING
    chunk = lambda height, dtype: jax.ShapeDtypeStruct((height, 2 * width), dtype)
    return pl.pallas_call(
        page_kernel,
        in_specs=[SCALAR] + [HERE] * 5,
        out_specs=[HERE] * 7,
        out_shape=[
            chunk(rows, F32),
            chunk(rows, BF),
            chunk(rows, BF),
            chunk(rows // 2, BF),
            chunk(rows // 2, BF),
            jax.ShapeDtypeStruct((3, width), F32),
            jax.ShapeDtypeStruct((1, joined.shape[1]), F32),
        ],
        compiler_params=pltpu.CompilerParams(vmem_limit_bytes=40 * 1024 * 1024),
        cost_estimate=HINT,
    )(z.reshape(1), joined, heads, patch_grads, cross_kv, normal)


def relay_add_kernel(plus_ref, minus_ref, got_a_ref, got_b_ref, plus_out_ref, minus_out_ref):
    half = got_a_ref.shape[0]
    plus_out_ref[:half] = (plus_ref[:half].astype(F32) + got_a_ref[...].astype(F32)).astype(BF)
    plus_out_ref[half:] = plus_ref[half:]
    minus_out_ref[:half] = minus_ref[:half]
    minus_out_ref[half:] = (minus_ref[half:].astype(F32) + got_b_ref[...].astype(F32)).astype(BF)


def relay_add(plus, minus, got_a, got_b):
    return pl.pallas_call(
        relay_add_kernel,
        in_specs=[HERE] * 4,
        out_specs=[HERE] * 2,
        out_shape=[jax.ShapeDtypeStruct(plus.shape, BF)] * 2,
        compiler_params=pltpu.CompilerParams(vmem_limit_bytes=32 * 1024 * 1024),
        cost_estimate=HINT,
    )(plus, minus, got_a, got_b)


def vectors_kernel(place_ref, *refs):
    *row_refs, heads_ref, bias_ref, keep_ref, send_ref = refs
    width = bias_ref.shape[1]
    quarter = width // 4
    at_heads = lax.broadcasted_iota(jnp.int32, (1, width), 1) // quarter == place_ref[0]
    own = [ref[...] for ref in row_refs]
    for place, first in ((6, 0), (7, 2 * quarter)):
        part = heads_ref[:, first : first + quarter]
        own.insert(place, jnp.where(at_heads, jnp.concatenate([part] * 4, axis=1), 0.0))
    group = lax.broadcasted_iota(jnp.int32, (32, width), 0)
    col = lax.broadcasted_iota(jnp.int32, (32, width), 1)

    def of_group(owner, y):
        return group == owner // 8 % 2 * 16 + (owner % 2 * 2 + owner // 16 % 2) * 4 + y

    eights = of_group(col // 8, col // 256)
    picked = [jnp.where(eights, row.astype(BF).astype(F32), 0.0).astype(BF) for row in own]
    for y in range(4):
        bias = bias_ref[y : y + 1, :].astype(BF).astype(F32)
        picked.append(jnp.where(of_group(col // 32, y), bias, 0.0).astype(BF))
    col = lax.broadcasted_iota(jnp.int32, (width, 128), 0)
    lane = lax.broadcasted_iota(jnp.int32, (width, 128), 1)
    narrow = (lane == col // 16 % 4 * 8 + col % 8).astype(F32).astype(BF)
    wide = (lane == col // 64 % 4 * 32 + col % 32).astype(F32).astype(BF)
    rows = dot_nn(jnp.concatenate(picked[:13], axis=0), narrow).astype(BF)
    bias = dot_nn(jnp.concatenate(picked[13:], axis=0), wide).astype(BF)
    bias = bias[:32] + bias[32:64] + bias[64:96] + bias[96:]
    lane = lax.broadcasted_iota(jnp.int32, (128, width), 0)
    spot = lax.broadcasted_iota(jnp.int32, (128, width), 1)
    packed = dot_nn(bias, (spot == lane // 32 * 256 + 104 + lane % 32).astype(F32).astype(BF))
    for place in range(13):
        here = (spot == lane // 8 * 256 + place * 8 + lane % 8) & (lane < 32)
        packed += dot_nn(rows[32 * place : 32 * place + 32], here.astype(F32).astype(BF))
    packed = packed.astype(BF)
    keep_ref[...] = jnp.where(place_ref[1] == 0, packed[:16], packed[16:])
    send_ref[...] = jnp.where(place_ref[1] == 0, packed[16:], packed[:16])


def pack_vectors(z, core, rows, head_sums, bias):
    width = bias.shape[1]
    return pl.pallas_call(
        vectors_kernel,
        in_specs=[SCALAR] + [HERE] * (len(rows) + 2),
        out_specs=[HERE] * 2,
        out_shape=[jax.ShapeDtypeStruct((16, width), BF)] * 2,
        compiler_params=pltpu.CompilerParams(vmem_limit_bytes=32 * 1024 * 1024),
        cost_estimate=HINT,
    )(jnp.stack([z, core]), *(row.reshape(1, width) for row in rows), head_sums, bias)


def last_kernel(*refs):
    parts, outs = refs[:RING], refs[RING:]
    total = sum(ref[...].astype(F32) for ref in parts)
    ffn_out, cross_out, ffn_in, cross_query, self_out, cross_kv, gains, shifts, biases, ffn_bias = outs
    width = total.shape[1]
    for at in range(4):
        ffn_out[:, at * width : at * width + width] = total[8 * at : 8 * at + 8]
    cross_out[...] = total[32:40]
    ffn_in[...] = total[40:72]
    cross_query[...] = total[72:80]
    self_out[...] = total[80:88]
    cross_kv[...] = total[88:104]
    line = total[104:112, :256]
    spot = lax.broadcasted_iota(jnp.int32, (24, 256), 1)
    picked = jnp.where(spot // 8 == lax.broadcasted_iota(jnp.int32, (24, 256), 0), line[0:1], 0.0)
    spot = lax.broadcasted_iota(jnp.int32, (256, 128), 0)
    lane = lax.broadcasted_iota(jnp.int32, (256, 128), 1)
    exact = functools.partial(jnp.dot, precision=lax.Precision.HIGHEST, preferred_element_type=F32)
    table = exact(picked, (spot % 8 == lane).astype(F32))
    gains[...] = table[0:3, :8]
    shifts[...] = table[3:6, :8]
    biases[...] = table[6:13, :8]
    ffn_bias[...] = exact(line, (spot == 104 + lane).astype(F32))[0:1, :32]


def last_sums(*parts):
    width = parts[0].shape[1]
    shapes = [(8, 4 * width), (8, width), (32, width), (8, width), (8, width), (16, width)]
    shapes += [(3, 8), (3, 8), (7, 8), (1, 32)]
    return pl.pallas_call(
        last_kernel,
        in_specs=[HERE] * RING,
        out_specs=[HERE] * len(shapes),
        out_shape=[jax.ShapeDtypeStruct(shape, F32) for shape in shapes],
        compiler_params=pltpu.CompilerParams(vmem_limit_bytes=32 * 1024 * 1024),
        cost_estimate=HINT,
    )(*parts)


def sum_kernel(*refs):
    total = refs[0][...].astype(F32)
    for ref in refs[1:-1]:
        total = total + ref[...].astype(F32)
    refs[-1][...] = total.astype(refs[-1].dtype)


def sum_low(*parts):
    return pl.pallas_call(
        sum_kernel,
        in_specs=[HERE] * len(parts),
        out_specs=HERE,
        out_shape=jax.ShapeDtypeStruct(parts[0].shape, BF),
        compiler_params=pltpu.CompilerParams(vmem_limit_bytes=32 * 1024 * 1024),
        cost_estimate=HINT,
    )(*parts)


def column_sums(rows):
    return jnp.sum(rows.astype(F32), axis=0)


def eight_order():
    cols = np.arange(1024).reshape(4, 2, 2, 4, 2, 8)
    return cols.transpose(2, 4, 1, 0, 3, 5).reshape(-1)


def shuffle_matrix(order):
    cols = order.shape[0]
    return (lax.broadcasted_iota(jnp.int32, (cols, cols), 0) == order[None, :]).astype(BF)


def qkv_order():
    order = np.zeros((4, 32, 3, 8), np.int32)
    sends, odd_sends = [], []
    odd_from, odd_to = np.zeros(128, np.int32), np.full(128, -1, np.int32)
    for z in range(4):
        owners = {}
        for group in (third * 128 + z * 32 + k for third in range(3) for k in range(32)):
            owners.setdefault(group // 3, []).append(group)
        by_size = {size: [owner for owner in sorted(owners) if len(owners[owner]) == size] for size in (1, 2, 3)}
        for place, owner in enumerate(by_size[3] + by_size[2]):
            c, x, y = place // 16, place // 4 % 4, place % 4
            source = (((y * 2 + x % 2) * 2 + c) * 4 + z) * 2 + x // 2
            sends.append((source, owner))
            groups = {group % 3: group for group in owners[owner]}
            if len(groups) == 2:
                odd_owner = by_size[1][place - len(by_size[3])]
                (odd,) = owners[odd_owner]
                (odd_from[source],) = {0, 1, 2} - set(groups)
                odd_to[odd_owner] = odd % 3
                odd_sends.append((source, odd_owner))
                groups[int(odd_from[source])] = odd
            for slot, group in groups.items():
                order[z, place, slot] = (group // 128) * 256 + (group % 32) * 8 + np.arange(8)
    return order.reshape(4, 768), sends, odd_sends, odd_from, odd_to


def on_device(
    tokens,
    memory,
    lengths,
    patch_counts,
    self_qkv,
    self_out,
    cross_query,
    cross_kv,
    cross_out,
    ffn_in,
    ffn_out,
    norm_gains,
    norm_shifts,
    proj_biases,
    ffn_bias,
    cotangent,
):
    y, xl, c, z, xh = (lax.axis_index(axis) for axis in AXES)
    x = xh * 2 + xl
    width = tokens.shape[2]
    rows = 2 * tokens.shape[1]
    page_rows = RING * rows
    length = lax.dynamic_index_in_dim(lengths, xh, 0, keepdims=False)
    count = lax.dynamic_slice(patch_counts, (xh,), (1,))
    valid = (z * rows + jnp.arange(rows) < length)[:, None]

    def swap_cores(part):
        return lax.ppermute(part, "c", FLIP)

    by_core = jnp.asarray(eight_order()).reshape(2, 512)
    sides = shuffle_matrix(
        jnp.concatenate([lax.dynamic_index_in_dim(by_core, side, 0, keepdims=False) for side in (c, 1 - c)])
    )

    def own_eights(grads):
        return product(grads, sides).astype(BF)

    def relay(chunks, axis, pairs):
        return lax.ppermute(chunks[3], axis, pairs(1)), lax.ppermute(chunks[4], axis, pairs(3))

    def add_on(chunks, got):
        return relay_add(chunks[1], chunks[2], *got)

    def send_on(sums, axis, pairs):
        return lax.ppermute(sums[0], axis, pairs(1)), lax.ppermute(sums[1], axis, pairs(3))

    def finish(chunks, got):
        return sum_low(chunks[0], *got)

    X_RING, Y_RING = (("xl", "xh"), x_pairs), ("y", ring_pairs)

    def then_y(part):
        part = part.reshape(4, 32, part.shape[1])
        return ring_sum(
            lambda target: lax.dynamic_index_in_dim(part, target, 0, keepdims=False), y, "y", ring_pairs
        ).astype(BF)

    def then_x(part):
        each = part.shape[0] // 16
        part = part.reshape(2, 4, 2, each, part.shape[1])

        def cut(target):
            piece = lax.dynamic_slice(
                part, (target % 2, 0, target // 2, 0, 0), (1, 4, 1, each, part.shape[4])
            )
            return piece.reshape(4 * each, part.shape[4])

        return ring_sum(cut, x, ("xl", "xh"), x_pairs).astype(BF)

    mine = lax.dynamic_index_in_dim(tokens, xh, 0, keepdims=False)
    other = lax.dynamic_index_in_dim(tokens, 1 - xh, 0, keepdims=False)
    other = lax.ppermute(other, "xh", FLIP)
    early_rows = [mine] + [lax.ppermute(mine, "z", ring_pairs(step)) for step in STEPS]
    late_row = after(other, *early_rows)
    late_rows = [late_row] + [lax.ppermute(late_row, "z", ring_pairs(step)) for step in STEPS]
    own_memory = swap_in(after(memory, *early_rows), xh)
    def side_by_side(own, other):
        return jnp.concatenate([jnp.where(xh == 0, own, other), jnp.where(xh == 0, other, own)], axis=0)

    own_tokens = side_by_side(mine, late_row)

    def head_cols(matrix, third):
        return lax.dynamic_slice(matrix, (0, third * width + z * 256), (matrix.shape[0], 256))

    heads_qkv = jnp.concatenate([head_cols(self_qkv, third) for third in range(3)], axis=1)
    bias_q = lax.dynamic_slice(proj_biases, (0, z * 256), (1, 256))
    bias_v = lax.dynamic_slice(proj_biases, (1, z * 256), (1, 256))
    bias_qkv = jnp.concatenate([bias_q, jnp.zeros_like(bias_q), bias_v], axis=1)
    joined, low_one, normal_one = project_heads(
        z, xh, early_rows, late_rows, heads_qkv, bias_qkv, norm_gains[0:1], norm_shifts[0:1]
    )
    heads_mix, self_level = attend(page_rows, page_rows, 2, True, joined, joined, joined, (0, 256, 512))

    memory_here = after(own_memory, *late_rows)
    before_got, behind_got = (lax.ppermute(memory_here, "z", ring_pairs(step)) for step in (1, 3))
    heads_mix, before_got, behind_got = lax.optimization_barrier((heads_mix, before_got, behind_got))
    far_got = (
        lax.ppermute(behind_got[: rows // 2], "z", ring_pairs(3)),
        lax.ppermute(before_got[rows // 2 :], "z", ring_pairs(1)),
    )
    mix_pick = lambda target: lax.dynamic_slice(heads_mix, (target * rows, 0), (rows, 256))
    mix_got = exchange(mix_pick, z, far_got)
    far_got = lax.optimization_barrier((*far_got, *(part for _, part in mix_got[1:])))[:2]
    page_memory = jnp.zeros((page_rows, width), BF)
    for hop, first, part in (
        (0, 0, memory_here),
        (1, 0, behind_got),
        (3, 0, before_got),
        (2, 0, far_got[0]),
        (2, rows // 2, far_got[1]),
    ):
        page_memory = lax.dynamic_update_slice(page_memory, part, (around(hop, z) * rows + first, 0))
    patch_bias = jnp.concatenate([jnp.zeros_like(proj_biases[4]), proj_biases[4]])
    page_kv = (product(page_memory, cross_kv) + patch_bias).astype(BF)

    grad_low = jnp.where(valid, swap_in(after(cotangent, heads_mix), xh), 0)
    mixture = jnp.zeros((rows, width), BF)
    for source, part in mix_got:
        mixture = lax.dynamic_update_slice(mixture, part, (0, source * 256))
    after_self = own_tokens.astype(F32) + product(mixture, self_out) + proj_biases[2]
    normal_two, inverse_two = unit(after_self)
    low_two = (normal_two * norm_gains[1] + norm_shifts[1]).astype(BF)
    cross_queries = (product(low_two, cross_query) + proj_biases[3]).astype(BF)
    cross_mix, cross_level = attend(
        rows, page_rows, 8, False, cross_queries, page_kv, page_kv, (0, 0, 1024), count
    )
    after_cross = after_self + product(cross_mix, cross_out) + proj_biases[5]
    normal_three, inverse_three = unit(after_cross)
    low_three = (normal_three * norm_gains[2] + norm_shifts[2]).astype(BF)
    before = product(low_three, ffn_in) + ffn_bias
    below = 0.5 * (1.0 + lax.erf(before * np.float32(np.sqrt(0.5))))
    hidden = (before * below).astype(BF)
    slope = below + before * jnp.exp(-0.5 * before * before) * np.float32(1 / np.sqrt(2 * np.pi))
    result = after_cross + product(hidden, ffn_out) + proj_biases[6]
    layer_rows = jnp.where(valid, result, 0.0).astype(BF)

    order, sends, odd_sends, odd_from, odd_to = qkv_order()
    head_order = lax.dynamic_index_in_dim(jnp.asarray(order), z, 0, keepdims=False)
    head_shuffle, sides = lax.optimization_barrier((shuffle_matrix(head_order), sides))

    out_grads = own_eights(grad_low)
    early = jnp.concatenate([cross_mix, low_two, mixture, low_three, out_grads[:, 512:]], axis=1)
    early_got = swap_cores(early)
    hidden_got = swap_cores(hidden)
    grad_before = (back_product(grad_low, ffn_out) * slope).astype(BF)
    before_sums = column_sums(grad_before)
    in_keep, in_send = split_wides(c, grad_before)
    in_got = swap_cores(in_send)
    grad_three = back_product(grad_before, ffn_in)
    grad_after_cross = grad_low.astype(F32) + unit_back(
        normal_three, inverse_three, grad_three, norm_gains[2]
    )
    cross_low = grad_after_cross.astype(BF)
    cross_grads = own_eights(cross_low)
    cross_got = swap_cores(cross_grads[:, 512:])
    grad_cross_mix = back_product(cross_low, cross_out).astype(BF)
    ffn_in_chunks = outer_chunks(
        y, 512, 512, [((in_keep, 0), (in_got, 0), (early, 3 * width), (early_got, 3 * width), 2)]
    )
    ffn_out_chunks = outer_chunks(
        x,
        128,
        width,
        [
            ((out_grads, 0), (early_got, 4 * width), (hidden, 0), (hidden_got, 0), 4),
            ((cross_grads, 0), (cross_got, 0), (early, 0), (early_got, 0), 1),
        ],
    )
    ffn_out_got = relay(ffn_out_chunks, *X_RING)
    ffn_in_got = relay(ffn_in_chunks, *Y_RING)

    grad_cross_mix, layer_rows, *got = lax.optimization_barrier(
        (grad_cross_mix, layer_rows, *ffn_out_got, *ffn_in_got)
    )
    ffn_out_sums, ffn_in_sums = add_on(ffn_out_chunks, got[:2]), add_on(ffn_in_chunks, got[2:])
    grad_cross_mix, *sums = lax.optimization_barrier((grad_cross_mix, *ffn_out_sums, *ffn_in_sums))
    ffn_out_got, ffn_in_got = send_on(sums[:2], *X_RING), send_on(sums[2:], *Y_RING)
    cross_query_low, patch_grads = attend_back(
        rows,
        page_rows,
        8,
        False,
        cross_queries,
        page_kv,
        page_kv,
        (0, 0, 1024),
        cross_mix,
        grad_cross_mix,
        cross_level,
        count,
    )
    cross_query_low, patch_grads, layer_rows, *got = lax.optimization_barrier(
        (cross_query_low, patch_grads, layer_rows, *ffn_out_got, *ffn_in_got)
    )
    layer_out = swap_out(layer_rows, xh)
    ffn_out_part, ffn_in_part = finish(ffn_out_chunks, got[:2]), finish(ffn_in_chunks, got[2:])
    grad_two = back_product(cross_query_low, cross_query)
    grad_after_self = grad_after_cross + unit_back(normal_two, inverse_two, grad_two, norm_gains[1])

    self_low = grad_after_self.astype(BF)
    grad_mix_rows = back_product(self_low, self_out).astype(BF)
    grads_here = after(patch_grads, grad_mix_rows)
    kv_send, kv_keep = patch_halves(c, grads_here, page_memory)
    grad_mixture = rows_to_heads(grad_mix_rows, z, (kv_send,))
    grads_here = after(patch_grads, grad_mixture)
    kv_rows = sum_low(kv_keep, swap_cores(kv_send))
    kv_quarters = kv_rows.reshape(RING, 256, width)

    def kv_chunk(hop):
        return lax.dynamic_index_in_dim(kv_quarters, around(hop, y), 0, keepdims=False)

    kv_own, kv_sends = kv_chunk(0), [kv_chunk(step) for step in STEPS]
    out_quarters = ffn_out_part.reshape(RING, 32, 5 * width)
    out_own, *out_sends = (
        lax.dynamic_index_in_dim(out_quarters, around(hop, y), 0, keepdims=False) for hop in (0,) + STEPS
    )
    query_grads, self_grads = own_eights(cross_query_low), own_eights(self_low)
    sent = swap_cores(jnp.concatenate([query_grads[:, 512:], self_grads[:, 512:]], axis=1))
    sent, *out_sends = lax.optimization_barrier((sent, *out_sends))
    out_got = [lax.ppermute(chunk, "y", ring_pairs(step)) for step, chunk in zip(STEPS, out_sends)]
    two_chunks = outer_chunks(
        x,
        128,
        width,
        [
            ((query_grads, 0), (sent, 0), (early, width), (early_got, width), 1),
            ((self_grads, 0), (sent, 512), (early, 2 * width), (early_got, 2 * width), 1),
        ],
        extra=ffn_in_part,
    )
    two_chunks = lax.optimization_barrier((*two_chunks, *out_got))
    two_chunks, out_got = two_chunks[:5], two_chunks[5:]
    grad_mixture, layer_out, *held = lax.optimization_barrier(
        (grad_mixture, layer_out, *kv_sends, *two_chunks)
    )
    kv_sends, two_chunks = held[:3], held[3:]

    two_got = relay(two_chunks, *X_RING)
    kv_got = [lax.ppermute(chunk, "y", ring_pairs(step)) for step, chunk in zip(STEPS, kv_sends)]
    (grad_joined,) = attend_back(
        page_rows, page_rows, 2, True, joined, joined, joined, (0, 256, 512), heads_mix, grad_mixture, self_level
    )
    grad_joined, grads_here, *two_got = lax.optimization_barrier((grad_joined, grads_here, *two_got))
    grad_joined, *two_sums = lax.optimization_barrier((grad_joined, *add_on(two_chunks, two_got)))
    two_got = send_on(two_sums, *X_RING)
    *page_chunks, page_sums, head_sums = page_back(z, grad_joined, heads_qkv, grads_here, cross_kv, normal_one)
    shuffled = product(grad_joined, head_shuffle).astype(BF)
    shuffled, page_sums, head_sums, *held = lax.optimization_barrier(
        (shuffled, page_sums, head_sums, *page_chunks, *kv_got)
    )
    page_chunks, kv_got = held[:5], held[5:]
    Z_RING = ("z", ring_pairs)
    page_got = relay(page_chunks, *Z_RING)

    def core_half(target):
        return outer(lax.dynamic_slice(shuffled, (0, target * 384), (page_rows, 384)), low_one)

    core_keep = core_half(c)
    core_send = core_half(1 - c).astype(BF)
    core_keep, core_send, *held = lax.optimization_barrier(
        (core_keep, core_send, *two_got, *kv_got, *out_got)
    )
    two_got, kv_got, out_got = held[:2], held[2:5], held[5:]
    ffn_out_part = sum_low(out_own, *out_got)

    core_got = swap_cores(core_send).astype(F32)
    vectors = [
        page_sums[0],
        column_sums(grad_two * normal_two),
        column_sums(grad_three * normal_three),
        page_sums[1],
        column_sums(grad_two),
        column_sums(grad_three),
        column_sums(grad_after_self),
        column_sums(cross_query_low),
        page_sums[2],
        column_sums(grad_after_cross),
        column_sums(grad_low),
    ]
    small_keep, small_send = pack_vectors(z, c, vectors, head_sums, before_sums.reshape(4, width))
    small_sum = (small_keep.astype(F32) + swap_cores(small_send).astype(F32)).astype(BF)
    core_sum = (core_keep + core_got).astype(BF)
    kv_part = sum_low(kv_own, *kv_got)
    core_sum, small_sum, kv_part, *page_got = lax.optimization_barrier(
        (core_sum, small_sum, kv_part, *page_got)
    )

    page_got = send_on(add_on(page_chunks, page_got), *Z_RING)
    small_sum = jnp.pad(small_sum.reshape(4, 4, 1, width), ((0, 0), (0, 0), (0, 7), (0, 0)))
    core_sum = jnp.concatenate([core_sum.reshape(4, 4, 24, width), small_sum], axis=2)
    kv_lines = kv_part.reshape(2, 4, 2, 16, width)

    def x_chunk(target):
        piece = lax.dynamic_slice(kv_lines, (target % 2, 0, target // 2, 0, 0), (1, 4, 1, 16, width))
        lines = lax.dynamic_index_in_dim(core_sum, target, 0, keepdims=False)
        return jnp.concatenate([lines.reshape(128, width), piece.reshape(64, width)], axis=0)

    x_sum = ring_sum(x_chunk, x, ("xl", "xh"), x_pairs).astype(BF)
    two_part = finish(two_chunks, two_got)
    x_sum, two_part, mine, late_row, *page_got = lax.optimization_barrier(
        (x_sum, two_part, mine, late_row, *page_got)
    )
    own_tokens = side_by_side(mine, late_row)

    two_part, ffn_in_part = two_part[:, : 2 * width].reshape(4, 32, 2 * width), two_part[:, 2 * width :]
    cross_kv_part = x_sum[128:]
    y_lines = jnp.concatenate([x_sum[:128].reshape(4, 32, width), two_part], axis=2)
    y_sum = ring_sum(
        lambda target: lax.dynamic_index_in_dim(y_lines, target, 0, keepdims=False), y, "y", ring_pairs
    )
    grad_own, memory_rows = (
        sum(part[:, at : at + width].astype(F32) for part in (page_chunks[0], *page_got)) for at in (0, width)
    )
    own_normal, own_inverse = unit(own_tokens.astype(F32))
    token_rows = grad_after_self + unit_back(own_normal, own_inverse, grad_own, norm_gains[0])
    both_grads = swap_out(jnp.concatenate([token_rows, memory_rows], axis=1).astype(BF), xh)
    token_grad, memory_grad = both_grads[..., :width], both_grads[..., width:]

    two_part, y_sum = y_sum[:, width:].astype(BF), y_sum[:, :width]
    small_part = jnp.pad(y_sum[24].astype(BF).reshape(4, 1, 256), ((0, 0), (0, 7), (0, 768)))
    me = (((y * 2 + xl) * 2 + c) * 4 + z) * 2 + xh
    odd_at = lax.dynamic_index_in_dim(jnp.asarray(odd_from), me, 0, keepdims=False) * 8
    odd_got = lax.ppermute(lax.dynamic_slice(y_sum, (odd_at, 0), (8, width)), AXES, odd_sends)
    odd_here = jnp.arange(24) // 8 == lax.dynamic_index_in_dim(jnp.asarray(odd_to), me, 0, keepdims=False)
    grad_qkv = lax.ppermute(y_sum[:24], AXES, sends)
    grad_qkv = jnp.where(odd_here[:, None], jnp.concatenate([odd_got] * 3, axis=0), grad_qkv)

    lines = []
    for part in (ffn_out_part, ffn_in_part, two_part, cross_kv_part, small_part):
        part = part.reshape(4, -1, part.shape[-1])
        lines += [part[..., at : at + width] for at in range(0, part.shape[-1], width)]
    lines = jnp.concatenate(lines, axis=1)
    z_line = lambda hop: lax.dynamic_index_in_dim(lines, around(hop, z), 0, keepdims=False)
    z_got = [lax.ppermute(z_line(step), "z", ring_pairs(step)) for step in STEPS]
    ffn_out_rows, cross_out_rows, ffn_in_rows, cross_query_rows, self_out_rows, cross_kv_rows, *small = last_sums(
        z_line(0), *z_got
    )

    return (
        layer_out,
        token_grad,
        memory_grad,
        grad_qkv.T,
        self_out_rows.T,
        cross_query_rows.T,
        cross_kv_rows.T,
        cross_out_rows.T,
        ffn_in_rows.T,
        ffn_out_rows.T,
        *small[:3],
        small[3].reshape(-1),
    )


def solution(mesh):
    split = jax.sharding.Mesh(mesh.devices.reshape(MESH_SHAPE), AXES)
    page, blk = AXES[:3], AXES[3:]
    blocks, cols = P(page, blk, None), P(None, AXES)
    in_specs = (blocks, blocks, P(page), P(page)) + (P(),) * 11 + (blocks,)
    out_specs = (blocks,) * 3 + (cols,) * 10 + (P(AXES),)
    return jax.shard_map(
        on_device, mesh=split, in_specs=in_specs, out_specs=out_specs, check_vma=False
    )
```

```python
import functools

import jax
import jax.numpy as jnp
import numpy as np
from jax import lax
from jax.experimental import pallas as pl
from jax.experimental.pallas import tpu as pltpu
from jax.sharding import PartitionSpec as P

EPS = 1e-05

BF = jnp.bfloat16
F32 = jnp.float32
NEG = -1e30
TILE = 256
PAIR = 128
HINT = pl.CostEstimate(flops=1 << 20, bytes_accessed=1 << 16, transcendentals=0)


def dot_tt(a, b):
    return lax.dot_general(a, b, (((1,), (1,)), ((), ())), preferred_element_type=F32)


def dot_nn(a, b):
    return lax.dot_general(a, b, (((1,), (0,)), ((), ())), preferred_element_type=F32)


def two_heads(rows):
    lanes = lax.broadcasted_iota(jnp.int32, rows.shape, 1)
    none = jnp.zeros_like(rows)
    return jnp.concatenate([jnp.where(lanes < 64, rows, none), jnp.where(lanes < 64, none, rows)], axis=0)


def later_key():
    keys = lax.broadcasted_iota(jnp.int32, (TILE, 2 * TILE), 0)
    return keys > lax.broadcasted_iota(jnp.int32, (TILE, 2 * TILE), 1) % TILE


def own_halves(both):
    return jnp.concatenate([both[:64, :TILE], both[64:, TILE:]], axis=0).T


def span(tile):
    return pl.ds(tile * TILE, TILE)


def forward_tiles(key_tiles, causal, q_ref, k_ref, o_ref, lse_ref, vt_ref, s_ref):
    for i in range(q_ref.shape[0] // TILE):
        tiles = i + 1 if causal else key_tiles
        queries = two_heads(q_ref[span(i), :] * 0.125)
        kept = s_ref.at[i % 2]
        top = None
        for j in range(tiles):
            scores = dot_tt(k_ref[span(j), :], queries)
            if causal and j == i:
                scores = jnp.where(later_key(), NEG, scores)
            kept[span(j), :] = scores
            tile_top = jnp.max(scores, axis=0, keepdims=True)
            top = tile_top if top is None else jnp.maximum(top, tile_top)
        total, mixed = None, None
        for j in range(tiles):
            shares = jnp.exp(kept[span(j), :] - top)
            tile_sum = jnp.sum(shares, axis=0, keepdims=True)
            tile_mix = dot_nn(vt_ref[:, span(j)], shares.astype(BF))
            total = tile_sum if total is None else total + tile_sum
            mixed = tile_mix if mixed is None else mixed + tile_mix
        level = top + jnp.log(total)
        lse_ref[0, 0:1, span(i)] = level[:, :TILE]
        lse_ref[0, 1:2, span(i)] = level[:, TILE:]
        o_ref[span(i), :] = own_halves(mixed / total).astype(o_ref.dtype)


def pair_columns(pair, first=0):
    return pl.ds(pl.multiple_of(pair * PAIR + first, PAIR), PAIR)


def every_pair(pairs, count_ref, tiles, run):
    def loop(live):
        @pl.loop(0, pairs // 2)
        def _(couple):
            run(2 * couple, 0, live)
            run(2 * couple + 1, 1, live)

    if count_ref is None:
        loop(tiles)
    else:
        pl.when(count_ref[0] > TILE)(lambda: loop(tiles))
        pl.when(count_ref[0] <= TILE)(lambda: loop(1))


def forward_kernel(pairs, causal, firsts, *refs):
    count_ref = None if causal else refs[0]
    refs = refs if causal else refs[1:]
    q_ref, k_ref, v_ref, o_ref, lse_ref, vt_ref, s_ref = refs

    def run(pair, slot, tiles):
        q, k, v = (ref.at[:, pair_columns(pair, at)] for ref, at in zip((q_ref, k_ref, v_ref), firsts))
        vt, kept = vt_ref.at[slot], s_ref.at[slot]
        vt[:, : tiles * TILE] = v[: tiles * TILE, :].T
        out, level = o_ref.at[:, pair_columns(pair)], lse_ref.at[pl.ds(pair, 1)]
        forward_tiles(tiles, causal, q, k, out, level, vt, kept)

    every_pair(pairs, count_ref, k_ref.shape[0] // TILE, run)


def backward_tiles(
    key_tiles, causal, q_ref, k_ref, v_ref, o_ref, do_ref, lse_ref, dq_ref, kt_ref, dk_ref, dv_ref
):
    ones = jnp.ones((8, PAIR), F32)
    for i in range(q_ref.shape[0] // TILE):
        tiles = i + 1 if causal else key_tiles
        queries = two_heads(q_ref[span(i), :] * 0.125)
        pulled = two_heads(do_ref[span(i), :])
        out = o_ref[span(i), :].astype(F32)
        weighed = pulled.astype(F32) * jnp.concatenate([out, out], axis=0)
        dots = lax.dot_general(
            ones,
            weighed,
            (((1,), (1,)), ((), ())),
            preferred_element_type=F32,
            precision=lax.Precision.HIGHEST,
        )[0:1, :]
        level = jnp.concatenate([lse_ref[0, 0:1, span(i)], lse_ref[0, 1:2, span(i)]], axis=1)
        drawn = None
        for j in range(tiles):
            shares = jnp.exp(dot_tt(k_ref[span(j), :], queries) - level)
            if causal and j == i:
                shares = jnp.where(later_key(), 0.0, shares)
            grad_shares = dot_tt(v_ref[span(j), :], pulled)
            grad_scores = (shares * (grad_shares - dots)).astype(BF)
            dv_part = dot_nn(shares.astype(BF), pulled)
            dk_part = dot_nn(grad_scores, queries)
            if i == (j if causal else 0):
                dv_ref[span(j), :] = dv_part
                dk_ref[span(j), :] = dk_part
            else:
                dv_ref[span(j), :] += dv_part
                dk_ref[span(j), :] += dk_part
            tile_drawn = dot_nn(kt_ref[:, span(j)], grad_scores)
            drawn = tile_drawn if drawn is None else drawn + tile_drawn
        dq_ref[span(i), :] = (own_halves(drawn) * 0.125).astype(dq_ref.dtype)


def backward_kernel(pairs, causal, firsts, *refs):
    count_ref = None if causal else refs[0]
    refs = refs if causal else refs[1:]
    q_ref, k_ref, v_ref, o_ref, do_ref, lse_ref, *outs, kt_ref, dk_ref, dv_ref = refs
    dq_ref, dkv_ref = outs[0], outs[-1]
    width = pairs * PAIR
    first = dkv_ref.shape[1] - 2 * width

    def run(pair, slot, tiles):
        q, k, v = (ref.at[:, pair_columns(pair, at)] for ref, at in zip((q_ref, k_ref, v_ref), firsts))
        cols, live = pair_columns(pair), tiles * TILE
        kt, dk, dv = kt_ref.at[slot], dk_ref.at[slot], dv_ref.at[slot]
        kt[:, :live] = k[:live, :].T
        if live < k.shape[0]:
            dk[...] = jnp.zeros_like(dk)
            dv[...] = jnp.zeros_like(dv)
        out, grads, level = o_ref.at[:, cols], do_ref.at[:, cols], lse_ref.at[pl.ds(pair, 1)]
        backward_tiles(
            tiles, causal, q, k, v, out, grads, level, dq_ref.at[:, cols], kt, dk, dv
        )
        dkv_ref[:, pair_columns(pair, first)] = dk[...].astype(BF)
        dkv_ref[:, pair_columns(pair, first + width)] = dv[...].astype(BF)

    every_pair(pairs, count_ref, k_ref.shape[0] // TILE, run)


SCALAR = pl.BlockSpec(memory_space=pltpu.SMEM)
HERE = pl.BlockSpec(memory_space=pltpu.VMEM)


def attend(q_rows, key_rows, pairs, causal, q, k, v, firsts, count=None):
    return pl.pallas_call(
        functools.partial(forward_kernel, pairs, causal, firsts),
        in_specs=([] if causal else [SCALAR]) + [HERE] * 3,
        out_specs=[HERE] * 2,
        out_shape=[
            jax.ShapeDtypeStruct((q_rows, pairs * PAIR), BF),
            jax.ShapeDtypeStruct((pairs, 2, q_rows), F32),
        ],
        scratch_shapes=[pltpu.VMEM((2, PAIR, key_rows), BF), pltpu.VMEM((2, 2, key_rows, 2 * TILE), F32)],
        compiler_params=pltpu.CompilerParams(vmem_limit_bytes=32 * 1024 * 1024),
        cost_estimate=HINT,
    )(*(() if causal else (count,)), q, k, v)


def attend_back(q_rows, key_rows, pairs, causal, q, k, v, firsts, o, do, lse, count=None):
    width = pairs * PAIR
    shapes = [jax.ShapeDtypeStruct((q_rows, width), BF), jax.ShapeDtypeStruct((key_rows, 2 * width), BF)]
    if causal:
        shapes = [jax.ShapeDtypeStruct((q_rows, 3 * width), BF)]
    return pl.pallas_call(
        functools.partial(backward_kernel, pairs, causal, firsts),
        in_specs=([] if causal else [SCALAR]) + [HERE] * 6,
        out_specs=[HERE] * len(shapes),
        out_shape=shapes,
        scratch_shapes=[
            pltpu.VMEM((2, PAIR, key_rows), BF),
            pltpu.VMEM((2, key_rows, PAIR), F32),
            pltpu.VMEM((2, key_rows, PAIR), F32),
        ],
        compiler_params=pltpu.CompilerParams(vmem_limit_bytes=32 * 1024 * 1024),
        cost_estimate=HINT,
    )(*(() if causal else (count,)), q, k, v, o, do, lse)

AXES = ("y", "xl", "c", "z", "xh")
MESH_SHAPE = (4, 2, 2, 4, 2)
RING = 4


def ring_pairs(step):
    return [(i, (i + step) % RING) for i in range(RING)]


def x_slot(x):
    return (x % 2) * 2 + x // 2


def x_pairs(step):
    return [(x_slot(x), x_slot((x + step) % RING)) for x in range(RING)]


FLIP = [(0, 1), (1, 0)]
STEPS = (1, 3, 2)


def around(step, coord):
    return lax.rem(coord + step, RING)


def swap_in(blocks, side):
    own = lax.dynamic_index_in_dim(blocks, side, 0, keepdims=False)
    got = lax.ppermute(lax.dynamic_index_in_dim(blocks, 1 - side, 0, keepdims=False), "xh", FLIP)
    return jnp.concatenate([jnp.where(side == 0, own, got), jnp.where(side == 0, got, own)], axis=0)


def swap_out(rows, side):
    blocks = rows.reshape(2, rows.shape[0] // 2, rows.shape[1])
    own = lax.dynamic_index_in_dim(blocks, side, 0, keepdims=False)
    got = lax.ppermute(lax.dynamic_index_in_dim(blocks, 1 - side, 0, keepdims=False), "xh", FLIP)
    return jnp.stack([jnp.where(side == 0, own, got), jnp.where(side == 0, got, own)])


def exchange(pick, z, behind=()):
    got = [lax.ppermute(pick(around(step, z)), "z", ring_pairs(step)) for step in STEPS]
    got = lax.optimization_barrier((*got, *behind))[: len(STEPS)]
    return [(z, pick(z))] + [(around(RING - step, z), part) for step, part in zip(STEPS, got)]


def rows_to_heads(rows, z, behind=()):
    height, width = rows.shape[0], rows.shape[1] // RING
    full = jnp.zeros((RING * height, width), rows.dtype)
    pick = lambda target: lax.dynamic_slice(rows, (0, target * width), (height, width))
    for source, part in exchange(pick, z, behind):
        full = lax.dynamic_update_slice(full, part, (source * height, 0))
    return full


def ring_sum(pick, coord, axis, pairs):
    total = pick(coord).astype(F32)
    for step in STEPS:
        got = lax.ppermute(pick(around(step, coord)).astype(BF), axis, pairs(step))
        total = total + got.astype(F32)
    return total


def after(value, *others):
    return lax.optimization_barrier((value, *others))[0]


def product(left, right):
    return jnp.dot(left, right, preferred_element_type=F32)


def back_product(grads, matrix):
    return lax.dot_general(grads, matrix, (((1,), (1,)), ((), ())), preferred_element_type=F32)


def outer(grads, inputs):
    return lax.dot_general(grads, inputs, (((0,), (0,)), ((), ())), preferred_element_type=F32)


def unit(rows):
    centred = rows - jnp.mean(rows, axis=-1, keepdims=True)
    inverse = lax.rsqrt(jnp.mean(centred * centred, axis=-1, keepdims=True) + EPS)
    return centred * inverse, inverse


def unit_back(normal, inverse, grads, gain):
    scaled = grads * gain
    mean = jnp.mean(scaled, axis=-1, keepdims=True)
    along = jnp.mean(scaled * normal, axis=-1, keepdims=True)
    return inverse * (scaled - mean - normal * along)


def chunks_kernel(width, block, segments, coord_ref, *refs):
    outs, turned_ref = refs[-6:-1], refs[-1]
    own_ref, plus_ref, minus_ref, far_a_ref, far_b_ref = outs
    tokens = refs[0].shape[0]
    half, each = width // 2, width // 4
    lane = 0

    def put(pick, lanes):
        own_ref[:, lanes] = pick(0, 0, width).astype(F32)
        plus_ref[:, lanes] = pick(1, 0, width).astype(BF)
        minus_ref[:, lanes] = pick(3, 0, width).astype(BF)
        far_a_ref[:, lanes] = pick(2, 0, half).astype(BF)
        far_b_ref[:, lanes] = pick(2, half, half).astype(BF)

    for at, (grads_at, got_grads_at, inputs_at, got_inputs_at, blocks) in enumerate(segments):
        grads_ref, got_grads_ref, inputs_ref, got_inputs_ref = refs[4 * at : 4 * at + 4]
        for hop in range(RING):
            column = around(hop, coord_ref[0]) * width
            rows = slice(hop * width, hop * width + width)
            turned_ref[at, rows, :tokens] = grads_ref[:, pl.ds(pl.multiple_of(grads_at + column, 128), width)].T
            turned_ref[at, rows, tokens:] = got_grads_ref[
                :, pl.ds(pl.multiple_of(got_grads_at + column, 128), width)
            ].T
        for number in range(blocks):
            mine = inputs_ref[:, inputs_at + number * block : inputs_at + number * block + block]
            got = got_inputs_ref[:, got_inputs_at + number * block : got_inputs_at + number * block + block]

            def pick(hop, first, rows, at=at, mine=mine, got=got):
                turned = turned_ref.at[at, hop * width + first : hop * width + first + rows, :]
                return dot_nn(turned[:, :tokens], mine) + dot_nn(turned[:, tokens:], got)

            put(pick, slice(lane, lane + block))
            lane += block

    if lane < own_ref.shape[1]:
        extra_ref = refs[4 * len(segments)]

        def pick(hop, first, rows):
            target = around(hop, coord_ref[0])
            zs = range(first // each, (first + rows) // each)
            return jnp.concatenate([extra_ref[target % 2, zz, target // 2] for zz in zs], axis=0)

        put(pick, slice(lane, own_ref.shape[1]))


def outer_chunks(coord, width, block, segments, extra=None):
    cols = RING * width
    tokens = segments[0][0][0].shape[0]
    operands = [array for segment in segments for array, _ in segment[:4]]
    places = tuple(tuple(first for _, first in segment[:4]) + (segment[4],) for segment in segments)
    lanes = sum(segment[4] for segment in segments) * block
    if extra is not None:
        operands.append(extra.reshape(2, 4, 2, width // 4, extra.shape[1]))
        lanes += extra.shape[1]
    shape = lambda rows, dtype: jax.ShapeDtypeStruct((rows, lanes), dtype)
    return pl.pallas_call(
        functools.partial(chunks_kernel, width, block, places),
        in_specs=[SCALAR] + [HERE] * len(operands),
        out_specs=[HERE] * 5,
        out_shape=[shape(width, F32), shape(width, BF), shape(width, BF)] + [shape(width // 2, BF)] * 2,
        scratch_shapes=[pltpu.VMEM((len(segments), cols, 2 * tokens), BF)],
        compiler_params=pltpu.CompilerParams(vmem_limit_bytes=40 * 1024 * 1024),
        cost_estimate=HINT,
    )(coord.reshape(1), *operands)


def project_kernel(place_ref, *refs):
    early, late = refs[:RING], refs[RING : 2 * RING]
    matrix_ref, bias_ref, gain_ref, shift_ref, joined_ref, low_ref, normal_ref = refs[2 * RING :]

    def run(at):
        first = jnp.where(place_ref[1] == 0, early[at][...], late[at][...])
        second = jnp.where(place_ref[1] == 0, late[at][...], early[at][...])
        normal, _ = unit(jnp.concatenate([first, second], axis=0).astype(F32))
        low = (normal * gain_ref[...] + shift_ref[...]).astype(BF)
        low_ref[...] = low
        normal_ref[...] = normal.astype(BF)
        joined_ref[...] = (dot_nn(low, matrix_ref[...]) + bias_ref[...]).astype(BF)

    for at in range(RING):
        pl.when(pl.program_id(0) == at)(functools.partial(run, at))


def project_heads(z, side, early, late, matrix, bias, gain, shift):
    half, width = early[0].shape
    rows = 2 * half

    def row_block(j, place):
        hop = jnp.where(j == 0, 0, jnp.where(j == 1, STEPS[0], jnp.where(j == 2, STEPS[1], STEPS[2])))
        return (lax.rem(place[0] + RING - hop, RING), 0)

    whole = lambda shape: pl.BlockSpec(shape, lambda j, place: (0, 0))
    return pl.pallas_call(
        project_kernel,
        grid_spec=pltpu.PrefetchScalarGridSpec(
            num_scalar_prefetch=1,
            grid=(RING,),
            in_specs=[whole((half, width))] * 8
            + [whole((width, 768)), whole((1, 768)), whole((1, width)), whole((1, width))],
            out_specs=[
                pl.BlockSpec((rows, 768), row_block),
                pl.BlockSpec((rows, width), row_block),
                pl.BlockSpec((rows, width), row_block),
            ],
        ),
        out_shape=[
            jax.ShapeDtypeStruct((RING * rows, 768), BF),
            jax.ShapeDtypeStruct((RING * rows, width), BF),
            jax.ShapeDtypeStruct((RING * rows, width), BF),
        ],
        compiler_params=pltpu.CompilerParams(vmem_limit_bytes=40 * 1024 * 1024),
        cost_estimate=HINT,
    )(jnp.stack([z, side]), *early, *late, matrix, bias, gain, shift)


def split_kernel(core_ref, grads_ref, keep_ref, send_ref):
    for at in range(grads_ref.shape[1] // 512):
        first = grads_ref[:, 512 * at : 512 * at + 256]
        second = grads_ref[:, 512 * at + 256 : 512 * at + 512]
        keep_ref[:, 256 * at : 256 * at + 256] = jnp.where(core_ref[0] == 0, first, second)
        send_ref[:, 256 * at : 256 * at + 256] = jnp.where(core_ref[0] == 0, second, first)


def split_wides(core, grads):
    rows, cols = grads.shape
    put = pl.BlockSpec((rows // 2, cols // 2), lambda j: (j, 0))
    return pl.pallas_call(
        split_kernel,
        grid=(2,),
        in_specs=[SCALAR, pl.BlockSpec((rows // 2, cols), lambda j: (j, 0))],
        out_specs=[put, put],
        out_shape=[jax.ShapeDtypeStruct((rows, cols // 2), BF)] * 2,
        compiler_params=pltpu.CompilerParams(vmem_limit_bytes=32 * 1024 * 1024),
        cost_estimate=HINT,
    )(core.reshape(1), grads)


def patch_halves_kernel(side_ref, grads_ref, inputs_ref, send_ref, keep_ref):
    for out_ref, side in ((send_ref, 1 - side_ref[0]), (keep_ref, side_ref[0])):
        for group in range(8):
            column = pl.multiple_of((group * 2 + side) * 128, 128)
            part = outer(grads_ref[:, pl.ds(column, 128)], inputs_ref[...])
            out_ref[group * 128 : group * 128 + 128, :] = part.astype(BF)


def patch_halves(side, grads, inputs):
    patches, width = inputs.shape
    return pl.pallas_call(
        patch_halves_kernel,
        in_specs=[SCALAR, HERE, HERE],
        out_specs=[HERE, HERE],
        out_shape=[jax.ShapeDtypeStruct((1024, width), BF)] * 2,
        compiler_params=pltpu.CompilerParams(vmem_limit_bytes=32 * 1024 * 1024),
        cost_estimate=HINT,
    )(side.reshape(1), grads, inputs)


def page_kernel(place_ref, joined_ref, heads_ref, patch_ref, cross_ref, normal_ref, *refs):
    own_ref, plus_ref, minus_ref, far_a_ref, far_b_ref, sums_ref, head_sums_ref = refs
    rows, width = own_ref.shape[0], cross_ref.shape[0]
    half = rows // 2
    sums, head_sums = [0.0, 0.0, 0.0], 0.0
    for hop in range(RING):
        here = pl.ds(pl.multiple_of(around(hop, place_ref[0]) * rows, rows), rows)
        one = dot_tt(joined_ref[here, :], heads_ref[...])
        sums[0] += jnp.sum(one * normal_ref[here, :].astype(F32), axis=0, keepdims=True)
        sums[1] += jnp.sum(one, axis=0, keepdims=True)
        sums[2] += jnp.sum(patch_ref[here, width:].astype(F32), axis=0, keepdims=True)
        head_sums += jnp.sum(joined_ref[here, :].astype(F32), axis=0, keepdims=True)
        two = dot_tt(patch_ref[here, :], cross_ref[...])
        for part, lanes in ((one, slice(0, width)), (two, slice(width, 2 * width))):
            if hop == 2:
                far_a_ref[:, lanes] = part[:half].astype(BF)
                far_b_ref[:, lanes] = part[half:].astype(BF)
            else:
                out_ref = {0: own_ref, 1: plus_ref, 3: minus_ref}[hop]
                out_ref[:, lanes] = part.astype(out_ref.dtype)
    sums_ref[...] = jnp.concatenate(sums, axis=0)
    head_sums_ref[...] = head_sums


def page_back(z, joined, heads, patch_grads, cross_kv, normal):
    page_rows, width = normal.shape
    rows = page_rows // RING
    chunk = lambda height, dtype: jax.ShapeDtypeStruct((height, 2 * width), dtype)
    return pl.pallas_call(
        page_kernel,
        in_specs=[SCALAR] + [HERE] * 5,
        out_specs=[HERE] * 7,
        out_shape=[
            chunk(rows, F32),
            chunk(rows, BF),
            chunk(rows, BF),
            chunk(rows // 2, BF),
            chunk(rows // 2, BF),
            jax.ShapeDtypeStruct((3, width), F32),
            jax.ShapeDtypeStruct((1, joined.shape[1]), F32),
        ],
        compiler_params=pltpu.CompilerParams(vmem_limit_bytes=40 * 1024 * 1024),
        cost_estimate=HINT,
    )(z.reshape(1), joined, heads, patch_grads, cross_kv, normal)


def relay_add_kernel(plus_ref, minus_ref, got_a_ref, got_b_ref, plus_out_ref, minus_out_ref):
    half = got_a_ref.shape[0]
    plus_out_ref[:half] = (plus_ref[:half].astype(F32) + got_a_ref[...].astype(F32)).astype(BF)
    plus_out_ref[half:] = plus_ref[half:]
    minus_out_ref[:half] = minus_ref[:half]
    minus_out_ref[half:] = (minus_ref[half:].astype(F32) + got_b_ref[...].astype(F32)).astype(BF)


def relay_add(plus, minus, got_a, got_b):
    return pl.pallas_call(
        relay_add_kernel,
        in_specs=[HERE] * 4,
        out_specs=[HERE] * 2,
        out_shape=[jax.ShapeDtypeStruct(plus.shape, BF)] * 2,
        compiler_params=pltpu.CompilerParams(vmem_limit_bytes=32 * 1024 * 1024),
        cost_estimate=HINT,
    )(plus, minus, got_a, got_b)


def vectors_kernel(place_ref, *refs):
    *row_refs, heads_ref, bias_ref, keep_ref, send_ref = refs
    width = bias_ref.shape[1]
    quarter = width // 4
    at_heads = lax.broadcasted_iota(jnp.int32, (1, width), 1) // quarter == place_ref[0]
    own = [ref[...] for ref in row_refs]
    for place, first in ((6, 0), (7, 2 * quarter)):
        part = heads_ref[:, first : first + quarter]
        own.insert(place, jnp.where(at_heads, jnp.concatenate([part] * 4, axis=1), 0.0))
    group = lax.broadcasted_iota(jnp.int32, (32, width), 0)
    col = lax.broadcasted_iota(jnp.int32, (32, width), 1)

    def of_group(owner, y):
        return group == owner // 8 % 2 * 16 + (owner % 2 * 2 + owner // 16 % 2) * 4 + y

    eights = of_group(col // 8, col // 256)
    picked = [jnp.where(eights, row.astype(BF).astype(F32), 0.0).astype(BF) for row in own]
    for y in range(4):
        bias = bias_ref[y : y + 1, :].astype(BF).astype(F32)
        picked.append(jnp.where(of_group(col // 32, y), bias, 0.0).astype(BF))
    col = lax.broadcasted_iota(jnp.int32, (width, 128), 0)
    lane = lax.broadcasted_iota(jnp.int32, (width, 128), 1)
    narrow = (lane == col // 16 % 4 * 8 + col % 8).astype(F32).astype(BF)
    wide = (lane == col // 64 % 4 * 32 + col % 32).astype(F32).astype(BF)
    rows = dot_nn(jnp.concatenate(picked[:13], axis=0), narrow).astype(BF)
    bias = dot_nn(jnp.concatenate(picked[13:], axis=0), wide).astype(BF)
    bias = bias[:32] + bias[32:64] + bias[64:96] + bias[96:]
    lane = lax.broadcasted_iota(jnp.int32, (128, width), 0)
    spot = lax.broadcasted_iota(jnp.int32, (128, width), 1)
    packed = dot_nn(bias, (spot == lane // 32 * 256 + 104 + lane % 32).astype(F32).astype(BF))
    for place in range(13):
        here = (spot == lane // 8 * 256 + place * 8 + lane % 8) & (lane < 32)
        packed += dot_nn(rows[32 * place : 32 * place + 32], here.astype(F32).astype(BF))
    packed = packed.astype(BF)
    keep_ref[...] = jnp.where(place_ref[1] == 0, packed[:16], packed[16:])
    send_ref[...] = jnp.where(place_ref[1] == 0, packed[16:], packed[:16])


def pack_vectors(z, core, rows, head_sums, bias):
    width = bias.shape[1]
    return pl.pallas_call(
        vectors_kernel,
        in_specs=[SCALAR] + [HERE] * (len(rows) + 2),
        out_specs=[HERE] * 2,
        out_shape=[jax.ShapeDtypeStruct((16, width), BF)] * 2,
        compiler_params=pltpu.CompilerParams(vmem_limit_bytes=32 * 1024 * 1024),
        cost_estimate=HINT,
    )(jnp.stack([z, core]), *(row.reshape(1, width) for row in rows), head_sums, bias)


def last_kernel(*refs):
    parts, outs = refs[:RING], refs[RING:]
    total = sum(ref[...].astype(F32) for ref in parts)
    ffn_out, cross_out, ffn_in, cross_query, self_out, cross_kv, gains, shifts, biases, ffn_bias = outs
    width = total.shape[1]
    for at in range(4):
        ffn_out[:, at * width : at * width + width] = total[8 * at : 8 * at + 8]
    cross_out[...] = total[32:40]
    ffn_in[...] = total[40:72]
    cross_query[...] = total[72:80]
    self_out[...] = total[80:88]
    cross_kv[...] = total[88:104]
    line = total[104:112, :256]
    spot = lax.broadcasted_iota(jnp.int32, (24, 256), 1)
    picked = jnp.where(spot // 8 == lax.broadcasted_iota(jnp.int32, (24, 256), 0), line[0:1], 0.0)
    spot = lax.broadcasted_iota(jnp.int32, (256, 128), 0)
    lane = lax.broadcasted_iota(jnp.int32, (256, 128), 1)
    exact = functools.partial(jnp.dot, precision=lax.Precision.HIGHEST, preferred_element_type=F32)
    table = exact(picked, (spot % 8 == lane).astype(F32))
    gains[...] = table[0:3, :8]
    shifts[...] = table[3:6, :8]
    biases[...] = table[6:13, :8]
    ffn_bias[...] = exact(line, (spot == 104 + lane).astype(F32))[0:1, :32]


def last_sums(*parts):
    width = parts[0].shape[1]
    shapes = [(8, 4 * width), (8, width), (32, width), (8, width), (8, width), (16, width)]
    shapes += [(3, 8), (3, 8), (7, 8), (1, 32)]
    return pl.pallas_call(
        last_kernel,
        in_specs=[HERE] * RING,
        out_specs=[HERE] * len(shapes),
        out_shape=[jax.ShapeDtypeStruct(shape, F32) for shape in shapes],
        compiler_params=pltpu.CompilerParams(vmem_limit_bytes=32 * 1024 * 1024),
        cost_estimate=HINT,
    )(*parts)


def sum_kernel(*refs):
    total = refs[0][...].astype(F32)
    for ref in refs[1:-1]:
        total = total + ref[...].astype(F32)
    refs[-1][...] = total.astype(refs[-1].dtype)


def sum_low(*parts):
    return pl.pallas_call(
        sum_kernel,
        in_specs=[HERE] * len(parts),
        out_specs=HERE,
        out_shape=jax.ShapeDtypeStruct(parts[0].shape, BF),
        compiler_params=pltpu.CompilerParams(vmem_limit_bytes=32 * 1024 * 1024),
        cost_estimate=HINT,
    )(*parts)


def column_sums(rows):
    return jnp.sum(rows.astype(F32), axis=0)


def eight_order():
    cols = np.arange(1024).reshape(4, 2, 2, 4, 2, 8)
    return cols.transpose(2, 4, 1, 0, 3, 5).reshape(-1)


def shuffle_matrix(order):
    cols = order.shape[0]
    return (lax.broadcasted_iota(jnp.int32, (cols, cols), 0) == order[None, :]).astype(BF)


def qkv_order():
    order = np.zeros((4, 32, 3, 8), np.int32)
    sends, odd_sends = [], []
    odd_from, odd_to = np.zeros(128, np.int32), np.full(128, -1, np.int32)
    for z in range(4):
        owners = {}
        for group in (third * 128 + z * 32 + k for third in range(3) for k in range(32)):
            owners.setdefault(group // 3, []).append(group)
        by_size = {size: [owner for owner in sorted(owners) if len(owners[owner]) == size] for size in (1, 2, 3)}
        for place, owner in enumerate(by_size[3] + by_size[2]):
            c, x, y = place // 16, place // 4 % 4, place % 4
            source = (((y * 2 + x % 2) * 2 + c) * 4 + z) * 2 + x // 2
            sends.append((source, owner))
            groups = {group % 3: group for group in owners[owner]}
            if len(groups) == 2:
                odd_owner = by_size[1][place - len(by_size[3])]
                (odd,) = owners[odd_owner]
                (odd_from[source],) = {0, 1, 2} - set(groups)
                odd_to[odd_owner] = odd % 3
                odd_sends.append((source, odd_owner))
                groups[int(odd_from[source])] = odd
            for slot, group in groups.items():
                order[z, place, slot] = (group // 128) * 256 + (group % 32) * 8 + np.arange(8)
    return order.reshape(4, 768), sends, odd_sends, odd_from, odd_to


def on_device(
    tokens,
    memory,
    lengths,
    patch_counts,
    self_qkv,
    self_out,
    cross_query,
    cross_kv,
    cross_out,
    ffn_in,
    ffn_out,
    norm_gains,
    norm_shifts,
    proj_biases,
    ffn_bias,
    cotangent,
):
    y, xl, c, z, xh = (lax.axis_index(axis) for axis in AXES)
    x = xh * 2 + xl
    width = tokens.shape[2]
    rows = 2 * tokens.shape[1]
    page_rows = RING * rows
    length = lax.dynamic_index_in_dim(lengths, xh, 0, keepdims=False)
    count = lax.dynamic_slice(patch_counts, (xh,), (1,))
    valid = (z * rows + jnp.arange(rows) < length)[:, None]

    def swap_cores(part):
        return lax.ppermute(part, "c", FLIP)

    by_core = jnp.asarray(eight_order()).reshape(2, 512)
    sides = shuffle_matrix(
        jnp.concatenate([lax.dynamic_index_in_dim(by_core, side, 0, keepdims=False) for side in (c, 1 - c)])
    )

    def own_eights(grads):
        return product(grads, sides).astype(BF)

    def relay(chunks, axis, pairs):
        return lax.ppermute(chunks[3], axis, pairs(1)), lax.ppermute(chunks[4], axis, pairs(3))

    def add_on(chunks, got):
        return relay_add(chunks[1], chunks[2], *got)

    def send_on(sums, axis, pairs):
        return lax.ppermute(sums[0], axis, pairs(1)), lax.ppermute(sums[1], axis, pairs(3))

    def finish(chunks, got):
        return sum_low(chunks[0], *got)

    X_RING, Y_RING = (("xl", "xh"), x_pairs), ("y", ring_pairs)

    def then_y(part):
        part = part.reshape(4, 32, part.shape[1])
        return ring_sum(
            lambda target: lax.dynamic_index_in_dim(part, target, 0, keepdims=False), y, "y", ring_pairs
        ).astype(BF)

    def then_x(part):
        each = part.shape[0] // 16
        part = part.reshape(2, 4, 2, each, part.shape[1])

        def cut(target):
            piece = lax.dynamic_slice(
                part, (target % 2, 0, target // 2, 0, 0), (1, 4, 1, each, part.shape[4])
            )
            return piece.reshape(4 * each, part.shape[4])

        return ring_sum(cut, x, ("xl", "xh"), x_pairs).astype(BF)

    mine = lax.dynamic_index_in_dim(tokens, xh, 0, keepdims=False)
    other = lax.dynamic_index_in_dim(tokens, 1 - xh, 0, keepdims=False)
    other = lax.ppermute(other, "xh", FLIP)
    early_rows = [mine] + [lax.ppermute(mine, "z", ring_pairs(step)) for step in STEPS]
    late_row = after(other, *early_rows)
    late_rows = [late_row] + [lax.ppermute(late_row, "z", ring_pairs(step)) for step in STEPS]
    own_memory = swap_in(after(memory, *early_rows), xh)
    def side_by_side(own, other):
        return jnp.concatenate([jnp.where(xh == 0, own, other), jnp.where(xh == 0, other, own)], axis=0)

    own_tokens = side_by_side(mine, late_row)

    def head_cols(matrix, third):
        return lax.dynamic_slice(matrix, (0, third * width + z * 256), (matrix.shape[0], 256))

    heads_qkv = jnp.concatenate([head_cols(self_qkv, third) for third in range(3)], axis=1)
    bias_q = lax.dynamic_slice(proj_biases, (0, z * 256), (1, 256))
    bias_v = lax.dynamic_slice(proj_biases, (1, z * 256), (1, 256))
    bias_qkv = jnp.concatenate([bias_q, jnp.zeros_like(bias_q), bias_v], axis=1)
    joined, low_one, normal_one = project_heads(
        z, xh, early_rows, late_rows, heads_qkv, bias_qkv, norm_gains[0:1], norm_shifts[0:1]
    )
    heads_mix, self_level = attend(page_rows, page_rows, 2, True, joined, joined, joined, (0, 256, 512))

    memory_here = after(own_memory, *late_rows)
    before_got, behind_got = (lax.ppermute(memory_here, "z", ring_pairs(step)) for step in (1, 3))
    heads_mix, before_got, behind_got = lax.optimization_barrier((heads_mix, before_got, behind_got))
    far_got = (
        lax.ppermute(behind_got[: rows // 2], "z", ring_pairs(3)),
        lax.ppermute(before_got[rows // 2 :], "z", ring_pairs(1)),
    )
    mix_pick = lambda target: lax.dynamic_slice(heads_mix, (target * rows, 0), (rows, 256))
    mix_got = exchange(mix_pick, z, far_got)
    far_got = lax.optimization_barrier((*far_got, *(part for _, part in mix_got[1:])))[:2]
    page_memory = jnp.zeros((page_rows, width), BF)
    for hop, first, part in (
        (0, 0, memory_here),
        (1, 0, behind_got),
        (3, 0, before_got),
        (2, 0, far_got[0]),
        (2, rows // 2, far_got[1]),
    ):
        page_memory = lax.dynamic_update_slice(page_memory, part, (around(hop, z) * rows + first, 0))
    patch_bias = jnp.concatenate([jnp.zeros_like(proj_biases[4]), proj_biases[4]])
    page_kv = (product(page_memory, cross_kv) + patch_bias).astype(BF)

    grad_low = jnp.where(valid, swap_in(after(cotangent, heads_mix), xh), 0)
    mixture = jnp.zeros((rows, width), BF)
    for source, part in mix_got:
        mixture = lax.dynamic_update_slice(mixture, part, (0, source * 256))
    after_self = own_tokens.astype(F32) + product(mixture, self_out) + proj_biases[2]
    normal_two, inverse_two = unit(after_self)
    low_two = (normal_two * norm_gains[1] + norm_shifts[1]).astype(BF)
    cross_queries = (product(low_two, cross_query) + proj_biases[3]).astype(BF)
    cross_mix, cross_level = attend(
        rows, page_rows, 8, False, cross_queries, page_kv, page_kv, (0, 0, 1024), count
    )
    after_cross = after_self + product(cross_mix, cross_out) + proj_biases[5]
    normal_three, inverse_three = unit(after_cross)
    low_three = (normal_three * norm_gains[2] + norm_shifts[2]).astype(BF)
    before = product(low_three, ffn_in) + ffn_bias
    below = 0.5 * (1.0 + lax.erf(before * np.float32(np.sqrt(0.5))))
    hidden = (before * below).astype(BF)
    slope = below + before * jnp.exp(-0.5 * before * before) * np.float32(1 / np.sqrt(2 * np.pi))
    result = after_cross + product(hidden, ffn_out) + proj_biases[6]
    layer_rows = jnp.where(valid, result, 0.0).astype(BF)

    order, sends, odd_sends, odd_from, odd_to = qkv_order()
    head_order = lax.dynamic_index_in_dim(jnp.asarray(order), z, 0, keepdims=False)
    head_shuffle, sides = lax.optimization_barrier((shuffle_matrix(head_order), sides))

    out_grads = own_eights(grad_low)
    early = jnp.concatenate([cross_mix, low_two, mixture, low_three, out_grads[:, 512:]], axis=1)
    early_got = swap_cores(early)
    hidden_got = swap_cores(hidden)
    grad_before = (back_product(grad_low, ffn_out) * slope).astype(BF)
    before_sums = column_sums(grad_before)
    in_keep, in_send = split_wides(c, grad_before)
    in_got = swap_cores(in_send)
    grad_three = back_product(grad_before, ffn_in)
    grad_after_cross = grad_low.astype(F32) + unit_back(
        normal_three, inverse_three, grad_three, norm_gains[2]
    )
    cross_low = grad_after_cross.astype(BF)
    cross_grads = own_eights(cross_low)
    cross_got = swap_cores(cross_grads[:, 512:])
    grad_cross_mix = back_product(cross_low, cross_out).astype(BF)
    ffn_in_chunks = outer_chunks(
        y, 512, 512, [((in_keep, 0), (in_got, 0), (early, 3 * width), (early_got, 3 * width), 2)]
    )
    ffn_out_chunks = outer_chunks(
        x,
        128,
        width,
        [
            ((out_grads, 0), (early_got, 4 * width), (hidden, 0), (hidden_got, 0), 4),
            ((cross_grads, 0), (cross_got, 0), (early, 0), (early_got, 0), 1),
        ],
    )
    ffn_out_got = relay(ffn_out_chunks, *X_RING)
    ffn_in_got = relay(ffn_in_chunks, *Y_RING)

    grad_cross_mix, layer_rows, *got = lax.optimization_barrier(
        (grad_cross_mix, layer_rows, *ffn_out_got, *ffn_in_got)
    )
    ffn_out_sums, ffn_in_sums = add_on(ffn_out_chunks, got[:2]), add_on(ffn_in_chunks, got[2:])
    grad_cross_mix, *sums = lax.optimization_barrier((grad_cross_mix, *ffn_out_sums, *ffn_in_sums))
    ffn_out_got, ffn_in_got = send_on(sums[:2], *X_RING), send_on(sums[2:], *Y_RING)
    cross_query_low, patch_grads = attend_back(
        rows,
        page_rows,
        8,
        False,
        cross_queries,
        page_kv,
        page_kv,
        (0, 0, 1024),
        cross_mix,
        grad_cross_mix,
        cross_level,
        count,
    )
    cross_query_low, patch_grads, layer_rows, *got = lax.optimization_barrier(
        (cross_query_low, patch_grads, layer_rows, *ffn_out_got, *ffn_in_got)
    )
    layer_out = swap_out(layer_rows, xh)
    ffn_out_part, ffn_in_part = finish(ffn_out_chunks, got[:2]), finish(ffn_in_chunks, got[2:])
    grad_two = back_product(cross_query_low, cross_query)
    grad_after_self = grad_after_cross + unit_back(normal_two, inverse_two, grad_two, norm_gains[1])

    self_low = grad_after_self.astype(BF)
    grad_mix_rows = back_product(self_low, self_out).astype(BF)
    grads_here = after(patch_grads, grad_mix_rows)
    kv_send, kv_keep = patch_halves(c, grads_here, page_memory)
    grad_mixture = rows_to_heads(grad_mix_rows, z, (kv_send,))
    grads_here = after(patch_grads, grad_mixture)
    kv_rows = sum_low(kv_keep, swap_cores(kv_send))
    kv_quarters = kv_rows.reshape(RING, 256, width)

    def kv_chunk(hop):
        return lax.dynamic_index_in_dim(kv_quarters, around(hop, y), 0, keepdims=False)

    kv_own, kv_sends = kv_chunk(0), [kv_chunk(step) for step in STEPS]
    out_quarters = ffn_out_part.reshape(RING, 32, 5 * width)
    out_own, *out_sends = (
        lax.dynamic_index_in_dim(out_quarters, around(hop, y), 0, keepdims=False) for hop in (0,) + STEPS
    )
    query_grads, self_grads = own_eights(cross_query_low), own_eights(self_low)
    sent = swap_cores(jnp.concatenate([query_grads[:, 512:], self_grads[:, 512:]], axis=1))
    sent, *out_sends = lax.optimization_barrier((sent, *out_sends))
    out_got = [lax.ppermute(chunk, "y", ring_pairs(step)) for step, chunk in zip(STEPS, out_sends)]
    two_chunks = outer_chunks(
        x,
        128,
        width,
        [
            ((query_grads, 0), (sent, 0), (early, width), (early_got, width), 1),
            ((self_grads, 0), (sent, 512), (early, 2 * width), (early_got, 2 * width), 1),
        ],
        extra=ffn_in_part,
    )
    two_chunks = lax.optimization_barrier((*two_chunks, *out_got))
    two_chunks, out_got = two_chunks[:5], two_chunks[5:]
    grad_mixture, layer_out, *held = lax.optimization_barrier(
        (grad_mixture, layer_out, *kv_sends, *two_chunks)
    )
    kv_sends, two_chunks = held[:3], held[3:]

    two_got = relay(two_chunks, *X_RING)
    kv_got = [lax.ppermute(chunk, "y", ring_pairs(step)) for step, chunk in zip(STEPS, kv_sends)]
    (grad_joined,) = attend_back(
        page_rows, page_rows, 2, True, joined, joined, joined, (0, 256, 512), heads_mix, grad_mixture, self_level
    )
    grad_joined, grads_here, *two_got = lax.optimization_barrier((grad_joined, grads_here, *two_got))
    grad_joined, *two_sums = lax.optimization_barrier((grad_joined, *add_on(two_chunks, two_got)))
    two_got = send_on(two_sums, *X_RING)
    *page_chunks, page_sums, head_sums = page_back(z, grad_joined, heads_qkv, grads_here, cross_kv, normal_one)
    shuffled = product(grad_joined, head_shuffle).astype(BF)
    shuffled, page_sums, head_sums, *held = lax.optimization_barrier(
        (shuffled, page_sums, head_sums, *page_chunks, *kv_got)
    )
    page_chunks, kv_got = held[:5], held[5:]
    Z_RING = ("z", ring_pairs)
    page_got = relay(page_chunks, *Z_RING)

    def core_half(target):
        return outer(lax.dynamic_slice(shuffled, (0, target * 384), (page_rows, 384)), low_one)

    core_keep = core_half(c)
    core_send = core_half(1 - c).astype(BF)
    core_keep, core_send, *held = lax.optimization_barrier(
        (core_keep, core_send, *two_got, *kv_got, *out_got)
    )
    two_got, kv_got, out_got = held[:2], held[2:5], held[5:]
    ffn_out_part = sum_low(out_own, *out_got)

    core_got = swap_cores(core_send).astype(F32)
    vectors = [
        page_sums[0],
        column_sums(grad_two * normal_two),
        column_sums(grad_three * normal_three),
        page_sums[1],
        column_sums(grad_two),
        column_sums(grad_three),
        column_sums(grad_after_self),
        column_sums(cross_query_low),
        page_sums[2],
        column_sums(grad_after_cross),
        column_sums(grad_low),
    ]
    small_keep, small_send = pack_vectors(z, c, vectors, head_sums, before_sums.reshape(4, width))
    small_sum = (small_keep.astype(F32) + swap_cores(small_send).astype(F32)).astype(BF)
    core_sum = (core_keep + core_got).astype(BF)
    kv_part = sum_low(kv_own, *kv_got)
    core_sum, small_sum, kv_part, *page_got = lax.optimization_barrier(
        (core_sum, small_sum, kv_part, *page_got)
    )

    half = rows // 2
    page_plus = (page_chunks[1][:half].astype(F32) + page_got[0].astype(F32)).astype(BF)
    page_minus = (page_chunks[2][half:].astype(F32) + page_got[1].astype(F32)).astype(BF)
    page_plus = jnp.concatenate([page_plus, page_chunks[1][half:]], axis=0)
    page_minus = jnp.concatenate([page_chunks[2][:half], page_minus], axis=0)
    page_got = send_on((page_plus, page_minus), *Z_RING)
    small_sum = jnp.pad(small_sum.reshape(4, 4, 1, width), ((0, 0), (0, 0), (0, 7), (0, 0)))
    core_sum = jnp.concatenate([core_sum.reshape(4, 4, 24, width), small_sum], axis=2)
    kv_lines = kv_part.reshape(2, 4, 2, 16, width)

    def x_chunk(target):
        piece = lax.dynamic_slice(kv_lines, (target % 2, 0, target // 2, 0, 0), (1, 4, 1, 16, width))
        lines = lax.dynamic_index_in_dim(core_sum, target, 0, keepdims=False)
        return jnp.concatenate([lines.reshape(128, width), piece.reshape(64, width)], axis=0)

    x_sum = ring_sum(x_chunk, x, ("xl", "xh"), x_pairs).astype(BF)
    two_part = finish(two_chunks, two_got)
    x_sum, two_part, mine, late_row, *page_got = lax.optimization_barrier(
        (x_sum, two_part, mine, late_row, *page_got)
    )
    own_tokens = side_by_side(mine, late_row)

    two_part, ffn_in_part = two_part[:, : 2 * width].reshape(4, 32, 2 * width), two_part[:, 2 * width :]
    cross_kv_part = x_sum[128:]
    y_lines = jnp.concatenate([x_sum[:128].reshape(4, 32, width), two_part], axis=2)
    y_sum = ring_sum(
        lambda target: lax.dynamic_index_in_dim(y_lines, target, 0, keepdims=False), y, "y", ring_pairs
    )
    grad_own, memory_rows = (
        sum(part[:, at : at + width].astype(F32) for part in (page_chunks[0], *page_got)) for at in (0, width)
    )
    own_normal, own_inverse = unit(own_tokens.astype(F32))
    token_rows = grad_after_self + unit_back(own_normal, own_inverse, grad_own, norm_gains[0])
    both_grads = swap_out(jnp.concatenate([token_rows, memory_rows], axis=1).astype(BF), xh)
    token_grad, memory_grad = both_grads[..., :width], both_grads[..., width:]

    two_part, y_sum = y_sum[:, width:].astype(BF), y_sum[:, :width]
    small_part = jnp.pad(y_sum[24].astype(BF).reshape(4, 1, 256), ((0, 0), (0, 7), (0, 768)))
    me = (((y * 2 + xl) * 2 + c) * 4 + z) * 2 + xh
    odd_at = lax.dynamic_index_in_dim(jnp.asarray(odd_from), me, 0, keepdims=False) * 8
    odd_got = lax.ppermute(lax.dynamic_slice(y_sum, (odd_at, 0), (8, width)), AXES, odd_sends)
    odd_here = jnp.arange(24) // 8 == lax.dynamic_index_in_dim(jnp.asarray(odd_to), me, 0, keepdims=False)
    grad_qkv = lax.ppermute(y_sum[:24], AXES, sends)
    grad_qkv = jnp.where(odd_here[:, None], jnp.concatenate([odd_got] * 3, axis=0), grad_qkv)

    lines = []
    for part in (ffn_out_part, ffn_in_part, two_part, cross_kv_part, small_part):
        part = part.reshape(4, -1, part.shape[-1])
        lines += [part[..., at : at + width] for at in range(0, part.shape[-1], width)]
    lines = jnp.concatenate(lines, axis=1)
    z_line = lambda hop: lax.dynamic_index_in_dim(lines, around(hop, z), 0, keepdims=False)
    z_got = [lax.ppermute(z_line(step), "z", ring_pairs(step)) for step in STEPS]
    ffn_out_rows, cross_out_rows, ffn_in_rows, cross_query_rows, self_out_rows, cross_kv_rows, *small = last_sums(
        z_line(0), *z_got
    )

    return (
        layer_out,
        token_grad,
        memory_grad,
        grad_qkv.T,
        self_out_rows.T,
        cross_query_rows.T,
        cross_kv_rows.T,
        cross_out_rows.T,
        ffn_in_rows.T,
        ffn_out_rows.T,
        *small[:3],
        small[3].reshape(-1),
    )


def solution(mesh):
    split = jax.sharding.Mesh(mesh.devices.reshape(MESH_SHAPE), AXES)
    page, blk = AXES[:3], AXES[3:]
    blocks, cols = P(page, blk, None), P(None, AXES)
    in_specs = (blocks, blocks, P(page), P(page)) + (P(),) * 11 + (blocks,)
    out_specs = (blocks,) * 3 + (cols,) * 10 + (P(AXES),)
    return jax.shard_map(
        on_device, mesh=split, in_specs=in_specs, out_specs=out_specs, check_vma=False
    )
```
